32 devices in a mesh: prow: 8 (over z, y), pcol: 4 (over x, core).
Axes of the slice: x: 2, y: 2, z: 4, core: 2. Of those that a mesh axis runs over, the one named last changes fastest.
Arguments:
- data: float32 [16384, 8192], P('prow', 'pcol'), may hold values from 0.05 to 5
- w_trans: float32 [32, 16384], P(None, ('prow', 'pcol')), as said below
- h_prior: float32 [32, 8192], P(None, 'pcol'), may hold values from 0.1 to 3
Outputs:
- h_next: float32 [32, 8192], P(None, 'pcol')
The draws below stay inside these ranges and needn't reach their ends.
Inputs may be any that keep to these rules, and one draw needn't show every extreme that they name: `w_trans`: every entry is positive.
All inputs are finite; a program needn't handle non-finite values.
Results may differ from the reference program's by a relative error of at most 0.0003.
Values sent between devices are 32-bit elements; how exact they have to be, the bound alone decides.
No kernel may reach another device: no remote copies, remote signals or barrier semaphores. Data moves between devices by JAX's collectives and lax.ppermute only.
A program may use at most 64 MiB of HBM per device.

```python
import math
import jax
import jax.numpy as jnp
from jax import lax

RANK = 32
ROWS = 16384
COLS = 8192


def draw_w_trans(key, part):
    key = jax.random.fold_in(key, 11)
    first = jax.random.fold_in(key, 0)
    place = jnp.arange(ROWS, dtype=jnp.float32) / ROWS
    rising = jnp.exp(jnp.log(3.0) * place)[None, :]
    values = (jnp.abs(jax.random.normal(first, (RANK, ROWS), jnp.float32)) + 0.1) * rising
    return (values / RANK).astype(jnp.float32)


def level_of(stream_key, dims, cuts, low, top_value):
    def one(dim, shards_of):
        heights = jax.random.uniform(jax.random.fold_in(jax.random.fold_in(stream_key, 6), dim), (shards_of,), jnp.float32, low / len(cuts), top_value / len(cuts))
        return jnp.repeat(jnp.exp(heights), dims[dim] // shards_of).reshape((-1,) + (1,) * (len(dims) - dim - 1))

    loudness = one(*cuts[0])
    for cut in cuts[1:]:
        loudness = loudness * one(*cut)
    return loudness


def setup_inputs(seed: int = 0) -> dict:
    key_list = jax.random.split(jax.random.key(seed), 4)
    return {
        "data": jnp.clip(jnp.exp(math.log(5.0) - 4.6051702 * jax.random.uniform(key_list[0], (ROWS, COLS), jnp.float32) ** level_of(key_list[0], (ROWS, COLS), ((0, 8), (1, 4)), -0.2, 0.2)), 0.05, 5.0),
        "w_trans": draw_w_trans(jax.random.fold_in(key_list[3], 71), 0),
        "h_prior": jnp.clip(jnp.exp(math.log(3.0) - 3.4011974 * jax.random.uniform(key_list[2], (RANK, COLS), jnp.float32) ** level_of(key_list[2], (RANK, COLS), ((1, 4),), -0.2, 0.2)), 0.1, 3.0),
    }


def sweep(h_start, cross, gram):
    rank = h_start.shape[0]
    block = 8
    h_now = h_start
    for first in range(0, rank, block):
        mixed = jnp.dot(gram[first:first + block], h_now, precision=lax.Precision.HIGHEST)
        olds = h_now[first:first + block]
        fresh_rows = []
        for inner in range(block):
            k = first + inner
            total = mixed[inner]
            for prior in range(inner):
                total = total + gram[k, first + prior] * (fresh_rows[prior] - olds[prior])
            fresh = jnp.maximum(olds[inner] + (cross[k] - total) / gram[k, k], 0.0)
            fresh_rows.append(fresh)
        h_now = lax.dynamic_update_slice_in_dim(h_now, jnp.stack(fresh_rows, 0), first, 0)
    return h_now


def reference(data, w_trans, h_prior):
    cross = jnp.dot(w_trans, data, precision=lax.Precision.HIGHEST)
    gram = jnp.dot(w_trans, w_trans.T, precision=lax.Precision.HIGHEST)
    return sweep(h_prior, cross, gram)
```

```python
import functools

import jax
import jax.numpy as jnp
from jax import lax
from jax.experimental import pallas as pl
from jax.experimental.pallas import tpu as pltpu
from jax.sharding import PartitionSpec as P

LANES = 128
GRAM_ROWS = 8
VMEM = pl.BlockSpec(memory_space=pltpu.VMEM)
ANY = pl.BlockSpec(memory_space=pl.ANY)


def split(value):
    high = value.astype(jnp.bfloat16)
    low = (value - high.astype(jnp.float32)).astype(jnp.bfloat16)
    return high, low


def exact_dot(left, right, dims):
    return lax.dot_general(
        left, right, (dims, ((), ())),
        precision=lax.Precision.HIGHEST, preferred_element_type=jnp.float32,
    )


def partial_kernel(n_row, n_col, width, *refs):
    w_refs, data_ref = refs[:n_col], refs[n_col]
    out_refs = refs[n_col + 1 : n_col + 1 + n_row]
    w_split, blocks, sems = refs[n_col + 1 + n_row :]
    rank, depth = w_refs[0].shape
    row_at, col_at = lax.axis_index("prow"), lax.axis_index("pcol")

    copies = []
    for turn in range(n_row):
        start = pl.multiple_of((row_at ^ turn) * width, width)
        copy = pltpu.make_async_copy(
            data_ref.at[:, pl.ds(start, width)], blocks.at[turn], sems.at[turn]
        )
        copy.start()
        copies.append(copy)

    gram = jnp.zeros((rank, rank), jnp.float32)
    for turn in range(n_col):
        part = w_refs[turn][...]
        high, low = split(part)
        columns = pl.ds(pl.multiple_of((col_at ^ turn) * depth, depth), depth)
        w_split[:rank, columns] = high
        w_split[rank:, columns] = low
        gram = gram + exact_dot(part, part, ((1,), (1,)))
    slabs = [gram[GRAM_ROWS * i : GRAM_ROWS * (i + 1)] for i in range(rank // GRAM_ROWS)]
    packed = jnp.concatenate(slabs, axis=1)

    both = w_split[...]
    first = w_split[:rank]
    for turn in range(n_row):
        copies[turn].wait()
        high, low = split(blocks[turn])
        upper = jnp.dot(both, high, preferred_element_type=jnp.float32)
        cross = (
            upper[:rank]
            + upper[rank:]
            + jnp.dot(first, low, preferred_element_type=jnp.float32)
        )
        for i in range(width // LANES):
            out_refs[turn][rank * i : rank * (i + 1)] = cross[:, LANES * i : LANES * (i + 1)]
        out_refs[turn][rank * (width // LANES) :] = packed


def sweep_kernel(n_row, width, *refs):
    parts, h_ref, out_ref = refs[:n_row], refs[n_row], refs[n_row + 1]
    rank = h_ref.shape[0]
    row_at = lax.axis_index("prow")
    total = parts[0][...]
    for turn in range(1, n_row):
        total = total + parts[turn][...]
    pieces = width // LANES
    cross = jnp.concatenate([total[rank * i : rank * (i + 1)] for i in range(pieces)], axis=1)
    packed = total[rank * pieces :]
    slabs = rank // GRAM_ROWS
    gram = jnp.concatenate(
        [packed[:, rank * i : rank * (i + 1)] for i in range(slabs)], axis=0
    )
    h = h_ref[:, pl.ds(pl.multiple_of(row_at * width, width), width)]
    rest = cross - exact_dot(gram, h, ((1,), (0,)))
    for k in range(rank):
        inverse = 1.0 / gram[k : k + 1, k : k + 1]
        old = h[k : k + 1]
        fresh = jnp.maximum(old + rest[k : k + 1] * inverse, 0.0)
        out_ref[k : k + 1, :] = fresh
        rest = rest - gram[:, k : k + 1] * (fresh - old)


def assemble_kernel(n_row, width, *refs):
    parts, out_ref = refs[:n_row], refs[n_row]
    row_at = lax.axis_index("prow")
    for turn in range(n_row):
        columns = pl.ds(pl.multiple_of((row_at ^ turn) * width, width), width)
        out_ref[:, columns] = parts[turn][...]


def exchange(value, axis, count, turn):
    return lax.ppermute(value, axis, [(i, i ^ turn) for i in range(count)])


def shards(n_row, n_col, data, w_trans, h_prior):
    rank, depth = w_trans.shape
    rows, cols = data.shape
    width = cols // n_row
    w_parts = [w_trans] + [exchange(w_trans, "pcol", n_col, t) for t in range(1, n_col)]

    slab = jax.ShapeDtypeStruct((rank * (width // LANES) + GRAM_ROWS, LANES), jnp.float32)
    partial = pl.pallas_call(
        functools.partial(partial_kernel, n_row, n_col, width),
        out_shape=[slab] * n_row,
        in_specs=[VMEM] * n_col + [ANY],
        out_specs=[VMEM] * n_row,
        scratch_shapes=[
            pltpu.VMEM((2 * rank, rows), jnp.bfloat16),
            pltpu.VMEM((n_row, rows, width), jnp.float32),
            pltpu.SemaphoreType.DMA((n_row,)),
        ],
        compiler_params=pltpu.CompilerParams(vmem_limit_bytes=40 * 1024 * 1024),
        name="partial_products",
    )(*w_parts, data)

    parts = [partial[0]] + [exchange(partial[t], "prow", n_row, t) for t in range(1, n_row)]
    fresh = pl.pallas_call(
        functools.partial(sweep_kernel, n_row, width),
        out_shape=jax.ShapeDtypeStruct((rank, width), jnp.float32),
        in_specs=[VMEM] * (n_row + 1),
        out_specs=VMEM,
        name="row_sweep",
    )(*parts, h_prior)

    pieces = [fresh] + [exchange(fresh, "prow", n_row, t) for t in range(1, n_row)]
    return pl.pallas_call(
        functools.partial(assemble_kernel, n_row, width),
        out_shape=jax.ShapeDtypeStruct((rank, cols), jnp.float32),
        in_specs=[VMEM] * n_row,
        out_specs=VMEM,
        name="assemble",
    )(*pieces)


def solution(mesh):
    n_row, n_col = mesh.shape["prow"], mesh.shape["pcol"]
    placed = (P("prow", "pcol"), P(None, ("prow", "pcol")), P(None, "pcol"))
    return jax.shard_map(
        functools.partial(shards, n_row, n_col),
        mesh=mesh, in_specs=placed, out_specs=P(None, "pcol"), check_vma=False,
    )
```

```python
import functools

import jax
import jax.numpy as jnp
from jax import lax
from jax.experimental import pallas as pl
from jax.experimental.pallas import tpu as pltpu
from jax.sharding import PartitionSpec as P

LANES = 128
GRAM_ROWS = 8
VMEM = pl.BlockSpec(memory_space=pltpu.VMEM)
ANY = pl.BlockSpec(memory_space=pl.ANY)


def split(value):
    high = value.astype(jnp.bfloat16)
    low = (value - high.astype(jnp.float32)).astype(jnp.bfloat16)
    return high, low


def exact_dot(left, right, dims):
    return lax.dot_general(
        left, right, (dims, ((), ())),
        precision=lax.Precision.HIGHEST, preferred_element_type=jnp.float32,
    )


def partial_kernel(n_row, n_col, width, *refs):
    w_refs, data_ref = refs[:n_col], refs[n_col]
    out_ref, w_split, blocks, sems = refs[n_col + 1 :]
    rank, depth = w_refs[0].shape
    row_at, col_at = lax.axis_index("prow"), lax.axis_index("pcol")

    copies = []
    for turn in range(n_row):
        start = pl.multiple_of((row_at ^ turn) * width, width)
        copy = pltpu.make_async_copy(
            data_ref.at[:, pl.ds(start, width)], blocks.at[turn], sems.at[turn]
        )
        copy.start()
        copies.append(copy)

    gram = jnp.zeros((rank, rank), jnp.float32)
    for turn in range(n_col):
        part = w_refs[turn][...]
        high, low = split(part)
        columns = pl.ds(pl.multiple_of((col_at ^ turn) * depth, depth), depth)
        w_split[:rank, columns] = high
        w_split[rank:, columns] = low
        gram = gram + exact_dot(part, part, ((1,), (1,)))
    slabs = [gram[GRAM_ROWS * i : GRAM_ROWS * (i + 1)] for i in range(rank // GRAM_ROWS)]
    packed = jnp.concatenate(slabs, axis=1)

    both = w_split[...]
    first = w_split[:rank]
    for turn in range(n_row):
        peer = row_at ^ turn
        copies[turn].wait()
        high, low = split(blocks[turn])
        upper = jnp.dot(both, high, preferred_element_type=jnp.float32)
        cross = (
            upper[:rank]
            + upper[rank:]
            + jnp.dot(first, low, preferred_element_type=jnp.float32)
        )
        for i in range(width // LANES):
            out_ref[peer, rank * i : rank * (i + 1)] = cross[:, LANES * i : LANES * (i + 1)]
        out_ref[peer, rank * (width // LANES) :] = packed


def sweep_kernel(n_row, width, parts, h_ref, out_ref):
    rank = h_ref.shape[0]
    row_at = lax.axis_index("prow")
    total = parts[0]
    for turn in range(1, n_row):
        total = total + parts[turn]
    pieces = width // LANES
    cross = jnp.concatenate([total[rank * i : rank * (i + 1)] for i in range(pieces)], axis=1)
    packed = total[rank * pieces :]
    slabs = rank // GRAM_ROWS
    gram = jnp.concatenate(
        [packed[:, rank * i : rank * (i + 1)] for i in range(slabs)], axis=0
    )
    h = h_ref[:, pl.ds(pl.multiple_of(row_at * width, width), width)]
    rest = cross - exact_dot(gram, h, ((1,), (0,)))
    for k in range(rank):
        inverse = 1.0 / gram[k : k + 1, k : k + 1]
        old = h[k : k + 1]
        fresh = jnp.maximum(old + rest[k : k + 1] * inverse, 0.0)
        out_ref[k : k + 1, :] = fresh
        rest = rest - gram[:, k : k + 1] * (fresh - old)


def exchange(value, axis, count, turn):
    return lax.ppermute(value, axis, [(i, i ^ turn) for i in range(count)])


def shards(n_row, n_col, data, w_trans, h_prior):
    rank, depth = w_trans.shape
    rows, cols = data.shape
    width = cols // n_row
    w_parts = [w_trans] + [exchange(w_trans, "pcol", n_col, t) for t in range(1, n_col)]

    slabs = jax.ShapeDtypeStruct(
        (n_row, rank * (width // LANES) + GRAM_ROWS, LANES), jnp.float32
    )
    partial = pl.pallas_call(
        functools.partial(partial_kernel, n_row, n_col, width),
        out_shape=slabs,
        in_specs=[VMEM] * n_col + [ANY],
        out_specs=VMEM,
        scratch_shapes=[
            pltpu.VMEM((2 * rank, rows), jnp.bfloat16),
            pltpu.VMEM((n_row, rows, width), jnp.float32),
            pltpu.SemaphoreType.DMA((n_row,)),
        ],
        compiler_params=pltpu.CompilerParams(vmem_limit_bytes=40 * 1024 * 1024),
        name="partial_products",
    )(*w_parts, data)

    parts = lax.all_to_all(partial, "prow", 0, 0)
    fresh = pl.pallas_call(
        functools.partial(sweep_kernel, n_row, width),
        out_shape=jax.ShapeDtypeStruct((rank, width), jnp.float32),
        in_specs=[VMEM] * 2,
        out_specs=VMEM,
        name="row_sweep",
    )(parts, h_prior)
    return lax.all_gather(fresh, "prow", axis=1, tiled=True)


def solution(mesh):
    n_row, n_col = mesh.shape["prow"], mesh.shape["pcol"]
    placed = (P("prow", "pcol"), P(None, ("prow", "pcol")), P(None, "pcol"))
    return jax.shard_map(
        functools.partial(shards, n_row, n_col),
        mesh=mesh, in_specs=placed, out_specs=P(None, "pcol"), check_vma=False,
    )
```

```python
import functools

import jax
import jax.numpy as jnp
from jax import lax
from jax.experimental import pallas as pl
from jax.experimental.pallas import tpu as pltpu
from jax.sharding import PartitionSpec as P

LANES = 128
GRAM_ROWS = 8
VMEM = pl.BlockSpec(memory_space=pltpu.VMEM)


def params(mebibytes):
    return pltpu.CompilerParams(vmem_limit_bytes=mebibytes * 1024 * 1024)


def split(value):
    high = value.astype(jnp.bfloat16)
    low = (value - high.astype(jnp.float32)).astype(jnp.bfloat16)
    return high, low


def exact_dot(left, right, dims):
    return lax.dot_general(
        left, right, (dims, ((), ())),
        precision=lax.Precision.HIGHEST, preferred_element_type=jnp.float32,
    )


def load_kernel(near, width, data_ref, high_ref, low_ref, stage, sems):
    count, slots = high_ref.shape[0], stage.shape[0]
    own_side = lax.rem(lax.axis_index("prow"), near)

    def copy(block):
        side, level = own_side ^ (near - 1 - block // (count // near)), block % (count // near)
        start = pl.multiple_of((level * near + side) * width, width)
        return pltpu.make_async_copy(
            data_ref.at[:, pl.ds(start, width)], stage.at[block % slots], sems.at[block % slots]
        )

    for block in range(min(slots, count)):
        copy(block).start()
    for block in range(count):
        copy(block).wait()
        high, low = split(stage[block % slots])
        high_ref[block] = high
        low_ref[block] = low
        if block + slots < count:
            copy(block + slots).start()


def write_blocks(w_split, high_ref, low_ref, out_ref, first_block, far, width):
    rank = w_split.shape[0] // 2
    both = w_split[...]
    first = w_split[:rank]
    rows = rank * (width // LANES)
    for level in range(far):
        upper = jnp.dot(both, high_ref[first_block + level], preferred_element_type=jnp.float32)
        cross = (
            upper[:rank]
            + upper[rank:]
            + jnp.dot(first, low_ref[first_block + level], preferred_element_type=jnp.float32)
        )
        for i in range(width // LANES):
            out_ref[rows * level + rank * i : rows * level + rank * (i + 1)] = cross[
                :, LANES * i : LANES * (i + 1)
            ]


def other_side_kernel(near, far, n_col, width, *refs):
    w_refs, high_ref, low_ref = refs[:n_col], refs[n_col], refs[n_col + 1]
    out_refs, w_split, gram_ref = refs[n_col + 2 : n_col + near + 1], refs[-2], refs[-1]
    rank, depth = w_refs[0].shape
    col_at = lax.axis_index("pcol")

    gram = jnp.zeros((rank, rank), jnp.float32)
    for turn in range(n_col):
        part = w_refs[turn][...]
        high, low = split(part)
        columns = pl.ds(pl.multiple_of((col_at ^ turn) * depth, depth), depth)
        w_split[:rank, columns] = high
        w_split[rank:, columns] = low
        gram = gram + exact_dot(part, part, ((1,), (1,)))
    slabs = [gram[GRAM_ROWS * i : GRAM_ROWS * (i + 1)] for i in range(rank // GRAM_ROWS)]
    packed = jnp.concatenate(slabs, axis=1)
    gram_ref[...] = packed
    for turn in range(1, near):
        out_ref = out_refs[turn - 1]
        write_blocks(w_split, high_ref, low_ref, out_ref, (near - 1 - turn) * far, far, width)
        out_ref[-GRAM_ROWS:] = packed


def own_side_kernel(near, far, width, w_split, high_ref, low_ref, out_ref):
    write_blocks(w_split, high_ref, low_ref, out_ref, (near - 1) * far, far, width)


def side_sum_kernel(far, own_ref, gram_ref, *refs):
    got_refs, out_ref = refs[:-1], refs[-1]
    rows = own_ref.shape[0] // far
    gram = gram_ref[...]
    for got in got_refs:
        gram = gram + got[-GRAM_ROWS:]
    for level in range(far):
        total = own_ref[rows * level : rows * (level + 1)]
        for got in got_refs:
            total = total + got[rows * level : rows * (level + 1)]
        out_ref[level, :rows] = total
        out_ref[level, rows:] = gram


def sweep_kernel(far, n_row, width, parts, h_ref, out_ref):
    rank = h_ref.shape[0]
    row_at = lax.axis_index("prow")
    total = parts[0]
    for level in range(1, far):
        total = total + parts[level]
    pieces = width // LANES
    cross = jnp.concatenate([total[rank * i : rank * (i + 1)] for i in range(pieces)], axis=1)
    packed = total[rank * pieces :]
    gram = jnp.concatenate(
        [packed[:, rank * i : rank * (i + 1)] for i in range(rank // GRAM_ROWS)], axis=0
    )
    h = h_ref[:, pl.ds(pl.multiple_of(row_at * width, width), width)]
    rest = cross - exact_dot(gram, h, ((1,), (0,)))
    rows = []
    for k in range(rank):
        inverse = 1.0 / gram[k : k + 1, k : k + 1]
        old = h[k : k + 1]
        fresh = jnp.maximum(old + rest[k : k + 1] * inverse, 0.0)
        rows.append(fresh)
        rest = rest - gram[:, k : k + 1] * (fresh - old)
    done = jnp.concatenate(rows, axis=0)
    for peer in range(n_row):
        out_ref[peer] = done


def assemble_kernel(n_row, width, parts, out_ref):
    for peer in range(n_row):
        out_ref[:, width * peer : width * (peer + 1)] = parts[peer]


def exchange(value, axis, pairs):
    return lax.ppermute(value, axis, pairs)


def shards(n_row, n_col, data, w_trans, h_prior):
    rank, depth = w_trans.shape
    rows, cols = data.shape
    width = cols // n_row
    near = max(1, n_row // 4)
    far = n_row // near
    slab = rank * (width // LANES)
    w_parts = [w_trans] + [
        exchange(w_trans, "pcol", [(i, i ^ t) for i in range(n_col)]) for t in range(1, n_col)
    ]
    high, low = pl.pallas_call(
        functools.partial(load_kernel, near, width),
        out_shape=[jax.ShapeDtypeStruct((n_row, rows, width), jnp.bfloat16)] * 2,
        in_specs=[pl.BlockSpec(memory_space=pltpu.HBM)],
        out_specs=[VMEM] * 2,
        scratch_shapes=[
            pltpu.VMEM((4, rows, width), jnp.float32),
            pltpu.SemaphoreType.DMA((4,)),
        ],
        compiler_params=params(16),
        cost_estimate=pl.CostEstimate(
            flops=4 * rows * cols, bytes_accessed=4 * rows * cols, transcendentals=0
        ),
        name="load_data",
    )(data)

    *others, w_split, gram = pl.pallas_call(
        functools.partial(other_side_kernel, near, far, n_col, width),
        out_shape=[jax.ShapeDtypeStruct((far * slab + GRAM_ROWS, LANES), jnp.float32)] * (near - 1)
        + [
            jax.ShapeDtypeStruct((2 * rank, rows), jnp.bfloat16),
            jax.ShapeDtypeStruct((GRAM_ROWS, LANES), jnp.float32),
        ],
        in_specs=[VMEM] * (n_col + 2),
        out_specs=[VMEM] * (near + 1),
        compiler_params=params(16),
        name="other_side",
    )(*w_parts, high, low)
    got = [
        exchange(others[t - 1], "prow", [(i, i ^ t) for i in range(n_row)])
        for t in range(1, near)
    ]
    own = pl.pallas_call(
        functools.partial(own_side_kernel, near, far, width),
        out_shape=jax.ShapeDtypeStruct((far * slab, LANES), jnp.float32),
        in_specs=[VMEM] * 3,
        out_specs=VMEM,
        compiler_params=params(16),
        cost_estimate=pl.CostEstimate(
            flops=6 * rank * rows * cols // near, bytes_accessed=4 * rows * cols // near,
            transcendentals=0,
        ),
        name="own_side",
    )(w_split, high, low)
    summed = pl.pallas_call(
        functools.partial(side_sum_kernel, far),
        out_shape=jax.ShapeDtypeStruct((far, slab + GRAM_ROWS, LANES), jnp.float32),
        in_specs=[VMEM] * (near + 1),
        out_specs=VMEM,
        compiler_params=params(8),
        name="side_sum",
    )(own, gram, *got)
    groups = [[level * near + side for level in range(far)] for side in range(near)]
    parts = lax.all_to_all(summed, "prow", 0, 0, axis_index_groups=groups)
    fresh = pl.pallas_call(
        functools.partial(sweep_kernel, far, n_row, width),
        out_shape=jax.ShapeDtypeStruct((n_row, rank, width), jnp.float32),
        in_specs=[VMEM] * 2,
        out_specs=VMEM,
        compiler_params=params(8),
        name="row_sweep",
    )(parts, h_prior)
    pieces = lax.all_to_all(fresh, "prow", 0, 0)
    return pl.pallas_call(
        functools.partial(assemble_kernel, n_row, width),
        out_shape=jax.ShapeDtypeStruct((rank, cols), jnp.float32),
        in_specs=[VMEM],
        out_specs=VMEM,
        compiler_params=params(8),
        name="assemble",
    )(pieces)


def solution(mesh):
    n_row, n_col = mesh.shape["prow"], mesh.shape["pcol"]
    placed = (P("prow", "pcol"), P(None, ("prow", "pcol")), P(None, "pcol"))
    return jax.shard_map(
        functools.partial(shards, n_row, n_col),
        mesh=mesh, in_specs=placed, out_specs=P(None, "pcol"), check_vma=False,
    )
```

```python
import functools

import jax
import jax.numpy as jnp
from jax import lax
from jax.experimental import pallas as pl
from jax.experimental.pallas import tpu as pltpu
from jax.sharding import PartitionSpec as P

LANES = 128
GRAM_ROWS = 8
SLOTS = 4
VMEM = pl.BlockSpec(memory_space=pltpu.VMEM)
HBM = pl.BlockSpec(memory_space=pltpu.HBM)


def call(kernel, out_shape, operands, name, mebibytes=4, in_specs=None, scratch=(), cost=None):
    many = isinstance(out_shape, list)
    return pl.pallas_call(
        kernel,
        out_shape=out_shape,
        in_specs=in_specs or [VMEM] * len(operands),
        out_specs=[VMEM] * len(out_shape) if many else VMEM,
        scratch_shapes=list(scratch),
        compiler_params=pltpu.CompilerParams(vmem_limit_bytes=mebibytes * 1024 * 1024),
        cost_estimate=cost,
        name=name,
    )(*operands)


def floats(*shape):
    return jax.ShapeDtypeStruct(shape, jnp.float32)


def split(value):
    high = value.astype(jnp.bfloat16)
    low = (value - high.astype(jnp.float32)).astype(jnp.bfloat16)
    return high, low


def exact_dot(left, right, dims):
    return lax.dot_general(
        left, right, (dims, ((), ())),
        precision=lax.Precision.HIGHEST, preferred_element_type=jnp.float32,
    )


def block_copies(near, width, blocks, data_ref, stage, sems):
    row_at = lax.axis_index("prow")
    side, level = lax.rem(row_at, near), lax.div(row_at, near)
    copies = []
    for at, (side_turn, level_turn) in enumerate(blocks):
        peer = (level ^ level_turn) * near + (side ^ side_turn)
        start = pl.multiple_of(peer * width, width)
        copies.append(
            pltpu.make_async_copy(
                data_ref.at[:, pl.ds(start, width)], stage.at[at % SLOTS], sems.at[at % SLOTS]
            )
        )
    return copies


def stream(copies, stage, body):
    for copy in copies[:SLOTS]:
        copy.start()
    for at, copy in enumerate(copies):
        copy.wait()
        body(at, *split(stage[at % SLOTS]))
        if at + SLOTS < len(copies):
            copies[at + SLOTS].start()


def load_kernel(near, width, blocks, data_ref, high_ref, low_ref, stage, sems):
    def body(at, high, low):
        high_ref[at] = high
        low_ref[at] = low

    stream(block_copies(near, width, blocks, data_ref, stage, sems), stage, body)


def product(w_split, high, low, out_ref, row):
    rank = w_split.shape[0] // 2
    upper = jnp.dot(w_split[...], high, preferred_element_type=jnp.float32)
    cross = (
        upper[:rank]
        + upper[rank:]
        + jnp.dot(w_split[:rank], low, preferred_element_type=jnp.float32)
    )
    for i in range(cross.shape[1] // LANES):
        at = row + rank * i
        out_ref[at : at + rank] = cross[:, LANES * i : LANES * (i + 1)]


def basis_kernel(n_col, *refs):
    w_refs, w_split, gram_ref = refs[:n_col], refs[-2], refs[-1]
    rank, depth = w_refs[0].shape
    col_at = lax.axis_index("pcol")
    gram = jnp.zeros((rank, rank), jnp.float32)
    for turn in range(n_col):
        part = w_refs[turn][...]
        high, low = split(part)
        columns = pl.ds(pl.multiple_of((col_at ^ turn) * depth, depth), depth)
        w_split[:rank, columns] = high
        w_split[rank:, columns] = low
        gram = gram + exact_dot(part, part, ((1,), (1,)))
    slabs = [gram[GRAM_ROWS * i : GRAM_ROWS * (i + 1)] for i in range(rank // GRAM_ROWS)]
    gram_ref[...] = jnp.concatenate(slabs, axis=1)


def other_side_kernel(first, slab, count, n_out, w_split, gram_ref, high_ref, low_ref, *out_refs):
    for at in range(count * n_out):
        block = first + at
        product(w_split, high_ref[block], low_ref[block], out_refs[at // count], slab * (at % count))
    for out_ref in out_refs:
        out_ref[slab * count :] = gram_ref[...]


def own_side_kernel(near, width, blocks, slab, w_split, data_ref, *refs):
    out_refs, (stage, sems) = refs[:-2], refs[-2:]

    def body(at, high, low):
        product(w_split, high, low, out_refs[at], 0)

    stream(block_copies(near, width, blocks, data_ref, stage, sems), stage, body)


def side_sum_kernel(count, slab, n_got, *refs):
    own_refs, gram_ref, got_refs = refs[:count], refs[count], refs[count + 1 : count + 1 + n_got]
    out_refs = refs[count + 1 + n_got :]
    gram = gram_ref[...]
    for got in got_refs:
        gram = gram + got[slab * count :]
    for at in range(count):
        total = own_refs[at][...]
        for got in got_refs:
            total = total + got[slab * at : slab * (at + 1)]
        out_refs[at][:slab] = total
        out_refs[at][slab:] = gram


def sweep_kernel(width, *refs):
    parts, h_ref, out_ref = refs[:-2], refs[-2], refs[-1]
    rank = h_ref.shape[0]
    row_at = lax.axis_index("prow")
    total = parts[0][...]
    for part in parts[1:]:
        total = total + part[...]
    pieces = width // LANES
    cross = jnp.concatenate([total[rank * i : rank * (i + 1)] for i in range(pieces)], axis=1)
    packed = total[rank * pieces :]
    gram = jnp.concatenate(
        [packed[:, rank * i : rank * (i + 1)] for i in range(rank // GRAM_ROWS)], axis=0
    )
    h = h_ref[:, pl.ds(pl.multiple_of(row_at * width, width), width)]
    rest = cross - exact_dot(gram, h, ((1,), (0,)))
    for k in range(rank):
        inverse = 1.0 / gram[k : k + 1, k : k + 1]
        old = h[k : k + 1]
        fresh = jnp.maximum(old + rest[k : k + 1] * inverse, 0.0)
        out_ref[k : k + 1, :] = fresh
        rest = rest - gram[:, k : k + 1] * (fresh - old)


def pack_kernel(*refs):
    for at, ref in enumerate(refs[:-1]):
        refs[-1][at] = ref[...]


def assemble_kernel(near, width, groups, *refs):
    own_refs = refs[: sum(len(group) for group in groups)]
    got_refs, out_ref = refs[len(own_refs) : -1], refs[-1]
    row_at = lax.axis_index("prow")
    side, level = lax.rem(row_at, near), lax.div(row_at, near)

    def store(level_turn, side_turn, value):
        peer = (level ^ level_turn) * near + (side ^ side_turn)
        out_ref[:, pl.ds(pl.multiple_of(peer * width, width), width)] = value

    turns = [turn for group in groups for turn in group]
    for turn, ref in zip(turns, own_refs):
        store(turn, 0, ref[...])
    for index, ref in enumerate(got_refs):
        group = groups[index // (near - 1)]
        for at, turn in enumerate(group):
            store(turn, index % (near - 1) + 1, ref[at])


def shards(n_row, n_col, data, w_trans, h_prior):
    rank, depth = w_trans.shape
    rows, cols = data.shape
    width = cols // n_row
    near = max(1, n_row // 4)
    far = n_row // near
    slab = rank * (width // LANES)
    groups = [list(range(far // 2, far)), list(range(far // 2 - 1, -1, -1))]
    count = far // 2
    sides = range(1, near)

    def permute(value, axis, turn):
        size = n_row if axis == "prow" else n_col
        return lax.ppermute(value, axis, [(i, i ^ turn) for i in range(size)])

    w_parts = [w_trans] + [permute(w_trans, "pcol", t) for t in range(1, n_col)]
    others = [(side, turn) for group in groups for side in sides for turn in group]
    stage = [pltpu.VMEM((SLOTS, rows, width), jnp.float32), pltpu.SemaphoreType.DMA((SLOTS,))]
    high, low = call(
        functools.partial(load_kernel, near, width, others),
        [jax.ShapeDtypeStruct((len(others), rows, width), jnp.bfloat16)] * 2,
        [data], "load_other_side", 42, [HBM], stage,
        pl.CostEstimate(flops=0, bytes_accessed=8 * rows * width * len(others), transcendentals=0),
    )
    w_split, gram = call(
        functools.partial(basis_kernel, n_col),
        [jax.ShapeDtypeStruct((2 * rank, rows), jnp.bfloat16), floats(GRAM_ROWS, LANES)],
        w_parts, "basis",
    )
    got = []
    for index in range(len(groups)):
        sent = call(
            functools.partial(
                other_side_kernel, index * len(sides) * count, slab, count, len(sides)
            ),
            [floats(count * slab + GRAM_ROWS, LANES)] * len(sides),
            [w_split, gram, high, low], "other_side",
        )
        got.append([permute(sent[side - 1], "prow", side) for side in sides])
    owns = [(0, turn) for group in groups for turn in group]
    own = call(
        functools.partial(own_side_kernel, near, width, owns, slab),
        [floats(slab, LANES)] * len(owns),
        [w_split, data], "own_side", 42, [VMEM, HBM], stage,
        pl.CostEstimate(
            flops=6 * rank * rows * width * far, bytes_accessed=4 * rows * width * far,
            transcendentals=0,
        ),
    )
    parts = []
    for index, group in enumerate(groups):
        sums = call(
            functools.partial(side_sum_kernel, count, slab, len(sides)),
            [floats(slab + GRAM_ROWS, LANES)] * count,
            [*own[index * count : (index + 1) * count], gram, *got[index]], "side_sum",
        )
        for turn, value in zip(group, sums):
            parts.append(permute(value, "prow", turn * near) if turn else value)
    fresh = call(
        functools.partial(sweep_kernel, width), floats(rank, width), [*parts, h_prior], "row_sweep"
    )
    pieces = {
        turn: permute(fresh, "prow", turn * near) if turn else fresh
        for group in groups for turn in group
    }
    final = []
    for group in reversed(groups):
        packed = call(
            pack_kernel, floats(count, rank, width), [pieces[turn] for turn in group], "pack"
        )
        final.extend(permute(packed, "prow", side) for side in sides)
    ordered = list(reversed(groups))
    return call(
        functools.partial(assemble_kernel, near, width, ordered),
        floats(rank, cols),
        [*(pieces[turn] for group in ordered for turn in group), *final], "assemble",
    )


def solution(mesh):
    n_row, n_col = mesh.shape["prow"], mesh.shape["pcol"]
    placed = (P("prow", "pcol"), P(None, ("prow", "pcol")), P(None, "pcol"))
    return jax.shard_map(
        functools.partial(shards, n_row, n_col),
        mesh=mesh, in_specs=placed, out_specs=P(None, "pcol"), check_vma=False,
    )
```

```python
import functools

import jax
import jax.numpy as jnp
from jax import lax
from jax.experimental import pallas as pl
from jax.experimental.pallas import tpu as pltpu
from jax.sharding import PartitionSpec as P

LANES = 128
GRAM_ROWS = 8
SLOTS = 4
PIECES = 2
VMEM = pl.BlockSpec(memory_space=pltpu.VMEM)
HBM = pl.BlockSpec(memory_space=pltpu.HBM)
ANY = pl.BlockSpec(memory_space=pl.ANY)


def call(kernel, out_shape, operands, name, mebibytes=4, in_specs=None, scratch=(), cost=None):
    many = isinstance(out_shape, list)
    return pl.pallas_call(
        kernel,
        out_shape=out_shape,
        in_specs=in_specs or [VMEM] * len(operands),
        out_specs=[VMEM] * len(out_shape) if many else VMEM,
        scratch_shapes=list(scratch),
        compiler_params=pltpu.CompilerParams(vmem_limit_bytes=mebibytes * 1024 * 1024),
        cost_estimate=cost,
        name=name,
    )(*operands)


def floats(*shape):
    return jax.ShapeDtypeStruct(shape, jnp.float32)


def split(value):
    high = value.astype(jnp.bfloat16)
    low = (value - high.astype(jnp.float32)).astype(jnp.bfloat16)
    return high, low


def exact_dot(left, right, dims):
    return lax.dot_general(
        left, right, (dims, ((), ())),
        precision=lax.Precision.HIGHEST, preferred_element_type=jnp.float32,
    )


def stream(near, width, blocks, data_ref, stage, sems, body):
    row_at = lax.axis_index("prow")
    side, level = lax.rem(row_at, near), lax.div(row_at, near)
    depth = data_ref.shape[0] // PIECES
    copies = []
    for side_turn, level_turn in blocks:
        peer = (level ^ level_turn) * near + (side ^ side_turn)
        columns = pl.ds(pl.multiple_of(peer * width, width), width)
        for piece in range(PIECES):
            slot = len(copies) % SLOTS
            rows = pl.ds(piece * depth, depth)
            copies.append(
                pltpu.make_async_copy(data_ref.at[rows, columns], stage.at[slot], sems.at[slot])
            )
    for copy in copies[:SLOTS]:
        copy.start()
    for at, copy in enumerate(copies):
        copy.wait()
        body(at // PIECES, at % PIECES * depth, *split(stage[at % SLOTS]))
        if at + SLOTS < len(copies):
            copies[at + SLOTS].start()


def load_kernel(near, width, blocks, data_ref, *refs):
    high_ref, low_ref, stage, sems = refs[-4:]

    def body(block, row, high, low):
        high_ref[block, row : row + high.shape[0]] = high
        low_ref[block, row : row + low.shape[0]] = low

    stream(near, width, blocks, data_ref, stage, sems, body)


def product(w_split, high, low, out_ref, row):
    rank = w_split.shape[0] // 2
    upper = jnp.dot(w_split[...], high, preferred_element_type=jnp.float32)
    cross = (
        upper[:rank]
        + upper[rank:]
        + jnp.dot(w_split[:rank], low, preferred_element_type=jnp.float32)
    )
    for i in range(cross.shape[1] // LANES):
        at = row + rank * i
        out_ref[at : at + rank] = cross[:, LANES * i : LANES * (i + 1)]


def relay_kernel(*refs):
    count = len(refs) // 2
    for ref, out_ref in zip(refs[:count], refs[count + 1 :]):
        out_ref[...] = ref[...]


def basis_kernel(n_col, *refs):
    w_refs, w_split, gram_ref = refs[:n_col], refs[-2], refs[-1]
    rank, depth = w_refs[0].shape
    col_at = lax.axis_index("pcol")
    gram = jnp.zeros((rank, rank), jnp.float32)
    for turn in range(n_col):
        part = w_refs[turn][...]
        high, low = split(part)
        columns = pl.ds(pl.multiple_of((col_at ^ turn) * depth, depth), depth)
        w_split[:rank, columns] = high
        w_split[rank:, columns] = low
        gram = gram + exact_dot(part, part, ((1,), (1,)))
    slabs = [gram[GRAM_ROWS * i : GRAM_ROWS * (i + 1)] for i in range(rank // GRAM_ROWS)]
    gram_ref[...] = jnp.concatenate(slabs, axis=1)


def other_side_kernel(first, slab, count, w_split, gram_ref, high_ref, low_ref, *out_refs):
    for at in range(count * len(out_refs)):
        block = first + at
        product(w_split, high_ref[block], low_ref[block], out_refs[at // count], slab * (at % count))
    for out_ref in out_refs:
        out_ref[slab * count :] = gram_ref[...]


def own_side_kernel(w_split, high_ref, low_ref, *out_refs):
    for block, out_ref in enumerate(out_refs):
        product(w_split, high_ref[block], low_ref[block], out_ref, 0)


def side_sum_kernel(count, slab, n_got, *refs):
    own_refs, gram_ref, got_refs = refs[:count], refs[count], refs[count + 1 : count + 1 + n_got]
    out_refs = refs[count + 1 + n_got :]
    gram = gram_ref[...]
    for got in got_refs:
        gram = gram + got[slab * count :]
    for at in range(count):
        total = own_refs[at][...]
        for got in got_refs:
            total = total + got[slab * at : slab * (at + 1)]
        out_refs[at][:slab] = total
        out_refs[at][slab:] = gram


def sweep_kernel(width, *refs):
    parts, h_ref, out_ref = refs[:-2], refs[-2], refs[-1]
    rank = h_ref.shape[0]
    row_at = lax.axis_index("prow")
    total = parts[0][...]
    for part in parts[1:]:
        total = total + part[...]
    pieces = width // LANES
    cross = jnp.concatenate([total[rank * i : rank * (i + 1)] for i in range(pieces)], axis=1)
    packed = total[rank * pieces :]
    gram = jnp.concatenate(
        [packed[:, rank * i : rank * (i + 1)] for i in range(rank // GRAM_ROWS)], axis=0
    )
    h = h_ref[:, pl.ds(pl.multiple_of(row_at * width, width), width)]
    rest = cross - exact_dot(gram, h, ((1,), (0,)))
    rows = []
    for k in range(rank):
        inverse = 1.0 / gram[k : k + 1, k : k + 1]
        old = h[k : k + 1]
        fresh = jnp.maximum(old + rest[k : k + 1] * inverse, 0.0)
        rows.append(fresh)
        rest = rest - gram[:, k : k + 1] * (fresh - old)
    done = jnp.concatenate(rows, axis=0)
    for peer in range(out_ref.shape[0]):
        out_ref[peer] = done


def assemble_kernel(width, pieces, out_ref):
    for peer in range(pieces.shape[0]):
        out_ref[:, width * peer : width * (peer + 1)] = pieces[peer]


def shards(n_row, n_col, data, w_trans, h_prior):
    rank, depth = w_trans.shape
    rows, cols = data.shape
    width = cols // n_row
    near = max(1, n_row // 4)
    far = n_row // near
    slab = rank * (width // LANES)
    groups = [list(range(far // 2, far)), list(range(far // 2 - 1, -1, -1))]
    count = far // 2
    sides = range(1, near)

    def permute(value, axis, turn):
        size = n_row if axis == "prow" else n_col
        return lax.ppermute(value, axis, [(i, i ^ turn) for i in range(size)])

    stage = [
        pltpu.VMEM((SLOTS, rows // PIECES, width), jnp.float32),
        pltpu.SemaphoreType.DMA((SLOTS,)),
    ]

    def load(blocks, name, after=()):
        size = rows * width * len(blocks)
        return call(
            functools.partial(load_kernel, near, width, blocks),
            [jax.ShapeDtypeStruct((len(blocks), rows, width), jnp.bfloat16)] * 2,
            [data, *after], name, 40, [HBM] + [ANY] * len(after), stage,
            pl.CostEstimate(flops=0, bytes_accessed=8 * size, transcendentals=0),
        )

    w_parts = {t: permute(w_trans, "pcol", t) if t else w_trans for t in range(0, n_col, 2)}
    w_parts[1] = permute(w_trans, "pcol", 1)
    others = [(side, turn) for group in groups for side in sides for turn in group]
    high, low = load(others, "load_other_side")
    far_turns = range(2, n_col, 2)
    relayed = call(
        relay_kernel, [floats(rank, depth)] * len(far_turns),
        [*(w_parts[t] for t in far_turns), high], "relay",
        in_specs=[VMEM] * len(far_turns) + [ANY],
    )
    for turn, value in zip(far_turns, relayed):
        w_parts[turn + 1] = permute(value, "pcol", 1)
    own_blocks = [
        load([(0, turn) for turn in group], "load_own_side", after=relayed) for group in groups
    ]
    w_split, gram = call(
        functools.partial(basis_kernel, n_col),
        [jax.ShapeDtypeStruct((2 * rank, rows), jnp.bfloat16), floats(GRAM_ROWS, LANES)],
        [*(w_parts[turn] for turn in range(n_col)), own_blocks[0][0]], "basis",
        in_specs=[VMEM] * n_col + [ANY],
    )
    got = []
    for index in range(len(groups)):
        sent = call(
            functools.partial(other_side_kernel, index * len(sides) * count, slab, count),
            [floats(count * slab + GRAM_ROWS, LANES)] * len(sides),
            [w_split, gram, high, low], "other_side",
        )
        got.append([permute(sent[side - 1], "prow", side) for side in sides])
    own = [
        call(own_side_kernel, [floats(slab, LANES)] * count, [w_split, *blocks], "own_side")
        for blocks in own_blocks
    ]
    parts = []
    for index, group in enumerate(groups):
        sums = call(
            functools.partial(side_sum_kernel, count, slab, len(sides)),
            [floats(slab + GRAM_ROWS, LANES)] * count,
            [*own[index], gram, *got[index]], "side_sum",
        )
        for turn, value in zip(group, sums):
            parts.append(permute(value, "prow", turn * near) if turn else value)
    fresh = call(
        functools.partial(sweep_kernel, width), floats(n_row, rank, width),
        [*parts, h_prior], "row_sweep",
    )
    pieces = lax.all_to_all(fresh, "prow", 0, 0)
    return call(
        functools.partial(assemble_kernel, width), floats(rank, cols), [pieces], "assemble"
    )


def solution(mesh):
    n_row, n_col = mesh.shape["prow"], mesh.shape["pcol"]
    placed = (P("prow", "pcol"), P(None, ("prow", "pcol")), P(None, "pcol"))
    return jax.shard_map(
        functools.partial(shards, n_row, n_col),
        mesh=mesh, in_specs=placed, out_specs=P(None, "pcol"), check_vma=False,
    )
```

```python
import functools

import jax
import jax.numpy as jnp
from jax import lax
from jax.experimental import pallas as pl
from jax.experimental.pallas import tpu as pltpu
from jax.sharding import PartitionSpec as P

LANES = 128
GRAM_ROWS = 8
SLOTS = 4
PIECES = 2
VMEM = pl.BlockSpec(memory_space=pltpu.VMEM)
HBM = pl.BlockSpec(memory_space=pltpu.HBM)


def call(kernel, out_shape, operands, name, mebibytes=4, in_specs=None, scratch=(), cost=None):
    many = isinstance(out_shape, list)
    return pl.pallas_call(
        kernel,
        out_shape=out_shape,
        in_specs=in_specs or [VMEM] * len(operands),
        out_specs=[VMEM] * len(out_shape) if many else VMEM,
        compiler_params=pltpu.CompilerParams(vmem_limit_bytes=mebibytes * 1024 * 1024),
        scratch_shapes=list(scratch),
        cost_estimate=cost,
        name=name,
    )(*operands)


def floats(*shape):
    return jax.ShapeDtypeStruct(shape, jnp.float32)


def split(value):
    high = value.astype(jnp.bfloat16)
    low = (value - high.astype(jnp.float32)).astype(jnp.bfloat16)
    return high, low


def exact_dot(left, right, dims):
    return lax.dot_general(
        left, right, (dims, ((), ())),
        precision=lax.Precision.HIGHEST, preferred_element_type=jnp.float32,
    )


def block_start(near, width, side_turn, level_turn):
    row_at = lax.axis_index("prow")
    side, level = lax.rem(row_at, near), lax.div(row_at, near)
    peer = (level ^ level_turn) * near + (side ^ side_turn)
    return pl.multiple_of(peer * width, width)


def load_kernel(near, width, blocks, data_ref, high_ref, low_ref, stage, sems):
    depth = data_ref.shape[0] // PIECES
    copies = []
    for turns in blocks:
        columns = pl.ds(block_start(near, width, *turns), width)
        for piece in range(PIECES):
            slot = len(copies) % SLOTS
            rows = pl.ds(piece * depth, depth)
            copies.append(
                pltpu.make_async_copy(data_ref.at[rows, columns], stage.at[slot], sems.at[slot])
            )
    for copy in copies[:SLOTS]:
        copy.start()
    for at, copy in enumerate(copies):
        copy.wait()
        high, low = split(stage[at % SLOTS])
        row = at % PIECES * depth
        high_ref[at // PIECES, row : row + depth] = high
        low_ref[at // PIECES, row : row + depth] = low
        if at + SLOTS < len(copies):
            copies[at + SLOTS].start()


def fetch(near, width, group, data_ref, out_ref, sems):
    copies = []
    for at, level_turn in enumerate(group):
        columns = pl.ds(block_start(near, width, 0, level_turn), width)
        copy = pltpu.make_async_copy(data_ref.at[:, columns], out_ref.at[at], sems.at[at])
        copy.start()
        copies.append(copy)
    return copies


def product(w_split, high, low, out_ref, row):
    rank = w_split.shape[0] // 2
    upper = jnp.dot(w_split[...], high, preferred_element_type=jnp.float32)
    cross = (
        upper[:rank]
        + upper[rank:]
        + jnp.dot(w_split[:rank], low, preferred_element_type=jnp.float32)
    )
    for i in range(cross.shape[1] // LANES):
        at = row + rank * i
        out_ref[at : at + rank] = cross[:, LANES * i : LANES * (i + 1)]


def other_products(slab, first, count, w_split, gram, high_ref, low_ref, out_refs):
    for index, out_ref in enumerate(out_refs):
        for at in range(count):
            block = first + index * count + at
            product(w_split, high_ref[block], low_ref[block], out_ref, slab * at)
        out_ref[slab * count :] = gram


def first_kernel(near, width, slab, count, own_group, n_col, *refs):
    w_refs, (high_ref, low_ref, data_ref) = refs[:n_col], refs[n_col : n_col + 3]
    *out_refs, w_split, gram_ref, own_ref, sems = refs[n_col + 3 :]
    copies = fetch(near, width, own_group, data_ref, own_ref, sems)
    rank, depth = w_refs[0].shape
    col_at = lax.axis_index("pcol")
    gram = jnp.zeros((rank, rank), jnp.float32)
    for turn in range(n_col):
        part = w_refs[turn][...]
        high, low = split(part)
        columns = pl.ds(pl.multiple_of((col_at ^ turn) * depth, depth), depth)
        w_split[:rank, columns] = high
        w_split[rank:, columns] = low
        gram = gram + exact_dot(part, part, ((1,), (1,)))
    slabs = [gram[GRAM_ROWS * i : GRAM_ROWS * (i + 1)] for i in range(rank // GRAM_ROWS)]
    packed = jnp.concatenate(slabs, axis=1)
    gram_ref[...] = packed
    other_products(slab, 0, count, w_split, packed, high_ref, low_ref, out_refs)
    for copy in copies:
        copy.wait()


def second_kernel(near, width, slab, first, count, own_group, *refs):
    w_split, gram_ref, high_ref, low_ref, data_ref = refs[:5]
    *out_refs, own_ref, sems = refs[5:]
    copies = fetch(near, width, own_group, data_ref, own_ref, sems)
    other_products(slab, first, count, w_split, gram_ref[...], high_ref, low_ref, out_refs)
    for copy in copies:
        copy.wait()


def own_first_kernel(near, width, own_group, n_blocks, w_split, *refs):
    block_refs, data_ref = refs[:n_blocks], refs[n_blocks]
    *out_refs, own_ref, sems = refs[n_blocks + 1 :]
    copies = fetch(near, width, own_group, data_ref, own_ref, sems)
    for block_ref, out_ref in zip(block_refs, out_refs):
        product(w_split, *split(block_ref[0]), out_ref, 0)
    for copy in copies:
        copy.wait()


def own_last_kernel(w_split, blocks, *out_refs):
    for at, out_ref in enumerate(out_refs):
        product(w_split, *split(blocks[at]), out_ref, 0)


def side_sum_kernel(count, slab, n_got, *refs):
    own_refs, gram_ref, got_refs = refs[:count], refs[count], refs[count + 1 : count + 1 + n_got]
    out_refs = refs[count + 1 + n_got :]
    gram = gram_ref[...]
    for got in got_refs:
        gram = gram + got[slab * count :]
    for at in range(count):
        total = own_refs[at][...]
        for got in got_refs:
            total = total + got[slab * at : slab * (at + 1)]
        out_refs[at][:slab] = total
        out_refs[at][slab:] = gram


def sweep_kernel(width, *refs):
    parts, h_ref, out_ref = refs[:-2], refs[-2], refs[-1]
    rank = h_ref.shape[0]
    row_at = lax.axis_index("prow")
    total = parts[0][...]
    for part in parts[1:]:
        total = total + part[...]
    pieces = width // LANES
    cross = jnp.concatenate([total[rank * i : rank * (i + 1)] for i in range(pieces)], axis=1)
    packed = total[rank * pieces :]
    gram = jnp.concatenate(
        [packed[:, rank * i : rank * (i + 1)] for i in range(rank // GRAM_ROWS)], axis=0
    )
    h = h_ref[:, pl.ds(pl.multiple_of(row_at * width, width), width)]
    rest = cross - exact_dot(gram, h, ((1,), (0,)))
    rows = []
    for k in range(rank):
        inverse = 1.0 / gram[k : k + 1, k : k + 1]
        old = h[k : k + 1]
        fresh = jnp.maximum(old + rest[k : k + 1] * inverse, 0.0)
        rows.append(fresh)
        rest = rest - gram[:, k : k + 1] * (fresh - old)
    out_ref[...] = jnp.concatenate(rows, axis=0)


def assemble_kernel(width, pieces, out_ref):
    for peer in range(pieces.shape[0]):
        out_ref[:, width * peer : width * (peer + 1)] = pieces[peer]


def shards(n_row, n_col, data, w_trans, h_prior):
    rank, depth = w_trans.shape
    rows, cols = data.shape
    width = cols // n_row
    near = max(1, n_row // 4)
    far = n_row // near
    slab = rank * (width // LANES)
    groups = [list(range(far // 2, far)), list(range(far // 2 - 1, -1, -1))]
    count = far // 2
    sides = range(1, near)

    def permute(value, axis, turn):
        size = n_row if axis == "prow" else n_col
        return lax.ppermute(value, axis, [(i, i ^ turn) for i in range(size)])

    w_parts = [w_trans] + [permute(w_trans, "pcol", t) for t in range(1, n_col)]
    others = [(side, turn) for group in groups for side in sides for turn in group]
    high, low = call(
        functools.partial(load_kernel, near, width, others),
        [jax.ShapeDtypeStruct((len(others), rows, width), jnp.bfloat16)] * 2,
        [data], "load_other_side", 40, [HBM],
        [
            pltpu.VMEM((SLOTS, rows // PIECES, width), jnp.float32),
            pltpu.SemaphoreType.DMA((SLOTS,)),
        ],
        pl.CostEstimate(
            flops=0, bytes_accessed=8 * rows * width * len(others), transcendentals=0
        ),
    )
    outward = [floats(count * slab + GRAM_ROWS, LANES)] * len(sides)
    own_block = floats(1, rows, width)
    *sent_first, w_split, gram, own_a = call(
        functools.partial(first_kernel, near, width, slab, count, groups[0][:1], n_col),
        [
            *outward,
            jax.ShapeDtypeStruct((2 * rank, rows), jnp.bfloat16),
            floats(GRAM_ROWS, LANES),
            own_block,
        ],
        [*w_parts, high, low, data], "basis_and_other_side", 40,
        [VMEM] * (n_col + 2) + [HBM], [pltpu.SemaphoreType.DMA((1,))],
    )
    *sent_second, own_b = call(
        functools.partial(
            second_kernel, near, width, slab, len(sides) * count, count, groups[0][1:]
        ),
        [*outward, own_block],
        [w_split, gram, high, low, data], "other_side", 40,
        [VMEM] * 4 + [HBM], [pltpu.SemaphoreType.DMA((1,))],
    )
    got = [
        [permute(sent[side - 1], "prow", side) for side in sides]
        for sent in (sent_first, sent_second)
    ]
    *own_first, own_c = call(
        functools.partial(own_first_kernel, near, width, groups[1], count),
        [floats(slab, LANES)] * count + [floats(count, rows, width)],
        [w_split, own_a, own_b, data], "own_side", 40,
        [VMEM] * 3 + [HBM], [pltpu.SemaphoreType.DMA((count,))],
    )
    own_last = call(
        own_last_kernel, [floats(slab, LANES)] * count, [w_split, own_c], "own_side_end", 8
    )
    own = [own_first, own_last]
    parts = []
    for index, group in enumerate(groups):
        sums = call(
            functools.partial(side_sum_kernel, count, slab, len(sides)),
            [floats(slab + GRAM_ROWS, LANES)] * count,
            [*own[index], gram, *got[index]], "side_sum",
        )
        for turn, value in zip(group, sums):
            parts.append(permute(value, "prow", turn * near) if turn else value)
    fresh = call(
        functools.partial(sweep_kernel, width), floats(rank, width),
        [*parts, h_prior], "row_sweep",
    )
    pieces = lax.all_gather(fresh, "prow", axis=0)
    return call(
        functools.partial(assemble_kernel, width), floats(rank, cols), [pieces], "assemble"
    )


def solution(mesh):
    n_row, n_col = mesh.shape["prow"], mesh.shape["pcol"]
    placed = (P("prow", "pcol"), P(None, ("prow", "pcol")), P(None, "pcol"))
    return jax.shard_map(
        functools.partial(shards, n_row, n_col),
        mesh=mesh, in_specs=placed, out_specs=P(None, "pcol"), check_vma=False,
    )
```

```python
import functools

import jax
import jax.numpy as jnp
from jax import lax
from jax.experimental import pallas as pl
from jax.experimental.pallas import tpu as pltpu
from jax.sharding import PartitionSpec as P

LANES = 128
GRAM_ROWS = 8
PIECES = 8
VMEM = pl.BlockSpec(memory_space=pltpu.VMEM)
HBM = pl.BlockSpec(memory_space=pltpu.HBM)


def call(kernel, out_shape, operands, name, mebibytes=4, in_specs=None, scratch=(), cost=None):
    many = isinstance(out_shape, list)
    return pl.pallas_call(
        kernel,
        out_shape=out_shape,
        in_specs=in_specs or [VMEM] * len(operands),
        out_specs=[VMEM] * len(out_shape) if many else VMEM,
        compiler_params=pltpu.CompilerParams(vmem_limit_bytes=mebibytes * 1024 * 1024),
        scratch_shapes=list(scratch),
        cost_estimate=cost,
        name=name,
    )(*operands)


def floats(*shape):
    return jax.ShapeDtypeStruct(shape, jnp.float32)


def split(value):
    high = value.astype(jnp.bfloat16)
    low = (value - high.astype(jnp.float32)).astype(jnp.bfloat16)
    return high, low


def exact_dot(left, right, dims):
    return lax.dot_general(
        left, right, (dims, ((), ())),
        precision=lax.Precision.HIGHEST, preferred_element_type=jnp.float32,
    )


def block_start(near, width, side_turn, level_turn):
    row_at = lax.axis_index("prow")
    side, level = lax.rem(row_at, near), lax.div(row_at, near)
    peer = (level ^ level_turn) * near + (side ^ side_turn)
    return pl.multiple_of(peer * width, width)


def start_copies(near, width, turns, data_ref, out_ref, sems):
    depth = data_ref.shape[0] // PIECES
    copies = []
    for at, (side_turn, level_turn) in enumerate(turns):
        columns = pl.ds(block_start(near, width, side_turn, level_turn), width)
        for piece in range(PIECES):
            rows = pl.ds(piece * depth, depth)
            copy = pltpu.make_async_copy(
                data_ref.at[rows, columns], out_ref.at[at, rows], sems.at[at, piece]
            )
            copy.start()
            copies.append(copy)
    return copies


def load_kernel(near, width, turns, data_ref, high_ref, low_ref, stage, sems):
    depth = data_ref.shape[0] // PIECES
    for index, copy in enumerate(start_copies(near, width, turns, data_ref, stage, sems)):
        at, rows = index // PIECES, pl.ds(index % PIECES * depth, depth)
        copy.wait()
        high, low = split(stage[at, rows])
        high_ref[at, rows] = high
        low_ref[at, rows] = low


def fetch(near, width, group, data_ref, out_ref, sems):
    return start_copies(near, width, [(0, turn) for turn in group], data_ref, out_ref, sems)


def product(w_split, high, low, out_ref, row):
    rank = w_split.shape[0] // 2
    upper = jnp.dot(w_split[...], high, preferred_element_type=jnp.float32)
    cross = (
        upper[:rank]
        + upper[rank:]
        + jnp.dot(w_split[:rank], low, preferred_element_type=jnp.float32)
    )
    for i in range(cross.shape[1] // LANES):
        at = row + rank * i
        out_ref[at : at + rank] = cross[:, LANES * i : LANES * (i + 1)]


def other_products(slab, first, count, w_split, gram, high_ref, low_ref, out_refs):
    for index, out_ref in enumerate(out_refs):
        for at in range(count):
            block = first + index * count + at
            product(w_split, high_ref[block], low_ref[block], out_ref, slab * at)
        out_ref[slab * count :] = gram


def first_kernel(near, width, slab, count, own_group, n_col, *refs):
    w_refs, (high_ref, low_ref, data_ref) = refs[:n_col], refs[n_col : n_col + 3]
    *out_refs, w_split, gram_ref, own_ref, sems = refs[n_col + 3 :]
    copies = fetch(near, width, own_group, data_ref, own_ref, sems)
    rank, depth = w_refs[0].shape
    col_at = lax.axis_index("pcol")
    gram = jnp.zeros((rank, rank), jnp.float32)
    for turn in range(n_col):
        part = w_refs[turn][...]
        high, low = split(part)
        columns = pl.ds(pl.multiple_of((col_at ^ turn) * depth, depth), depth)
        w_split[:rank, columns] = high
        w_split[rank:, columns] = low
        gram = gram + exact_dot(part, part, ((1,), (1,)))
    slabs = [gram[GRAM_ROWS * i : GRAM_ROWS * (i + 1)] for i in range(rank // GRAM_ROWS)]
    packed = jnp.concatenate(slabs, axis=1)
    gram_ref[...] = packed
    other_products(slab, 0, count, w_split, packed, high_ref, low_ref, out_refs)
    for copy in copies:
        copy.wait()


def second_kernel(near, width, slab, first, count, own_group, *refs):
    w_split, gram_ref, high_ref, low_ref, data_ref = refs[:5]
    *out_refs, own_ref, sems = refs[5:]
    copies = fetch(near, width, own_group, data_ref, own_ref, sems)
    other_products(slab, first, count, w_split, gram_ref[...], high_ref, low_ref, out_refs)
    for copy in copies:
        copy.wait()


def own_first_kernel(near, width, own_group, n_blocks, w_split, *refs):
    block_refs, data_ref = refs[:n_blocks], refs[n_blocks]
    *out_refs, own_ref, sems = refs[n_blocks + 1 :]
    copies = fetch(near, width, own_group, data_ref, own_ref, sems)
    for block_ref, out_ref in zip(block_refs, out_refs):
        product(w_split, *split(block_ref[0]), out_ref, 0)
    for copy in copies:
        copy.wait()


def own_last_kernel(w_split, blocks, *out_refs):
    for at, out_ref in enumerate(out_refs):
        product(w_split, *split(blocks[at]), out_ref, 0)


def side_sum_kernel(count, slab, n_got, *refs):
    own_refs, gram_ref, got_refs = refs[:count], refs[count], refs[count + 1 : count + 1 + n_got]
    out_refs = refs[count + 1 + n_got :]
    gram = gram_ref[...]
    for got in got_refs:
        gram = gram + got[slab * count :]
    for at in range(count):
        total = own_refs[at][...]
        for got in got_refs:
            total = total + got[slab * at : slab * (at + 1)]
        out_refs[at][:slab] = total
        out_refs[at][slab:] = gram


def sweep_kernel(width, *refs):
    parts, h_ref, out_ref = refs[:-2], refs[-2], refs[-1]
    rank = h_ref.shape[0]
    row_at = lax.axis_index("prow")
    total = parts[0][...]
    for part in parts[1:]:
        total = total + part[...]
    pieces = width // LANES
    cross = jnp.concatenate([total[rank * i : rank * (i + 1)] for i in range(pieces)], axis=1)
    packed = total[rank * pieces :]
    gram = jnp.concatenate(
        [packed[:, rank * i : rank * (i + 1)] for i in range(rank // GRAM_ROWS)], axis=0
    )
    h = h_ref[:, pl.ds(pl.multiple_of(row_at * width, width), width)]
    rest = cross - exact_dot(gram, h, ((1,), (0,)))
    rows = []
    for k in range(rank):
        inverse = 1.0 / gram[k : k + 1, k : k + 1]
        old = h[k : k + 1]
        fresh = jnp.maximum(old + rest[k : k + 1] * inverse, 0.0)
        rows.append(fresh)
        rest = rest - gram[:, k : k + 1] * (fresh - old)
    done = jnp.concatenate(rows, axis=0)
    for peer in range(out_ref.shape[0]):
        out_ref[peer] = done


def assemble_kernel(width, pieces, out_ref):
    for peer in range(pieces.shape[0]):
        out_ref[:, width * peer : width * (peer + 1)] = pieces[peer]


def shards(n_row, n_col, data, w_trans, h_prior):
    rank, depth = w_trans.shape
    rows, cols = data.shape
    width = cols // n_row
    near = max(1, n_row // 4)
    far = n_row // near
    slab = rank * (width // LANES)
    groups = [list(range(far // 2, far)), list(range(far // 2 - 1, -1, -1))]
    count = far // 2
    sides = range(1, near)

    def permute(value, axis, turn):
        size = n_row if axis == "prow" else n_col
        return lax.ppermute(value, axis, [(i, i ^ turn) for i in range(size)])

    w_parts = [w_trans] + [permute(w_trans, "pcol", t) for t in range(1, n_col)]
    others = [(side, turn) for group in groups for side in sides for turn in group]
    high, low = call(
        functools.partial(load_kernel, near, width, others),
        [jax.ShapeDtypeStruct((len(others), rows, width), jnp.bfloat16)] * 2,
        [data], "load_other_side", 40, [HBM],
        [
            pltpu.VMEM((len(others), rows, width), jnp.float32),
            pltpu.SemaphoreType.DMA((len(others), PIECES)),
        ],
        pl.CostEstimate(
            flops=0, bytes_accessed=8 * rows * width * len(others), transcendentals=0
        ),
    )
    outward = [floats(count * slab + GRAM_ROWS, LANES)] * len(sides)
    own_block = floats(1, rows, width)
    *sent_first, w_split, gram, own_a = call(
        functools.partial(first_kernel, near, width, slab, count, groups[0][:1], n_col),
        [
            *outward,
            jax.ShapeDtypeStruct((2 * rank, rows), jnp.bfloat16),
            floats(GRAM_ROWS, LANES),
            own_block,
        ],
        [*w_parts, high, low, data], "basis_and_other_side", 40,
        [VMEM] * (n_col + 2) + [HBM], [pltpu.SemaphoreType.DMA((1, PIECES))],
    )
    *sent_second, own_b = call(
        functools.partial(
            second_kernel, near, width, slab, len(sides) * count, count, groups[0][1:]
        ),
        [*outward, own_block],
        [w_split, gram, high, low, data], "other_side", 40,
        [VMEM] * 4 + [HBM], [pltpu.SemaphoreType.DMA((1, PIECES))],
    )
    got = [
        [permute(sent[side - 1], "prow", side) for side in sides]
        for sent in (sent_first, sent_second)
    ]
    *own_first, own_c = call(
        functools.partial(own_first_kernel, near, width, groups[1], count),
        [floats(slab, LANES)] * count + [floats(count, rows, width)],
        [w_split, own_a, own_b, data], "own_side", 40,
        [VMEM] * 3 + [HBM], [pltpu.SemaphoreType.DMA((count, PIECES))],
    )
    own_last = call(
        own_last_kernel, [floats(slab, LANES)] * count, [w_split, own_c], "own_side_end", 8
    )
    own = [own_first, own_last]
    parts = []
    for index, group in enumerate(groups):
        sums = call(
            functools.partial(side_sum_kernel, count, slab, len(sides)),
            [floats(slab + GRAM_ROWS, LANES)] * count,
            [*own[index], gram, *got[index]], "side_sum",
        )
        for turn, value in zip(group, sums):
            parts.append(permute(value, "prow", turn * near) if turn else value)
    fresh = call(
        functools.partial(sweep_kernel, width), floats(n_row, rank, width),
        [*parts, h_prior], "row_sweep",
    )
    pieces = lax.all_to_all(fresh, "prow", 0, 0)
    return call(
        functools.partial(assemble_kernel, width), floats(rank, cols), [pieces], "assemble"
    )


def solution(mesh):
    n_row, n_col = mesh.shape["prow"], mesh.shape["pcol"]
    placed = (P("prow", "pcol"), P(None, ("prow", "pcol")), P(None, "pcol"))
    return jax.shard_map(
        functools.partial(shards, n_row, n_col),
        mesh=mesh, in_specs=placed, out_specs=P(None, "pcol"), check_vma=False,
    )
```

```python
import functools

import jax
import jax.numpy as jnp
from jax import lax
from jax.experimental import pallas as pl
from jax.experimental.pallas import tpu as pltpu
from jax.sharding import PartitionSpec as P

LANES = 128
GRAM_ROWS = 8
PIECES = 8
VMEM = pl.BlockSpec(memory_space=pltpu.VMEM)
HBM = pl.BlockSpec(memory_space=pltpu.HBM)


def call(kernel, out_shape, operands, name, mebibytes=4, in_specs=None, scratch=(), cost=None):
    many = isinstance(out_shape, list)
    return pl.pallas_call(
        kernel,
        out_shape=out_shape,
        in_specs=in_specs or [VMEM] * len(operands),
        out_specs=[VMEM] * len(out_shape) if many else VMEM,
        compiler_params=pltpu.CompilerParams(vmem_limit_bytes=mebibytes * 1024 * 1024),
        scratch_shapes=list(scratch),
        cost_estimate=cost,
        name=name,
    )(*operands)


def floats(*shape):
    return jax.ShapeDtypeStruct(shape, jnp.float32)


def split(value):
    high = value.astype(jnp.bfloat16)
    low = (value - high.astype(jnp.float32)).astype(jnp.bfloat16)
    return high, low


def exact_dot(left, right, dims):
    return lax.dot_general(
        left, right, (dims, ((), ())),
        precision=lax.Precision.HIGHEST, preferred_element_type=jnp.float32,
    )


def block_start(near, width, side_turn, level_turn):
    row_at = lax.axis_index("prow")
    side, level = lax.rem(row_at, near), lax.div(row_at, near)
    peer = (level ^ level_turn) * near + (side ^ side_turn)
    return pl.multiple_of(peer * width, width)


def start_copies(near, width, turns, data_ref, out_ref, sems):
    depth = data_ref.shape[0] // PIECES
    copies = []
    for at, (side_turn, level_turn) in enumerate(turns):
        columns = pl.ds(block_start(near, width, side_turn, level_turn), width)
        for piece in range(PIECES):
            rows = pl.ds(piece * depth, depth)
            copy = pltpu.make_async_copy(
                data_ref.at[rows, columns], out_ref.at[at, rows], sems.at[at, piece]
            )
            copy.start()
            copies.append(copy)
    return copies


def load_kernel(near, width, turn_lists, data_ref, *refs):
    count = len(turn_lists)
    copies = []
    for turns, out_ref, sems in zip(turn_lists, refs[:count], refs[count:]):
        copies += start_copies(near, width, turns, data_ref, out_ref, sems)
    for copy in copies:
        copy.wait()


def beside_copies(copies, compute):
    pl.when(lax.axis_index("prow") >= 0)(compute)
    for copy in copies:
        copy.wait()


def product(w_split, block, out_ref, row):
    rank = w_split.shape[0] // 2
    high, low = split(block)
    upper = jnp.dot(w_split[...], high, preferred_element_type=jnp.float32)
    cross = (
        upper[:rank]
        + upper[rank:]
        + jnp.dot(w_split[:rank], low, preferred_element_type=jnp.float32)
    )
    for i in range(cross.shape[1] // LANES):
        at = row + rank * i
        out_ref[at : at + rank] = cross[:, LANES * i : LANES * (i + 1)]


def other_products(slab, first, count, w_split, gram, blocks, out_refs):
    for index, out_ref in enumerate(out_refs):
        for at in range(count):
            product(w_split, blocks[first + index * count + at], out_ref, slab * at)
        out_ref[slab * count :] = gram


def first_kernel(near, width, slab, count, own_turns, n_col, *refs):
    w_refs, (blocks, data_ref) = refs[:n_col], refs[n_col : n_col + 2]
    *out_refs, w_split, gram_ref, own_ref, sems = refs[n_col + 2 :]
    rank, depth = w_refs[0].shape
    col_at = lax.axis_index("pcol")

    def compute():
        gram = jnp.zeros((rank, rank), jnp.float32)
        for turn in range(n_col):
            part = w_refs[turn][...]
            high, low = split(part)
            columns = pl.ds(pl.multiple_of((col_at ^ turn) * depth, depth), depth)
            w_split[:rank, columns] = high
            w_split[rank:, columns] = low
            gram = gram + exact_dot(part, part, ((1,), (1,)))
        slabs = [gram[GRAM_ROWS * i : GRAM_ROWS * (i + 1)] for i in range(rank // GRAM_ROWS)]
        packed = jnp.concatenate(slabs, axis=1)
        gram_ref[...] = packed
        other_products(slab, 0, count, w_split, packed, blocks, out_refs)

    beside_copies(start_copies(near, width, own_turns, data_ref, own_ref, sems), compute)


def second_kernel(near, width, slab, first, count, own_turns, *refs):
    w_split, gram_ref, blocks, data_ref = refs[:4]
    *out_refs, own_ref, sems = refs[4:]

    def compute():
        other_products(slab, first, count, w_split, gram_ref[...], blocks, out_refs)

    beside_copies(start_copies(near, width, own_turns, data_ref, own_ref, sems), compute)


def own_first_kernel(near, width, own_turns, n_blocks, w_split, *refs):
    block_refs, data_ref = refs[:n_blocks], refs[n_blocks]
    *out_refs, own_ref, sems = refs[n_blocks + 1 :]

    def compute():
        for block_ref, out_ref in zip(block_refs, out_refs):
            product(w_split, block_ref[0], out_ref, 0)

    beside_copies(start_copies(near, width, own_turns, data_ref, own_ref, sems), compute)


def own_last_kernel(w_split, *refs):
    count = len(refs) // 2
    for block_ref, out_ref in zip(refs[:count], refs[count:]):
        product(w_split, block_ref[0], out_ref, 0)


def side_sum_kernel(count, slab, n_got, *refs):
    own_refs, gram_ref, got_refs = refs[:count], refs[count], refs[count + 1 : count + 1 + n_got]
    out_refs = refs[count + 1 + n_got :]
    gram = gram_ref[...]
    for got in got_refs:
        gram = gram + got[slab * count :]
    for at in range(count):
        total = own_refs[at][...]
        for got in got_refs:
            total = total + got[slab * at : slab * (at + 1)]
        out_refs[at][:slab] = total
        out_refs[at][slab:] = gram


def sweep_kernel(width, *refs):
    parts, h_ref, out_ref = refs[:-2], refs[-2], refs[-1]
    rank = h_ref.shape[0]
    row_at = lax.axis_index("prow")
    total = parts[0][...]
    for part in parts[1:]:
        total = total + part[...]
    pieces = width // LANES
    cross = jnp.concatenate([total[rank * i : rank * (i + 1)] for i in range(pieces)], axis=1)
    packed = total[rank * pieces :]
    gram = jnp.concatenate(
        [packed[:, rank * i : rank * (i + 1)] for i in range(rank // GRAM_ROWS)], axis=0
    )
    h = h_ref[:, pl.ds(pl.multiple_of(row_at * width, width), width)]
    rest = cross - exact_dot(gram, h, ((1,), (0,)))
    rows = []
    for k in range(rank):
        inverse = 1.0 / gram[k : k + 1, k : k + 1]
        old = h[k : k + 1]
        fresh = jnp.maximum(old + rest[k : k + 1] * inverse, 0.0)
        rows.append(fresh)
        rest = rest - gram[:, k : k + 1] * (fresh - old)
    done = jnp.concatenate(rows, axis=0)
    for peer in range(out_ref.shape[0]):
        out_ref[peer] = done


def assemble_kernel(width, pieces, out_ref):
    for peer in range(pieces.shape[0]):
        out_ref[:, width * peer : width * (peer + 1)] = pieces[peer]


def shards(n_row, n_col, data, w_trans, h_prior):
    rank, depth = w_trans.shape
    rows, cols = data.shape
    width = cols // n_row
    near = max(1, n_row // 4)
    far = n_row // near
    slab = rank * (width // LANES)
    groups = [list(range(far // 2, far)), list(range(far // 2 - 1, -1, -1))]
    count = far // 2
    sides = range(1, near)

    def permute(value, axis, turn):
        size = n_row if axis == "prow" else n_col
        return lax.ppermute(value, axis, [(i, i ^ turn) for i in range(size)])

    w_parts = [w_trans] + [permute(w_trans, "pcol", t) for t in range(1, n_col)]
    others = [(side, turn) for group in groups for side in sides for turn in group]
    owns = [[(0, turn)] for group in groups for turn in group]
    own_block = floats(1, rows, width)
    fetch_sems = pltpu.SemaphoreType.DMA((1, PIECES))
    blocks, own_a = call(
        functools.partial(load_kernel, near, width, [others, owns[0]]),
        [floats(len(others), rows, width), own_block],
        [data], "load_blocks", 40, [HBM],
        [pltpu.SemaphoreType.DMA((len(others), PIECES)), fetch_sems],
        pl.CostEstimate(
            flops=0, bytes_accessed=8 * rows * width * (len(others) + 1), transcendentals=0
        ),
    )
    outward = [floats(count * slab + GRAM_ROWS, LANES)] * len(sides)
    *sent_first, w_split, gram, own_b = call(
        functools.partial(first_kernel, near, width, slab, count, owns[1], n_col),
        [
            *outward,
            jax.ShapeDtypeStruct((2 * rank, rows), jnp.bfloat16),
            floats(GRAM_ROWS, LANES),
            own_block,
        ],
        [*w_parts, blocks, data], "basis_and_other_side", 40,
        [VMEM] * (n_col + 1) + [HBM], [fetch_sems],
    )
    *sent_second, own_c = call(
        functools.partial(
            second_kernel, near, width, slab, len(sides) * count, count, owns[2]
        ),
        [*outward, own_block],
        [w_split, gram, blocks, data], "other_side", 40, [VMEM] * 3 + [HBM], [fetch_sems],
    )
    got = [
        [permute(sent[side - 1], "prow", side) for side in sides]
        for sent in (sent_first, sent_second)
    ]
    *own_first, own_d = call(
        functools.partial(own_first_kernel, near, width, owns[3], count),
        [floats(slab, LANES)] * count + [own_block],
        [w_split, own_a, own_b, data], "own_side", 40, [VMEM] * 3 + [HBM], [fetch_sems],
    )
    own_last = call(
        own_last_kernel, [floats(slab, LANES)] * count, [w_split, own_c, own_d], "own_side_end", 8
    )
    own = [own_first, own_last]
    parts = []
    for index, group in enumerate(groups):
        sums = call(
            functools.partial(side_sum_kernel, count, slab, len(sides)),
            [floats(slab + GRAM_ROWS, LANES)] * count,
            [*own[index], gram, *got[index]], "side_sum",
        )
        for turn, value in zip(group, sums):
            parts.append(permute(value, "prow", turn * near) if turn else value)
    fresh = call(
        functools.partial(sweep_kernel, width), floats(n_row, rank, width),
        [*parts, h_prior], "row_sweep",
    )
    pieces = lax.all_to_all(fresh, "prow", 0, 0)
    return call(
        functools.partial(assemble_kernel, width), floats(rank, cols), [pieces], "assemble"
    )


def solution(mesh):
    n_row, n_col = mesh.shape["prow"], mesh.shape["pcol"]
    placed = (P("prow", "pcol"), P(None, ("prow", "pcol")), P(None, "pcol"))
    return jax.shard_map(
        functools.partial(shards, n_row, n_col),
        mesh=mesh, in_specs=placed, out_specs=P(None, "pcol"), check_vma=False,
    )
```

```python
import functools

import jax
import jax.numpy as jnp
from jax import lax
from jax.experimental import pallas as pl
from jax.experimental.pallas import tpu as pltpu
from jax.sharding import PartitionSpec as P

LANES = 128
GRAM_ROWS = 8
VMEM = pl.BlockSpec(memory_space=pltpu.VMEM)
HBM = pl.BlockSpec(memory_space=pltpu.HBM)


def call(kernel, out_shape, operands, name, mebibytes=4, in_specs=None, scratch=(), cost=None):
    many = isinstance(out_shape, list)
    return pl.pallas_call(
        kernel,
        out_shape=out_shape,
        in_specs=in_specs or [VMEM] * len(operands),
        out_specs=[VMEM] * len(out_shape) if many else VMEM,
        compiler_params=pltpu.CompilerParams(vmem_limit_bytes=mebibytes * 1024 * 1024),
        scratch_shapes=list(scratch),
        cost_estimate=cost,
        name=name,
    )(*operands)


def floats(*shape):
    return jax.ShapeDtypeStruct(shape, jnp.float32)


def split(value):
    high = value.astype(jnp.bfloat16)
    low = (value - high.astype(jnp.float32)).astype(jnp.bfloat16)
    return high, low


def exact_dot(left, right, dims):
    return lax.dot_general(
        left, right, (dims, ((), ())),
        precision=lax.Precision.HIGHEST, preferred_element_type=jnp.float32,
    )


def block_start(near, width, side_turn, level_turn):
    row_at = lax.axis_index("prow")
    side, level = lax.rem(row_at, near), lax.div(row_at, near)
    peer = (level ^ level_turn) * near + (side ^ side_turn)
    return pl.multiple_of(peer * width, width)


def row_part(depth, turn):
    return pl.ds(pl.multiple_of((lax.axis_index("pcol") ^ turn) * depth, depth), depth)


def start_copies(near, width, n_col, blocks, data_ref, out_ref, sems):
    depth = data_ref.shape[0] // n_col
    copies = {}
    for at, turn in blocks:
        columns = pl.ds(block_start(near, width, *at[1]), width)
        rows = row_part(depth, turn)
        copies[at[0], turn] = pltpu.make_async_copy(
            data_ref.at[rows, columns], out_ref.at[at[0], rows], sems.at[at[0], turn]
        )
        copies[at[0], turn].start()
    return copies


def split_basis(part_ref, out_ref, turn):
    rank = part_ref.shape[0]
    part = part_ref[...]
    high, low = split(part)
    out_ref[turn, :rank] = high
    out_ref[turn, rank:] = low
    return exact_dot(part, part, ((1,), (1,)))


def product(w_split, blocks, at, turns):
    rank, depth = w_split.shape[1] // 2, w_split.shape[2]
    total = None
    for turn in turns:
        high, low = split(blocks[at, row_part(depth, turn)])
        upper = jnp.dot(w_split[turn], high, preferred_element_type=jnp.float32)
        term = (
            upper[:rank]
            + upper[rank:]
            + jnp.dot(w_split[turn, :rank], low, preferred_element_type=jnp.float32)
        )
        total = term if total is None else total + term
    return total


def store(cross, out_ref, row, before=None):
    rank = cross.shape[0]
    for i in range(cross.shape[1] // LANES):
        rows = slice(row + rank * i, row + rank * (i + 1))
        piece = cross[:, LANES * i : LANES * (i + 1)]
        out_ref[rows] = piece if before is None else piece + before[rows]


def own_region(compute):
    pl.when(lax.axis_index("prow") >= 0)(compute)


def load_kernel(near, width, n_col, early, late, others, *refs):
    w_refs, data_ref = refs[: len(early)], refs[len(early)]
    blocks, begun, w_split, gram_ref, sems = refs[len(early) + 1 :]
    order = [(at, turn) for turn in early + late for at in enumerate(others)]
    copies = start_copies(near, width, n_col, order, data_ref, blocks, sems)

    def compute():
        gram = split_basis(w_refs[0], w_split, early[0])
        for turn, ref in list(zip(early, w_refs))[1:]:
            gram = gram + split_basis(ref, w_split, turn)
        gram_ref[...] = gram
        for at in range(len(others)):
            for turn in early:
                copies[at, turn].wait()
            store(product(w_split, blocks, at, early), begun.at[at], 0)

    own_region(compute)
    for (_, turn), copy in copies.items():
        if turn not in early:
            copy.wait()


def finish(slab, first, count, w_split, late, blocks, begun, gram, out_refs):
    for index, out_ref in enumerate(out_refs):
        for at in range(count):
            block = first + index * count + at
            store(
                product(w_split, blocks, block, late), out_ref.at[pl.ds(slab * at, slab)], 0,
                begun.at[block],
            )
        if gram is not None:
            out_ref[slab * count :] = gram


def first_kernel(slab, count, early, late, *refs):
    w_refs, (w_early, gram_early, blocks, begun) = refs[: len(late)], refs[len(late) :][:4]
    *out_refs, w_split, gram_ref = refs[len(late) + 4 :]
    rank = w_refs[0].shape[0]
    for turn in early:
        w_split[turn] = w_early[turn]
    gram = gram_early[...]
    for turn, ref in zip(late, w_refs):
        gram = gram + split_basis(ref, w_split, turn)
    slabs = [gram[GRAM_ROWS * i : GRAM_ROWS * (i + 1)] for i in range(rank // GRAM_ROWS)]
    packed = jnp.concatenate(slabs, axis=1)
    gram_ref[...] = packed
    finish(slab, 0, count, w_split, late, blocks, begun, packed, out_refs)


def second_kernel(near, width, n_col, slab, count, n_sides, late, owns, *refs):
    w_split, blocks, begun, data_ref = refs[:4]
    out_refs, own_refs, (own_blocks, sems) = refs[4 : 4 + n_sides], refs[4 + n_sides : -2], refs[-2:]
    order = [(at, turn) for at in enumerate(owns) for turn in range(n_col)]
    copies = start_copies(near, width, n_col, order, data_ref, own_blocks, sems)

    def compute():
        first = n_sides * count
        finish(slab, first, count, w_split, late, blocks, begun, None, out_refs)

    def multiply(at):
        for turn in range(n_col):
            copies[at, turn].wait()
        store(product(w_split, own_blocks, at, range(n_col)), own_refs[at], 0)

    own_region(compute)
    for at in range(len(owns)):
        own_region(functools.partial(multiply, at))


def side_sum_kernel(count, slab, n_got, gram_sent, *refs):
    own_refs, gram_ref, got_refs = refs[:count], refs[count], refs[count + 1 : count + 1 + n_got]
    out_refs = refs[count + 1 + n_got :]
    gram = gram_ref[...]
    if gram_sent:
        for got in got_refs:
            gram = gram + got[slab * count :]
        out_refs[count][...] = gram
    for at in range(count):
        total = own_refs[at][...]
        for got in got_refs:
            total = total + got[slab * at : slab * (at + 1)]
        out_refs[at][:slab] = total
        out_refs[at][slab:] = gram


def sweep_kernel(width, *refs):
    parts, h_ref, out_ref = refs[:-2], refs[-2], refs[-1]
    rank = h_ref.shape[0]
    row_at = lax.axis_index("prow")
    total = parts[0][...]
    for part in parts[1:]:
        total = total + part[...]
    pieces = width // LANES
    cross = jnp.concatenate([total[rank * i : rank * (i + 1)] for i in range(pieces)], axis=1)
    packed = total[rank * pieces :]
    gram = jnp.concatenate(
        [packed[:, rank * i : rank * (i + 1)] for i in range(rank // GRAM_ROWS)], axis=0
    )
    h = h_ref[:, pl.ds(pl.multiple_of(row_at * width, width), width)]
    rest = cross - exact_dot(gram, h, ((1,), (0,)))
    rows = []
    for k in range(rank):
        inverse = 1.0 / gram[k : k + 1, k : k + 1]
        old = h[k : k + 1]
        fresh = jnp.maximum(old + rest[k : k + 1] * inverse, 0.0)
        rows.append(fresh)
        rest = rest - gram[:, k : k + 1] * (fresh - old)
    done = jnp.concatenate(rows, axis=0)
    for peer in range(out_ref.shape[0]):
        out_ref[peer] = done


def assemble_kernel(width, pieces, out_ref):
    for peer in range(pieces.shape[0]):
        out_ref[:, width * peer : width * (peer + 1)] = pieces[peer]


def shards(n_row, n_col, data, w_trans, h_prior):
    rank, depth = w_trans.shape
    rows, cols = data.shape
    width = cols // n_row
    near = max(1, n_row // 4)
    far = n_row // near
    slab = rank * (width // LANES)
    groups = [list(range(far // 2, far)), list(range(far // 2 - 1, -1, -1))]
    count = far // 2
    sides = range(1, near)

    def permute(value, axis, turn):
        size = n_row if axis == "prow" else n_col
        return lax.ppermute(value, axis, [(i, i ^ turn) for i in range(size)])

    w_parts = [w_trans] + [permute(w_trans, "pcol", t) for t in range(1, n_col)]
    early = list(range(1, min(2, n_col)))
    late = [turn for turn in range(n_col) if turn not in early]
    others = [(side, turn) for group in groups for side in sides for turn in group]
    owns = [(0, turn) for group in groups for turn in group]
    split_parts = jax.ShapeDtypeStruct((n_col, 2 * rank, depth), jnp.bfloat16)
    outward = [floats(count * slab + GRAM_ROWS, LANES)] * len(sides)
    blocks, begun, w_early, gram_early = call(
        functools.partial(load_kernel, near, width, n_col, early, late, others),
        [
            floats(len(others), rows, width),
            floats(len(others), slab, LANES),
            split_parts,
            floats(rank, rank),
        ],
        [*(w_parts[t] for t in early), data], "load_other_side", 40,
        [VMEM] * len(early) + [HBM], [pltpu.SemaphoreType.DMA((len(others), n_col))],
        pl.CostEstimate(
            flops=0, bytes_accessed=8 * rows * width * len(others), transcendentals=0
        ),
    )
    *sent_first, w_split, gram = call(
        functools.partial(first_kernel, slab, count, early, late),
        [*outward, split_parts, floats(GRAM_ROWS, LANES)],
        [*(w_parts[t] for t in late), w_early, gram_early, blocks, begun], "first_group", 8,
    )
    got = [[permute(sent_first[side - 1], "prow", side) for side in sides]]
    outs = call(
        functools.partial(
            second_kernel, near, width, n_col, slab, count, len(sides), late, owns
        ),
        [floats(count * slab, LANES)] * len(sides) + [floats(slab, LANES)] * len(owns),
        [w_split, blocks, begun, data], "second_group_and_own_side", 40,
        [VMEM] * 3 + [HBM],
        [
            pltpu.VMEM((len(owns), rows, width), jnp.float32),
            pltpu.SemaphoreType.DMA((len(owns), n_col)),
        ],
    )
    sent_second, own = outs[: len(sides)], outs[len(sides) :]
    got.append([permute(sent_second[side - 1], "prow", side) for side in sides])
    parts = []
    for index, group in enumerate(groups):
        gram_sent = index == 0
        sums = call(
            functools.partial(side_sum_kernel, count, slab, len(sides), gram_sent),
            [floats(slab + GRAM_ROWS, LANES)] * count + [floats(GRAM_ROWS, LANES)] * gram_sent,
            [*own[index * count : (index + 1) * count], gram, *got[index]], "side_sum",
        )
        if gram_sent:
            *sums, gram = sums
        for turn, value in zip(group, sums):
            parts.append(permute(value, "prow", turn * near) if turn else value)
    fresh = call(
        functools.partial(sweep_kernel, width), floats(n_row, rank, width),
        [*parts, h_prior], "row_sweep",
    )
    pieces = lax.all_to_all(fresh, "prow", 0, 0)
    return call(
        functools.partial(assemble_kernel, width), floats(rank, cols), [pieces], "assemble"
    )


def solution(mesh):
    n_row, n_col = mesh.shape["prow"], mesh.shape["pcol"]
    placed = (P("prow", "pcol"), P(None, ("prow", "pcol")), P(None, "pcol"))
    return jax.shard_map(
        functools.partial(shards, n_row, n_col),
        mesh=mesh, in_specs=placed, out_specs=P(None, "pcol"), check_vma=False,
    )
```

```python
import functools

import jax
import jax.numpy as jnp
from jax import lax
from jax.experimental import pallas as pl
from jax.experimental.pallas import tpu as pltpu
from jax.sharding import PartitionSpec as P

LANES = 128
GRAM_ROWS = 8
VMEM = pl.BlockSpec(memory_space=pltpu.VMEM)
HBM = pl.BlockSpec(memory_space=pltpu.HBM)


def call(kernel, out_shape, operands, name, mebibytes=4, in_specs=None, scratch=(), cost=None):
    many = isinstance(out_shape, list)
    return pl.pallas_call(
        kernel,
        out_shape=out_shape,
        in_specs=in_specs or [VMEM] * len(operands),
        out_specs=[VMEM] * len(out_shape) if many else VMEM,
        compiler_params=pltpu.CompilerParams(vmem_limit_bytes=mebibytes * 1024 * 1024),
        scratch_shapes=list(scratch),
        cost_estimate=cost,
        name=name,
    )(*operands)


def floats(*shape):
    return jax.ShapeDtypeStruct(shape, jnp.float32)


def split(value):
    high = value.astype(jnp.bfloat16)
    low = (value - high.astype(jnp.float32)).astype(jnp.bfloat16)
    return high, low


def exact_dot(left, right, dims):
    return lax.dot_general(
        left, right, (dims, ((), ())),
        precision=lax.Precision.HIGHEST, preferred_element_type=jnp.float32,
    )


def block_start(near, width, side_turn, level_turn):
    row_at = lax.axis_index("prow")
    side, level = lax.rem(row_at, near), lax.div(row_at, near)
    peer = (level ^ level_turn) * near + (side ^ side_turn)
    return pl.multiple_of(peer * width, width)


def row_part(depth, turn):
    return pl.ds(pl.multiple_of((lax.axis_index("pcol") ^ turn) * depth, depth), depth)


def block_copies(near, width, n_col, order, data_ref, out_ref, sems):
    depth = data_ref.shape[0] // n_col
    copies = {}
    for (at, turns), turn in order:
        columns = pl.ds(block_start(near, width, *turns), width)
        rows = row_part(depth, turn)
        copies[at, turn] = pltpu.make_async_copy(
            data_ref.at[rows, columns], out_ref.at[at, rows], sems.at[at, turn]
        )
    return copies


def split_basis(part_ref, out_ref, turn):
    rank = part_ref.shape[0]
    part = part_ref[...]
    high, low = split(part)
    out_ref[turn, :rank] = high
    out_ref[turn, rank:] = low
    return exact_dot(part, part, ((1,), (1,)))


def product(w_split, blocks, at, turns):
    rank, depth = w_split.shape[1] // 2, w_split.shape[2]
    total = None
    for turn in turns:
        high, low = split(blocks[at, row_part(depth, turn)])
        upper = jnp.dot(w_split[turn], high, preferred_element_type=jnp.float32)
        term = (
            upper[:rank]
            + upper[rank:]
            + jnp.dot(w_split[turn, :rank], low, preferred_element_type=jnp.float32)
        )
        total = term if total is None else total + term
    return total


def store(cross, out_ref, row, before=None):
    rank = cross.shape[0]
    for i in range(cross.shape[1] // LANES):
        rows = slice(row + rank * i, row + rank * (i + 1))
        piece = cross[:, LANES * i : LANES * (i + 1)]
        out_ref[rows] = piece if before is None else piece + before[rows]


def own_region(compute):
    pl.when(lax.axis_index("prow") >= 0)(compute)


def load_kernel(near, width, n_col, early, late, others, *refs):
    w_refs, data_ref = refs[: len(early)], refs[len(early)]
    blocks, begun, w_split, gram_ref, sems = refs[len(early) + 1 :]
    order = [(at, turn) for turn in early + late for at in enumerate(others)]
    copies = block_copies(near, width, n_col, order, data_ref, blocks, sems)
    for copy in copies.values():
        copy.start()

    def compute():
        gram = split_basis(w_refs[0], w_split, early[0])
        for turn, ref in list(zip(early, w_refs))[1:]:
            gram = gram + split_basis(ref, w_split, turn)
        gram_ref[...] = gram
        for at in range(len(others)):
            for turn in early:
                copies[at, turn].wait()
            store(product(w_split, blocks, at, early), begun.at[at], 0)

    own_region(compute)
    for (_, turn), copy in copies.items():
        if turn not in early:
            copy.wait()


def other_side_kernel(slab, far, early, late, *refs):
    w_refs, (w_early, gram_early, blocks, begun) = refs[: len(late)], refs[len(late) :][:4]
    *out_refs, w_split, gram_ref = refs[len(late) + 4 :]
    rank = w_refs[0].shape[0]
    for turn in early:
        w_split[turn] = w_early[turn]
    gram = gram_early[...]
    for turn, ref in zip(late, w_refs):
        gram = gram + split_basis(ref, w_split, turn)
    slabs = [gram[GRAM_ROWS * i : GRAM_ROWS * (i + 1)] for i in range(rank // GRAM_ROWS)]
    packed = jnp.concatenate(slabs, axis=1)
    gram_ref[...] = packed
    for index, out_ref in enumerate(out_refs):
        for at in range(far):
            block = index * far + at
            store(
                product(w_split, blocks, block, late), out_ref.at[pl.ds(slab * at, slab)], 0,
                begun.at[block],
            )
        out_ref[slab * far :] = packed


def own_side_kernel(near, width, n_col, owns, w_split, data_ref, out_ref, blocks, sems):
    order = [(at, turn) for at in enumerate(owns) for turn in range(n_col)]
    copies = block_copies(near, width, n_col, order, data_ref, blocks, sems)
    waiting = list(copies.values())
    ahead = n_col + n_col // 2

    def multiply(at):
        store(product(w_split, blocks, at, range(n_col)), out_ref.at[at], 0)

    for copy in waiting[:ahead]:
        copy.start()
    for index, copy in enumerate(waiting):
        copy.wait()
        if index + ahead < len(waiting):
            waiting[index + ahead].start()
        if (index + 1) % n_col == 0:
            own_region(functools.partial(multiply, index // n_col))


def side_sum_kernel(slab, own_ref, gram_ref, *refs):
    far = own_ref.shape[0]
    got_refs, out_refs = refs[:-far], refs[-far:]
    gram = gram_ref[...]
    for got in got_refs:
        gram = gram + got[slab * far :]
    for at, out_ref in enumerate(out_refs):
        total = own_ref[at]
        for got in got_refs:
            total = total + got[slab * at : slab * (at + 1)]
        out_ref[:slab] = total
        out_ref[slab:] = gram


def sweep_kernel(width, *refs):
    parts, h_ref, out_ref = refs[:-2], refs[-2], refs[-1]
    rank = h_ref.shape[0]
    row_at = lax.axis_index("prow")
    total = parts[0][...]
    for part in parts[1:]:
        total = total + part[...]
    pieces = width // LANES
    cross = jnp.concatenate([total[rank * i : rank * (i + 1)] for i in range(pieces)], axis=1)
    packed = total[rank * pieces :]
    gram = jnp.concatenate(
        [packed[:, rank * i : rank * (i + 1)] for i in range(rank // GRAM_ROWS)], axis=0
    )
    h = h_ref[:, pl.ds(pl.multiple_of(row_at * width, width), width)]
    rest = cross - exact_dot(gram, h, ((1,), (0,)))
    rows = []
    for k in range(rank):
        inverse = 1.0 / gram[k : k + 1, k : k + 1]
        old = h[k : k + 1]
        fresh = jnp.maximum(old + rest[k : k + 1] * inverse, 0.0)
        rows.append(fresh)
        rest = rest - gram[:, k : k + 1] * (fresh - old)
    done = jnp.concatenate(rows, axis=0)
    for peer in range(out_ref.shape[0]):
        out_ref[peer] = done


def assemble_kernel(width, pieces, out_ref):
    for peer in range(pieces.shape[0]):
        out_ref[:, width * peer : width * (peer + 1)] = pieces[peer]


def shards(n_row, n_col, data, w_trans, h_prior):
    rank, depth = w_trans.shape
    rows, cols = data.shape
    width = cols // n_row
    near = max(1, n_row // 4)
    far = n_row // near
    slab = rank * (width // LANES)
    turns = list(range(far - 1, -1, -1))
    sides = range(1, near)

    def permute(value, axis, turn):
        size = n_row if axis == "prow" else n_col
        return lax.ppermute(value, axis, [(i, i ^ turn) for i in range(size)])

    w_parts = [w_trans] + [permute(w_trans, "pcol", t) for t in range(1, n_col)]
    early = list(range(1, min(2, n_col)))
    late = [turn for turn in range(n_col) if turn not in early]
    others = [(side, turn) for side in sides for turn in turns]
    owns = [(0, turn) for turn in turns]
    split_parts = jax.ShapeDtypeStruct((n_col, 2 * rank, depth), jnp.bfloat16)
    blocks, begun, w_early, gram_early = call(
        functools.partial(load_kernel, near, width, n_col, early, late, others),
        [
            floats(len(others), rows, width),
            floats(len(others), slab, LANES),
            split_parts,
            floats(rank, rank),
        ],
        [*(w_parts[t] for t in early), data], "load_other_side", 40,
        [VMEM] * len(early) + [HBM], [pltpu.SemaphoreType.DMA((len(others), n_col))],
        pl.CostEstimate(
            flops=0, bytes_accessed=8 * rows * width * len(others), transcendentals=0
        ),
    )
    *sent, w_split, gram = call(
        functools.partial(other_side_kernel, slab, far, early, late),
        [floats(far * slab + GRAM_ROWS, LANES)] * len(sides)
        + [split_parts, floats(GRAM_ROWS, LANES)],
        [*(w_parts[t] for t in late), w_early, gram_early, blocks, begun], "other_side", 8,
    )
    got = [permute(sent[side - 1], "prow", side) for side in sides]
    own = call(
        functools.partial(own_side_kernel, near, width, n_col, owns),
        floats(far, slab, LANES), [w_split, data], "own_side", 40, [VMEM, HBM],
        [
            pltpu.VMEM((far, rows, width), jnp.float32),
            pltpu.SemaphoreType.DMA((far, n_col)),
        ],
    )
    sums = call(
        functools.partial(side_sum_kernel, slab),
        [floats(slab + GRAM_ROWS, LANES)] * far, [own, gram, *got], "side_sum",
    )
    parts = [
        permute(value, "prow", turn * near) if turn else value
        for turn, value in zip(turns, sums)
    ]
    fresh = call(
        functools.partial(sweep_kernel, width), floats(n_row, rank, width),
        [*parts, h_prior], "row_sweep",
    )
    pieces = lax.all_to_all(fresh, "prow", 0, 0)
    return call(
        functools.partial(assemble_kernel, width), floats(rank, cols), [pieces], "assemble"
    )


def solution(mesh):
    n_row, n_col = mesh.shape["prow"], mesh.shape["pcol"]
    placed = (P("prow", "pcol"), P(None, ("prow", "pcol")), P(None, "pcol"))
    return jax.shard_map(
        functools.partial(shards, n_row, n_col),
        mesh=mesh, in_specs=placed, out_specs=P(None, "pcol"), check_vma=False,
    )
```

```python
import functools

import jax
import jax.numpy as jnp
from jax import lax
from jax.experimental import pallas as pl
from jax.experimental.pallas import tpu as pltpu
from jax.sharding import PartitionSpec as P

LANES = 128
GRAM_ROWS = 8
VMEM = pl.BlockSpec(memory_space=pltpu.VMEM)
HBM = pl.BlockSpec(memory_space=pltpu.HBM)


def call(kernel, out_shape, operands, name, mebibytes=4, in_specs=None, scratch=(), cost=None):
    many = isinstance(out_shape, list)
    return pl.pallas_call(
        kernel,
        out_shape=out_shape,
        in_specs=in_specs or [VMEM] * len(operands),
        out_specs=[VMEM] * len(out_shape) if many else VMEM,
        compiler_params=pltpu.CompilerParams(vmem_limit_bytes=mebibytes * 1024 * 1024),
        scratch_shapes=list(scratch),
        cost_estimate=cost,
        name=name,
    )(*operands)


def floats(*shape):
    return jax.ShapeDtypeStruct(shape, jnp.float32)


def split(value):
    high = value.astype(jnp.bfloat16)
    low = (value - high.astype(jnp.float32)).astype(jnp.bfloat16)
    return high, low


def exact_dot(left, right, dims):
    return lax.dot_general(
        left, right, (dims, ((), ())),
        precision=lax.Precision.HIGHEST, preferred_element_type=jnp.float32,
    )


def block_start(near, width, side_turn, level_turn):
    row_at = lax.axis_index("prow")
    side, level = lax.rem(row_at, near), lax.div(row_at, near)
    peer = (level ^ level_turn) * near + (side ^ side_turn)
    return pl.multiple_of(peer * width, width)


def row_part(depth, turn):
    return pl.ds(pl.multiple_of((lax.axis_index("pcol") ^ turn) * depth, depth), depth)


def block_copies(near, width, n_col, order, data_ref, out_ref, sems):
    depth = data_ref.shape[0] // n_col
    copies = {}
    for (at, turns), turn in order:
        columns = pl.ds(block_start(near, width, *turns), width)
        rows = row_part(depth, turn)
        copies[at, turn] = pltpu.make_async_copy(
            data_ref.at[rows, columns], out_ref.at[at, rows], sems.at[at, turn]
        )
    return copies


def split_basis(part_refs, out_ref):
    gram = None
    for at, part_ref in enumerate(part_refs):
        rank = part_ref.shape[0]
        part = part_ref[...]
        high, low = split(part)
        out_ref[at, :rank] = high
        out_ref[at, rank:] = low
        own = exact_dot(part, part, ((1,), (1,)))
        gram = own if gram is None else gram + own
    return gram


def product(basis, blocks, at):
    total = None
    for turn, part_ref, index in basis:
        rank, depth = part_ref.shape[1] // 2, part_ref.shape[2]
        high, low = split(blocks[at, row_part(depth, turn)])
        upper = jnp.dot(part_ref[index], high, preferred_element_type=jnp.float32)
        term = (
            upper[:rank]
            + upper[rank:]
            + jnp.dot(part_ref[index, :rank], low, preferred_element_type=jnp.float32)
        )
        total = term if total is None else total + term
    return total


def parts_of(turns, part_ref):
    return [(turn, part_ref, index) for index, turn in enumerate(turns)]


def store(cross, out_ref, row, before=None):
    rank = cross.shape[0]
    for i in range(cross.shape[1] // LANES):
        rows = slice(row + rank * i, row + rank * (i + 1))
        piece = cross[:, LANES * i : LANES * (i + 1)]
        out_ref[rows] = piece if before is None else piece + before[rows]


def own_region(compute):
    pl.when(lax.axis_index("prow") >= 0)(compute)


def add_to(cross, out_ref, row, before):
    store(cross, out_ref.at[pl.ds(row, before.shape[0])], 0, before)


def load_kernel(near, width, n_col, stages, others, *refs):
    first = stages[0]
    w_refs, data_ref = refs[: len(first)], refs[len(first)]
    blocks, begun, w_split, gram_ref, sems = refs[len(first) + 1 :]
    order = [(at, turn) for stage in stages for turn in stage for at in enumerate(others)]
    copies = block_copies(near, width, n_col, order, data_ref, blocks, sems)
    for copy in copies.values():
        copy.start()

    def compute():
        gram_ref[...] = split_basis(w_refs, w_split)
        for at in range(len(others)):
            for turn in first:
                copies[at, turn].wait()
            store(product(parts_of(first, w_split), blocks, at), begun.at[at], 0)

    own_region(compute)
    for (_, turn), copy in copies.items():
        if turn not in first:
            copy.wait()


def relay_kernel(*refs):
    count = len(refs) // 2
    for ref, out_ref in zip(refs[:count], refs[count + 1 :]):
        out_ref[...] = ref[...]


def middle_kernel(near, width, n_col, turns, own, *refs):
    w_refs, (gram_before, blocks, begun, data_ref) = refs[: len(turns)], refs[len(turns) :][:4]
    further, w_split, gram_ref, own_block, sems = refs[len(turns) + 4 :]
    order = [((0, own), turn) for turn in range(n_col)]
    copies = block_copies(near, width, n_col, order, data_ref, own_block, sems)
    for copy in copies.values():
        copy.start()

    def compute():
        gram_ref[...] = gram_before[...] + split_basis(w_refs, w_split)
        for at in range(blocks.shape[0]):
            add_to(
                product(parts_of(turns, w_split), blocks, at), further.at[at], 0, begun.at[at]
            )

    own_region(compute)
    for copy in copies.values():
        copy.wait()


def first_group_kernel(slab, count, turns, *refs):
    w_refs, (gram_before, blocks, further) = refs[: len(turns)], refs[len(turns) :][:3]
    *out_refs, w_split, gram_ref = refs[len(turns) + 3 :]
    gram = gram_before[...] + split_basis(w_refs, w_split)
    slabs = [gram[GRAM_ROWS * i : GRAM_ROWS * (i + 1)] for i in range(gram.shape[0] // GRAM_ROWS)]
    packed = jnp.concatenate(slabs, axis=1)
    gram_ref[...] = packed
    for index, out_ref in enumerate(out_refs):
        for at in range(count):
            block = index * count + at
            add_to(
                product(parts_of(turns, w_split), blocks, block), out_ref, slab * at,
                further.at[block],
            )
        out_ref[slab * count :] = packed


def second_group_kernel(near, width, n_col, slab, count, n_sides, stages, owns, *refs):
    w_refs, (blocks, further, own_block, data_ref) = refs[:3], refs[3:7]
    out_refs, (own_ref, rest, sems) = refs[7 : 7 + n_sides], refs[7 + n_sides :]
    basis = [part for turns, ref in zip(stages, w_refs) for part in parts_of(turns, ref)]
    order = [(at, turn) for at in enumerate(owns[1:]) for turn in range(n_col)]
    copies = block_copies(near, width, n_col, order, data_ref, rest, sems)
    for copy in copies.values():
        copy.start()

    def compute():
        for index, out_ref in enumerate(out_refs):
            for at in range(count):
                block = (n_sides + index) * count + at
                add_to(
                    product(parts_of(stages[2], w_refs[2]), blocks, block), out_ref, slab * at,
                    further.at[block],
                )
        store(product(basis, own_block, 0), own_ref.at[0], 0)

    def multiply(at):
        for turn in range(n_col):
            copies[at, turn].wait()
        store(product(basis, rest, at), own_ref.at[at + 1], 0)

    own_region(compute)
    for at in range(len(owns) - 2):
        own_region(functools.partial(multiply, at))
    for turn in range(n_col):
        copies[len(owns) - 2, turn].wait()


def last_block_kernel(stages, *refs):
    w_refs, rest, out_ref = refs[:3], refs[3], refs[4]
    basis = [part for turns, ref in zip(stages, w_refs) for part in parts_of(turns, ref)]
    store(product(basis, rest, rest.shape[0] - 1), out_ref, 0)


def side_sum_kernel(slab, levels, gram_sent, n_got, *refs):
    count = len(levels)
    own_refs, gram_ref, got_refs = refs[:count], refs[count], refs[count + 1 : count + 1 + n_got]
    out_refs = refs[count + 1 + n_got :]
    gram = gram_ref[...]
    if gram_sent:
        for got in got_refs:
            gram = gram + got[slab * count :]
        out_refs[count][...] = gram
    for at, level in enumerate(levels):
        total = own_refs[at][...] if level is None else own_refs[at][level]
        for got in got_refs:
            total = total + got[slab * at : slab * (at + 1)]
        out_refs[at][:slab] = total
        out_refs[at][slab:] = gram


def sweep_kernel(width, *refs):
    parts, h_ref, out_ref = refs[:-2], refs[-2], refs[-1]
    rank = h_ref.shape[0]
    row_at = lax.axis_index("prow")
    total = parts[0][...]
    for part in parts[1:]:
        total = total + part[...]
    pieces = width // LANES
    cross = jnp.concatenate([total[rank * i : rank * (i + 1)] for i in range(pieces)], axis=1)
    packed = total[rank * pieces :]
    gram = jnp.concatenate(
        [packed[:, rank * i : rank * (i + 1)] for i in range(rank // GRAM_ROWS)], axis=0
    )
    h = h_ref[:, pl.ds(pl.multiple_of(row_at * width, width), width)]
    rest = cross - exact_dot(gram, h, ((1,), (0,)))
    rows = []
    for k in range(rank):
        inverse = 1.0 / gram[k : k + 1, k : k + 1]
        old = h[k : k + 1]
        fresh = jnp.maximum(old + rest[k : k + 1] * inverse, 0.0)
        rows.append(fresh)
        rest = rest - gram[:, k : k + 1] * (fresh - old)
    done = jnp.concatenate(rows, axis=0)
    for peer in range(out_ref.shape[0]):
        out_ref[peer] = done


def assemble_kernel(width, pieces, out_ref):
    for peer in range(pieces.shape[0]):
        out_ref[:, width * peer : width * (peer + 1)] = pieces[peer]


def shards(n_row, n_col, data, w_trans, h_prior):
    rank, depth = w_trans.shape
    rows, cols = data.shape
    width = cols // n_row
    near = max(1, n_row // 4)
    far = n_row // near
    slab = rank * (width // LANES)
    count = far // 2
    groups = [list(range(far - 1, count - 1, -1)), list(range(count - 1, -1, -1))]
    sides = range(1, near)

    def permute(value, axis, turn):
        size = n_row if axis == "prow" else n_col
        return lax.ppermute(value, axis, [(i, i ^ turn) for i in range(size)])

    stages = [[1], list(range(0, n_col, 2)), list(range(3, n_col, 2))]
    w_parts = {1: permute(w_trans, "pcol", 1), 0: w_trans}
    for turn in stages[1][1:]:
        w_parts[turn] = permute(w_trans, "pcol", turn)
    others = [(side, turn) for group in groups for side in sides for turn in group]
    owns = [(0, turn) for group in groups for turn in group]

    def split_parts(stage):
        return jax.ShapeDtypeStruct((len(stage), 2 * rank, depth), jnp.bfloat16)

    def semaphores(count):
        return pltpu.SemaphoreType.DMA((count, n_col))

    products = floats(len(others), slab, LANES)
    blocks, begun, w_first, gram = call(
        functools.partial(load_kernel, near, width, n_col, stages, others),
        [floats(len(others), rows, width), products, split_parts(stages[0]), floats(rank, rank)],
        [*(w_parts[t] for t in stages[0]), data], "load_other_side", 40,
        [VMEM] * len(stages[0]) + [HBM], [semaphores(len(others))],
        pl.CostEstimate(
            flops=0, bytes_accessed=8 * rows * width * len(others), transcendentals=0
        ),
    )
    arrived = call(
        relay_kernel, [floats(rank, depth)] * (len(stages[1]) - 1),
        [*(w_parts[t] for t in stages[1][1:]), gram], "relay",
    )
    for turn, value in zip(stages[1][1:], arrived):
        w_parts[turn] = value
        w_parts[turn + 1] = permute(value, "pcol", 1)
    further, w_second, gram, own_block = call(
        functools.partial(middle_kernel, near, width, n_col, stages[1], owns[0]),
        [products, split_parts(stages[1]), floats(rank, rank), floats(1, rows, width)],
        [*(w_parts[t] for t in stages[1]), gram, blocks, begun, data], "middle", 37,
        [VMEM] * (len(stages[1]) + 3) + [HBM], [semaphores(1)],
    )
    *sent_first, w_third, gram = call(
        functools.partial(first_group_kernel, slab, count, stages[2]),
        [floats(count * slab + GRAM_ROWS, LANES)] * len(sides)
        + [split_parts(stages[2]), floats(GRAM_ROWS, LANES)],
        [*(w_parts[t] for t in stages[2]), gram, blocks, further], "first_group", 8,
    )
    w_split = [w_first, w_second, w_third]
    got = [[permute(sent_first[side - 1], "prow", side) for side in sides]]
    *sent_second, own, rest = call(
        functools.partial(
            second_group_kernel, near, width, n_col, slab, count, len(sides), stages, owns
        ),
        [floats(count * slab, LANES)] * len(sides)
        + [floats(far - 1, slab, LANES), floats(far - 1, rows, width)],
        [*w_split, blocks, further, own_block, data], "second_group_and_own_side", 36,
        [VMEM] * 6 + [HBM], [semaphores(far - 1)],
    )
    got.append([permute(sent_second[side - 1], "prow", side) for side in sides])
    last = call(
        functools.partial(last_block_kernel, stages), floats(slab, LANES), [*w_split, rest],
        "last_block", 8,
    )
    parts = []
    for index, group in enumerate(groups):
        gram_sent = index == 0
        levels = [index * count + at for at in range(count)]
        levels = [level if level < far - 1 else None for level in levels]
        sums = call(
            functools.partial(side_sum_kernel, slab, levels, gram_sent, len(sides)),
            [floats(slab + GRAM_ROWS, LANES)] * count + [floats(GRAM_ROWS, LANES)] * gram_sent,
            [*(last if level is None else own for level in levels), gram, *got[index]],
            "side_sum",
        )
        if gram_sent:
            *sums, gram = sums
        for turn, value in zip(group, sums):
            parts.append(permute(value, "prow", turn * near) if turn else value)
    fresh = call(
        functools.partial(sweep_kernel, width), floats(n_row, rank, width),
        [*parts, h_prior], "row_sweep",
    )
    pieces = lax.all_to_all(fresh, "prow", 0, 0)
    return call(
        functools.partial(assemble_kernel, width), floats(rank, cols), [pieces], "assemble"
    )


def solution(mesh):
    n_row, n_col = mesh.shape["prow"], mesh.shape["pcol"]
    placed = (P("prow", "pcol"), P(None, ("prow", "pcol")), P(None, "pcol"))
    return jax.shard_map(
        functools.partial(shards, n_row, n_col),
        mesh=mesh, in_specs=placed, out_specs=P(None, "pcol"), check_vma=False,
    )
```

```python
import functools

import jax
import jax.numpy as jnp
from jax import lax
from jax.experimental import pallas as pl
from jax.experimental.pallas import tpu as pltpu
from jax.sharding import PartitionSpec as P

LANES = 128
GRAM_ROWS = 8
VMEM = pl.BlockSpec(memory_space=pltpu.VMEM)
HBM = pl.BlockSpec(memory_space=pltpu.HBM)


def call(kernel, out_shape, operands, name, mebibytes=4, in_specs=None, scratch=(), cost=None):
    many = isinstance(out_shape, list)
    return pl.pallas_call(
        kernel,
        out_shape=out_shape,
        in_specs=in_specs or [VMEM] * len(operands),
        out_specs=[VMEM] * len(out_shape) if many else VMEM,
        compiler_params=pltpu.CompilerParams(vmem_limit_bytes=mebibytes * 1024 * 1024),
        scratch_shapes=list(scratch),
        cost_estimate=cost,
        name=name,
    )(*operands)


def floats(*shape):
    return jax.ShapeDtypeStruct(shape, jnp.float32)


def split(value):
    high = value.astype(jnp.bfloat16)
    low = (value - high.astype(jnp.float32)).astype(jnp.bfloat16)
    return high, low


def exact_dot(left, right, dims):
    return lax.dot_general(
        left, right, (dims, ((), ())),
        precision=lax.Precision.HIGHEST, preferred_element_type=jnp.float32,
    )


def block_start(near, width, side_turn, level_turn):
    row_at = lax.axis_index("prow")
    side, level = lax.rem(row_at, near), lax.div(row_at, near)
    peer = (level ^ level_turn) * near + (side ^ side_turn)
    return pl.multiple_of(peer * width, width)


def row_part(depth, turn):
    return pl.ds(pl.multiple_of((lax.axis_index("pcol") ^ turn) * depth, depth), depth)


def block_copies(near, width, n_col, order, data_ref, out_ref, sems):
    depth = data_ref.shape[0] // n_col
    copies = {}
    for (at, turns), turn in order:
        columns = pl.ds(block_start(near, width, *turns), width)
        rows = row_part(depth, turn)
        copies[at, turn] = pltpu.make_async_copy(
            data_ref.at[rows, columns], out_ref.at[at, rows], sems.at[at, turn]
        )
    return copies


def split_basis(part_refs, out_ref):
    gram = None
    for at, part_ref in enumerate(part_refs):
        rank = part_ref.shape[0]
        part = part_ref[...]
        high, low = split(part)
        out_ref[at, :rank] = high
        out_ref[at, rank:] = low
        own = exact_dot(part, part, ((1,), (1,)))
        gram = own if gram is None else gram + own
    return gram


def product(basis, blocks, at):
    total = None
    for turn, part_ref, index in basis:
        rank, depth = part_ref.shape[1] // 2, part_ref.shape[2]
        high, low = split(blocks[at, row_part(depth, turn)])
        upper = jnp.dot(part_ref[index], high, preferred_element_type=jnp.float32)
        term = (
            upper[:rank]
            + upper[rank:]
            + jnp.dot(part_ref[index, :rank], low, preferred_element_type=jnp.float32)
        )
        total = term if total is None else total + term
    return total


def parts_of(turns, part_ref):
    return [(turn, part_ref, index) for index, turn in enumerate(turns)]


def store(cross, out_ref, row, before=None):
    rank = cross.shape[0]
    for i in range(cross.shape[1] // LANES):
        rows = slice(row + rank * i, row + rank * (i + 1))
        piece = cross[:, LANES * i : LANES * (i + 1)]
        out_ref[rows] = piece if before is None else piece + before[rows]


def own_region(compute):
    pl.when(lax.axis_index("prow") >= 0)(compute)


def load_kernel(near, width, n_col, others, data_ref, blocks, sems):
    order = [(at, turn) for at in enumerate(others) for turn in range(n_col)]
    copies = block_copies(near, width, n_col, order, data_ref, blocks, sems)
    for copy in copies.values():
        copy.start()
    for copy in copies.values():
        copy.wait()


def relay_kernel(*refs):
    count = len(refs) // 2
    for ref, out_ref in zip(refs[:count], refs[count + 1 :]):
        out_ref[...] = ref[...]


def middle_kernel(near, width, n_col, turns, own, *refs):
    w_refs, (blocks, data_ref) = refs[: len(turns)], refs[len(turns) :][:2]
    begun, w_split, gram_ref, own_block, sems = refs[len(turns) + 2 :]
    order = [((0, own), turn) for turn in range(n_col)]
    copies = block_copies(near, width, n_col, order, data_ref, own_block, sems)
    for copy in copies.values():
        copy.start()

    def compute():
        gram_ref[...] = split_basis(w_refs, w_split)
        for at in range(blocks.shape[0]):
            store(product(parts_of(turns, w_split), blocks, at), begun.at[at], 0)

    own_region(compute)
    for copy in copies.values():
        copy.wait()


def other_side_kernel(slab, far, turns, *refs):
    w_refs, (gram_before, blocks, begun) = refs[: len(turns)], refs[len(turns) :][:3]
    *out_refs, w_split, gram_ref = refs[len(turns) + 3 :]
    gram = gram_before[...] + split_basis(w_refs, w_split)
    slabs = [gram[GRAM_ROWS * i : GRAM_ROWS * (i + 1)] for i in range(gram.shape[0] // GRAM_ROWS)]
    packed = jnp.concatenate(slabs, axis=1)
    gram_ref[...] = packed
    for index, out_ref in enumerate(out_refs):
        for at in range(far):
            block = index * far + at
            cross = product(parts_of(turns, w_split), blocks, block)
            store(cross, out_ref.at[pl.ds(slab * at, slab)], 0, begun.at[block])
        out_ref[slab * far :] = packed


def own_side_kernel(near, width, n_col, stages, owns, *refs):
    w_refs, (own_block, data_ref, out_ref, rest, sems) = refs[:2], refs[2:]
    basis = [part for turns, ref in zip(stages, w_refs) for part in parts_of(turns, ref)]
    order = [(at, turn) for at in enumerate(owns[1:]) for turn in range(n_col)]
    copies = block_copies(near, width, n_col, order, data_ref, rest, sems)
    for copy in copies.values():
        copy.start()

    def multiply(at):
        for turn in range(n_col):
            copies[at, turn].wait()
        store(product(basis, rest, at), out_ref.at[at + 1], 0)

    own_region(lambda: store(product(basis, own_block, 0), out_ref.at[0], 0))
    for at in range(len(owns) - 1):
        own_region(functools.partial(multiply, at))


def side_sum_kernel(slab, own_ref, gram_ref, *refs):
    far = own_ref.shape[0]
    got_refs, out_refs = refs[:-far], refs[-far:]
    gram = gram_ref[...]
    for got in got_refs:
        gram = gram + got[slab * far :]
    for at, out_ref in enumerate(out_refs):
        total = own_ref[at]
        for got in got_refs:
            total = total + got[slab * at : slab * (at + 1)]
        out_ref[:slab] = total
        out_ref[slab:] = gram


def sweep_kernel(width, *refs):
    parts, h_ref, out_ref = refs[:-2], refs[-2], refs[-1]
    rank = h_ref.shape[0]
    row_at = lax.axis_index("prow")
    total = parts[0][...]
    for part in parts[1:]:
        total = total + part[...]
    pieces = width // LANES
    cross = jnp.concatenate([total[rank * i : rank * (i + 1)] for i in range(pieces)], axis=1)
    packed = total[rank * pieces :]
    gram = jnp.concatenate(
        [packed[:, rank * i : rank * (i + 1)] for i in range(rank // GRAM_ROWS)], axis=0
    )
    h = h_ref[:, pl.ds(pl.multiple_of(row_at * width, width), width)]
    rest = cross - exact_dot(gram, h, ((1,), (0,)))
    rows = []
    for k in range(rank):
        inverse = 1.0 / gram[k : k + 1, k : k + 1]
        old = h[k : k + 1]
        fresh = jnp.maximum(old + rest[k : k + 1] * inverse, 0.0)
        rows.append(fresh)
        rest = rest - gram[:, k : k + 1] * (fresh - old)
    done = jnp.concatenate(rows, axis=0)
    for peer in range(out_ref.shape[0]):
        out_ref[peer] = done


def assemble_kernel(width, pieces, out_ref):
    for peer in range(pieces.shape[0]):
        out_ref[:, width * peer : width * (peer + 1)] = pieces[peer]


def shards(n_row, n_col, data, w_trans, h_prior):
    rank, depth = w_trans.shape
    rows, cols = data.shape
    width = cols // n_row
    near = max(1, n_row // 4)
    far = n_row // near
    slab = rank * (width // LANES)
    levels = list(range(far - 1, -1, -1))
    sides = range(1, near)

    def permute(value, axis, turn):
        size = n_row if axis == "prow" else n_col
        return lax.ppermute(value, axis, [(i, i ^ turn) for i in range(size)])

    stages = [[1, *range(0, n_col, 2)], list(range(3, n_col, 2))]
    w_parts = {1: permute(w_trans, "pcol", 1), 0: w_trans}
    far_turns = range(2, n_col, 2)
    for turn in far_turns:
        w_parts[turn] = permute(w_trans, "pcol", turn)
    others = [(side, level) for side in sides for level in levels]
    owns = [(0, level) for level in levels]

    def split_parts(stage):
        return jax.ShapeDtypeStruct((len(stage), 2 * rank, depth), jnp.bfloat16)

    def semaphores(count):
        return pltpu.SemaphoreType.DMA((count, n_col))

    blocks = call(
        functools.partial(load_kernel, near, width, n_col, others),
        floats(len(others), rows, width), [data], "load_other_side", 40, [HBM],
        [semaphores(len(others))],
        pl.CostEstimate(
            flops=0, bytes_accessed=8 * rows * width * len(others), transcendentals=0
        ),
    )
    arrived = call(
        relay_kernel, [floats(rank, depth)] * len(far_turns),
        [*(w_parts[t] for t in far_turns), blocks], "relay",
        in_specs=[VMEM] * (len(far_turns) + 1),
    )
    for turn, value in zip(far_turns, arrived):
        w_parts[turn] = value
        w_parts[turn + 1] = permute(value, "pcol", 1)
    begun, w_first, gram, own_block = call(
        functools.partial(middle_kernel, near, width, n_col, stages[0], owns[0]),
        [
            floats(len(others), slab, LANES),
            split_parts(stages[0]),
            floats(rank, rank),
            floats(1, rows, width),
        ],
        [*(w_parts[t] for t in stages[0]), blocks, data], "middle", 37,
        [VMEM] * (len(stages[0]) + 1) + [HBM], [semaphores(1)],
    )
    *sent, w_last, gram = call(
        functools.partial(other_side_kernel, slab, far, stages[1]),
        [floats(far * slab + GRAM_ROWS, LANES)] * len(sides)
        + [split_parts(stages[1]), floats(GRAM_ROWS, LANES)],
        [*(w_parts[t] for t in stages[1]), gram, blocks, begun], "other_side", 8,
    )
    got = [permute(sent[side - 1], "prow", side) for side in sides]
    own = call(
        functools.partial(own_side_kernel, near, width, n_col, stages, owns),
        floats(far, slab, LANES), [w_first, w_last, own_block, data], "own_side", 40,
        [VMEM] * 3 + [HBM],
        [pltpu.VMEM((far - 1, rows, width), jnp.float32), semaphores(far - 1)],
    )
    sums = call(
        functools.partial(side_sum_kernel, slab),
        [floats(slab + GRAM_ROWS, LANES)] * far, [own, gram, *got], "side_sum",
    )
    parts = [
        permute(value, "prow", level * near) if level else value
        for level, value in zip(levels, sums)
    ]
    fresh = call(
        functools.partial(sweep_kernel, width), floats(n_row, rank, width),
        [*parts, h_prior], "row_sweep",
    )
    pieces = lax.all_to_all(fresh, "prow", 0, 0)
    return call(
        functools.partial(assemble_kernel, width), floats(rank, cols), [pieces], "assemble"
    )


def solution(mesh):
    n_row, n_col = mesh.shape["prow"], mesh.shape["pcol"]
    placed = (P("prow", "pcol"), P(None, ("prow", "pcol")), P(None, "pcol"))
    return jax.shard_map(
        functools.partial(shards, n_row, n_col),
        mesh=mesh, in_specs=placed, out_specs=P(None, "pcol"), check_vma=False,
    )
```

```python
import functools

import jax
import jax.numpy as jnp
from jax import lax
from jax.experimental import pallas as pl
from jax.experimental.pallas import tpu as pltpu
from jax.sharding import PartitionSpec as P

LANES = 128
GRAM_ROWS = 8
VMEM = pl.BlockSpec(memory_space=pltpu.VMEM)
HBM = pl.BlockSpec(memory_space=pltpu.HBM)


def call(kernel, out_shape, operands, name, mebibytes=4, in_specs=None, scratch=(), cost=None):
    many = isinstance(out_shape, list)
    return pl.pallas_call(
        kernel,
        out_shape=out_shape,
        in_specs=in_specs or [VMEM] * len(operands),
        out_specs=[VMEM] * len(out_shape) if many else VMEM,
        compiler_params=pltpu.CompilerParams(vmem_limit_bytes=mebibytes * 1024 * 1024),
        scratch_shapes=list(scratch),
        cost_estimate=cost,
        name=name,
    )(*operands)


def floats(*shape):
    return jax.ShapeDtypeStruct(shape, jnp.float32)


def split(value):
    high = value.astype(jnp.bfloat16)
    low = (value - high.astype(jnp.float32)).astype(jnp.bfloat16)
    return high, low


def exact_dot(left, right, dims):
    return lax.dot_general(
        left, right, (dims, ((), ())),
        precision=lax.Precision.HIGHEST, preferred_element_type=jnp.float32,
    )


def block_start(near, width, side_turn, level_turn):
    row_at = lax.axis_index("prow")
    side, level = lax.rem(row_at, near), lax.div(row_at, near)
    peer = (level ^ level_turn) * near + (side ^ side_turn)
    return pl.multiple_of(peer * width, width)


def row_part(depth, turn):
    return pl.ds(pl.multiple_of((lax.axis_index("pcol") ^ turn) * depth, depth), depth)


def block_copies(near, width, n_col, order, data_ref, out_ref, sems):
    depth = data_ref.shape[0] // n_col
    copies = {}
    for (at, turns), turn in order:
        columns = pl.ds(block_start(near, width, *turns), width)
        rows = row_part(depth, turn)
        copies[at, turn] = pltpu.make_async_copy(
            data_ref.at[rows, columns], out_ref.at[at, rows], sems.at[at, turn]
        )
    return copies


def split_basis(part_refs, out_ref):
    gram = None
    for at, part_ref in enumerate(part_refs):
        rank = part_ref.shape[0]
        part = part_ref[...]
        high, low = split(part)
        out_ref[at, :rank] = high
        out_ref[at, rank:] = low
        own = exact_dot(part, part, ((1,), (1,)))
        gram = own if gram is None else gram + own
    return gram


def product(basis, blocks, at):
    total = None
    for turn, part_ref, index in basis:
        rank, depth = part_ref.shape[1] // 2, part_ref.shape[2]
        high, low = split(blocks[at, row_part(depth, turn)])
        upper = jnp.dot(part_ref[index], high, preferred_element_type=jnp.float32)
        term = (
            upper[:rank]
            + upper[rank:]
            + jnp.dot(part_ref[index, :rank], low, preferred_element_type=jnp.float32)
        )
        total = term if total is None else total + term
    return total


def parts_of(turns, part_ref):
    return [(turn, part_ref, index) for index, turn in enumerate(turns)]


def store(cross, out_ref, row, before=None):
    rank = cross.shape[0]
    for i in range(cross.shape[1] // LANES):
        rows = slice(row + rank * i, row + rank * (i + 1))
        piece = cross[:, LANES * i : LANES * (i + 1)]
        out_ref[rows] = piece if before is None else piece + before[rows]


def own_region(compute):
    pl.when(lax.axis_index("prow") >= 0)(compute)


def load_kernel(near, width, n_col, others, data_ref, blocks, sems):
    order = [(at, turn) for at in enumerate(others) for turn in range(n_col)]
    copies = block_copies(near, width, n_col, order, data_ref, blocks, sems)
    for copy in copies.values():
        copy.start()
    for copy in copies.values():
        copy.wait()


def relay_kernel(*refs):
    count = len(refs) // 2
    for ref, out_ref in zip(refs[:count], refs[count + 1 :]):
        out_ref[...] = ref[...]


def middle_kernel(near, width, n_col, turns, own, *refs):
    w_refs, (blocks, data_ref) = refs[: len(turns)], refs[len(turns) :][:2]
    begun, w_split, gram_ref, own_block, sems = refs[len(turns) + 2 :]
    order = [((0, own), turn) for turn in range(n_col)]
    copies = block_copies(near, width, n_col, order, data_ref, own_block, sems)
    for copy in copies.values():
        copy.start()

    def compute():
        gram_ref[...] = split_basis(w_refs, w_split)
        for at in range(blocks.shape[0]):
            store(product(parts_of(turns, w_split), blocks, at), begun.at[at], 0)

    own_region(compute)
    for copy in copies.values():
        copy.wait()


def other_side_kernel(slab, far, turns, *refs):
    w_refs, (gram_before, blocks, begun) = refs[: len(turns)], refs[len(turns) :][:3]
    *out_refs, w_split, gram_ref = refs[len(turns) + 3 :]
    gram = gram_before[...] + split_basis(w_refs, w_split)
    slabs = [gram[GRAM_ROWS * i : GRAM_ROWS * (i + 1)] for i in range(gram.shape[0] // GRAM_ROWS)]
    packed = jnp.concatenate(slabs, axis=1)
    gram_ref[...] = packed
    for index, out_ref in enumerate(out_refs):
        for at in range(far):
            block = index * far + at
            cross = product(parts_of(turns, w_split), blocks, block)
            store(cross, out_ref.at[pl.ds(slab * at, slab)], 0, begun.at[block])
        out_ref[slab * far :] = packed


def own_side_kernel(near, width, n_col, stages, owns, *refs):
    w_refs, (own_block, data_ref, out_ref, rest, sems) = refs[:2], refs[2:]
    basis = [part for turns, ref in zip(stages, w_refs) for part in parts_of(turns, ref)]
    order = [(at, turn) for at in enumerate(owns[1:]) for turn in range(n_col)]
    copies = block_copies(near, width, n_col, order, data_ref, rest, sems)
    for copy in copies.values():
        copy.start()

    def multiply(at):
        for turn in range(n_col):
            copies[at, turn].wait()
        store(product(basis, rest, at), out_ref.at[at + 1], 0)

    own_region(lambda: store(product(basis, own_block, 0), out_ref.at[0], 0))
    for at in range(len(owns) - 1):
        own_region(functools.partial(multiply, at))


def side_sum_kernel(slab, own_ref, gram_ref, *refs):
    far = own_ref.shape[0]
    count = far + far - 2
    got_refs, out_refs, up_refs = refs[:-count], refs[-count:][:far], refs[-count:][far:]
    gram = gram_ref[...]
    for got in got_refs:
        gram = gram + got[slab * far :]
    for at, out_ref in enumerate(out_refs):
        total = own_ref[at]
        for got in got_refs:
            total = total + got[slab * at : slab * (at + 1)]
        for ref in [out_ref, *up_refs[at : at + 1]]:
            ref[:slab] = total
            ref[slab:] = gram


def sweep_kernel(width, *refs):
    parts, h_ref, out_ref = refs[:-2], refs[-2], refs[-1]
    rank = h_ref.shape[0]
    row_at = lax.axis_index("prow")
    total = parts[0][...]
    for part in parts[1:]:
        total = total + part[...]
    pieces = width // LANES
    cross = jnp.concatenate([total[rank * i : rank * (i + 1)] for i in range(pieces)], axis=1)
    packed = total[rank * pieces :]
    gram = jnp.concatenate(
        [packed[:, rank * i : rank * (i + 1)] for i in range(rank // GRAM_ROWS)], axis=0
    )
    h = h_ref[:, pl.ds(pl.multiple_of(row_at * width, width), width)]
    rest = cross - exact_dot(gram, h, ((1,), (0,)))
    rows = []
    for k in range(rank):
        inverse = 1.0 / gram[k : k + 1, k : k + 1]
        old = h[k : k + 1]
        fresh = jnp.maximum(old + rest[k : k + 1] * inverse, 0.0)
        rows.append(fresh)
        rest = rest - gram[:, k : k + 1] * (fresh - old)
    out_ref[...] = jnp.concatenate(rows, axis=0)


def pack_kernel(place, *refs):
    out_ref = refs[-1]
    for index in range(out_ref.shape[0]):
        total = None
        for at, ref in zip(place, refs[:-1]):
            if at == index:
                total = ref[...] if total is None else total + ref[...]
        out_ref[index] = total


def assemble_kernel(near, width, level_groups, *refs):
    out_ref = refs[-1]
    row_at = lax.axis_index("prow")
    side, level = lax.rem(row_at, near), lax.div(row_at, near)
    for index, ref in enumerate(refs[:-1]):
        for at, level_turn in enumerate(level_groups[index // near]):
            peer = (level ^ level_turn) * near + (side ^ (index % near))
            columns = pl.ds(pl.multiple_of(peer * width, width), width)
            out_ref[:, columns] = ref[at]


def shards(n_row, n_col, data, w_trans, h_prior):
    rank, depth = w_trans.shape
    rows, cols = data.shape
    width = cols // n_row
    near = max(1, n_row // 4)
    far = n_row // near
    slab = rank * (width // LANES)
    levels = list(range(far - 1, -1, -1))
    sides = range(1, near)

    def permute(value, axis, turn):
        size = n_row if axis == "prow" else n_col
        return lax.ppermute(value, axis, [(i, i ^ turn) for i in range(size)])

    stages = [[1, *range(0, n_col, 2)], list(range(3, n_col, 2))]
    w_parts = {1: permute(w_trans, "pcol", 1), 0: w_trans}
    far_turns = range(2, n_col, 2)
    for turn in far_turns:
        w_parts[turn] = permute(w_trans, "pcol", turn)
    others = [(side, level) for side in sides for level in levels]
    owns = [(0, level) for level in levels]

    def split_parts(stage):
        return jax.ShapeDtypeStruct((len(stage), 2 * rank, depth), jnp.bfloat16)

    def semaphores(count):
        return pltpu.SemaphoreType.DMA((count, n_col))

    blocks = call(
        functools.partial(load_kernel, near, width, n_col, others),
        floats(len(others), rows, width), [data], "load_other_side", 40, [HBM],
        [semaphores(len(others))],
        pl.CostEstimate(
            flops=0, bytes_accessed=8 * rows * width * len(others), transcendentals=0
        ),
    )
    arrived = call(
        relay_kernel, [floats(rank, depth)] * len(far_turns),
        [*(w_parts[t] for t in far_turns), blocks], "relay",
        in_specs=[VMEM] * (len(far_turns) + 1),
    )
    for turn, value in zip(far_turns, arrived):
        w_parts[turn] = value
        w_parts[turn + 1] = permute(value, "pcol", 1)
    begun, w_first, gram, own_block = call(
        functools.partial(middle_kernel, near, width, n_col, stages[0], owns[0]),
        [
            floats(len(others), slab, LANES),
            split_parts(stages[0]),
            floats(rank, rank),
            floats(1, rows, width),
        ],
        [*(w_parts[t] for t in stages[0]), blocks, data], "middle", 37,
        [VMEM] * (len(stages[0]) + 1) + [HBM], [semaphores(1)],
    )
    *sent, w_last, gram = call(
        functools.partial(other_side_kernel, slab, far, stages[1]),
        [floats(far * slab + GRAM_ROWS, LANES)] * len(sides)
        + [split_parts(stages[1]), floats(GRAM_ROWS, LANES)],
        [*(w_parts[t] for t in stages[1]), gram, blocks, begun], "other_side", 8,
    )
    got = [permute(sent[side - 1], "prow", side) for side in sides]
    own = call(
        functools.partial(own_side_kernel, near, width, n_col, stages, owns),
        floats(far, slab, LANES), [w_first, w_last, own_block, data], "own_side", 40,
        [VMEM] * 3 + [HBM],
        [pltpu.VMEM((far - 1, rows, width), jnp.float32), semaphores(far - 1)],
    )
    sums = call(
        functools.partial(side_sum_kernel, slab),
        [floats(slab + GRAM_ROWS, LANES)] * (far + far - 2), [own, gram, *got], "side_sum",
    )
    def along_levels(values, up_values):
        got = {1: permute(values[1], "prow", near)}
        distant = [level for level in levels if level > 1]
        for downwards in (True, False):
            for level in distant:
                pairs = [(i, i ^ (level * near)) for i in range(n_row)]
                pairs = [(i, j) for i, j in pairs if (j < i) == downwards]
                value = values[level] if downwards else up_values[level]
                got[level, downwards] = lax.ppermute(value, "prow", pairs)
        return got

    order = [(level, down) for down in (False, True) for level in reversed(levels) if level > 1]
    arrived = along_levels(dict(zip(levels, sums)), dict(zip(levels, sums[far:])))
    keys = [key for key in reversed(order)]
    keys.insert(len(keys) // 2, 1)
    parts = [sums[levels.index(0)], *(arrived[key] for key in keys)]
    fresh = call(
        functools.partial(sweep_kernel, width), floats(rank, width), [*parts, h_prior], "row_sweep"
    )
    everywhere = {level: fresh for level in levels}
    arrived = along_levels(everywhere, everywhere)
    near_levels, far_levels = levels[far // 2 :], levels[: far // 2]
    pieces = []
    for group, place, values in (
        (near_levels, [0, 1], [arrived[1], fresh]),
        (far_levels, [far_levels.index(level) for level, _ in order], [arrived[k] for k in order]),
    ):
        packed = call(
            functools.partial(pack_kernel, place), floats(len(group), rank, width), values, "pack"
        )
        pieces.append(packed)
        pieces.extend(permute(packed, "prow", side) for side in sides)
    return call(
        functools.partial(assemble_kernel, near, width, [near_levels, far_levels]),
        floats(rank, cols), pieces, "assemble",
    )


def solution(mesh):
    n_row, n_col = mesh.shape["prow"], mesh.shape["pcol"]
    placed = (P("prow", "pcol"), P(None, ("prow", "pcol")), P(None, "pcol"))
    return jax.shard_map(
        functools.partial(shards, n_row, n_col),
        mesh=mesh, in_specs=placed, out_specs=P(None, "pcol"), check_vma=False,
    )
```

```python
import functools

import jax
import jax.numpy as jnp
from jax import lax
from jax.experimental import pallas as pl
from jax.experimental.pallas import tpu as pltpu
from jax.sharding import PartitionSpec as P

LANES = 128
GRAM_ROWS = 8
VMEM = pl.BlockSpec(memory_space=pltpu.VMEM)
HBM = pl.BlockSpec(memory_space=pltpu.HBM)


def call(kernel, out_shape, operands, name, mebibytes=4, in_specs=None, scratch=(), cost=None,
         out_specs=VMEM):
    many = isinstance(out_shape, list)
    return pl.pallas_call(
        kernel,
        out_shape=out_shape,
        in_specs=in_specs or [VMEM] * len(operands),
        out_specs=[out_specs] * len(out_shape) if many else out_specs,
        compiler_params=pltpu.CompilerParams(vmem_limit_bytes=mebibytes * 1024 * 1024),
        scratch_shapes=list(scratch),
        cost_estimate=cost,
        name=name,
    )(*operands)


def floats(*shape):
    return jax.ShapeDtypeStruct(shape, jnp.float32)


def split(value):
    high = value.astype(jnp.bfloat16)
    low = (value - high.astype(jnp.float32)).astype(jnp.bfloat16)
    return high, low


def exact_dot(left, right, dims):
    return lax.dot_general(
        left, right, (dims, ((), ())),
        precision=lax.Precision.HIGHEST, preferred_element_type=jnp.float32,
    )


def block_start(near, width, side_turn, level_turn):
    row_at = lax.axis_index("prow")
    side, level = lax.rem(row_at, near), lax.div(row_at, near)
    peer = (level ^ level_turn) * near + (side ^ side_turn)
    return pl.multiple_of(peer * width, width)


def row_part(depth, turn):
    return pl.ds(pl.multiple_of((lax.axis_index("pcol") ^ turn) * depth, depth), depth)


def block_copies(near, width, n_col, order, data_ref, out_ref, sems):
    depth = data_ref.shape[0] // n_col
    copies = {}
    for (at, turns), turn in order:
        columns = pl.ds(block_start(near, width, *turns), width)
        rows = row_part(depth, turn)
        copies[at, turn] = pltpu.make_async_copy(
            data_ref.at[rows, columns], out_ref.at[at, rows], sems.at[at, turn]
        )
    return copies


def split_basis(part_ref, out_ref, turn):
    rank = part_ref.shape[0]
    part = part_ref[...]
    high, low = split(part)
    out_ref[turn, :rank] = high
    out_ref[turn, rank:] = low
    return exact_dot(part, part, ((1,), (1,)))


def product(w_split, blocks, at, turns):
    rank, depth = w_split.shape[1] // 2, w_split.shape[2]
    total = None
    for turn in turns:
        high, low = split(blocks[at, row_part(depth, turn)])
        upper = jnp.dot(w_split[turn], high, preferred_element_type=jnp.float32)
        term = (
            upper[:rank]
            + upper[rank:]
            + jnp.dot(w_split[turn, :rank], low, preferred_element_type=jnp.float32)
        )
        total = term if total is None else total + term
    return total


def store(cross, out_ref, row, before=None):
    rank = cross.shape[0]
    for i in range(cross.shape[1] // LANES):
        rows = slice(row + rank * i, row + rank * (i + 1))
        piece = cross[:, LANES * i : LANES * (i + 1)]
        out_ref[rows] = piece if before is None else piece + before[rows]


def own_region(compute):
    pl.when(lax.axis_index("prow") >= 0)(compute)


def load_kernel(near, width, n_col, early, late, others, *refs):
    w_refs, data_ref = refs[: len(early)], refs[len(early)]
    blocks, begun, w_split, gram_ref, sems = refs[len(early) + 1 :]
    order = [(at, turn) for turn in early + late for at in enumerate(others)]
    copies = block_copies(near, width, n_col, order, data_ref, blocks, sems)
    for copy in copies.values():
        copy.start()

    def compute():
        gram = split_basis(w_refs[0], w_split, early[0])
        for turn, ref in list(zip(early, w_refs))[1:]:
            gram = gram + split_basis(ref, w_split, turn)
        gram_ref[...] = gram
        for at in range(len(others)):
            for turn in early:
                copies[at, turn].wait()
            store(product(w_split, blocks, at, early), begun.at[at], 0)

    own_region(compute)
    for (_, turn), copy in copies.items():
        if turn not in early:
            copy.wait()


def other_side_kernel(slab, far, early, late, *refs):
    w_refs, (w_early, gram_early, blocks, begun) = refs[: len(late)], refs[len(late) :][:4]
    *out_refs, w_split, gram_ref = refs[len(late) + 4 :]
    rank = w_refs[0].shape[0]
    for turn in early:
        w_split[turn] = w_early[turn]
    gram = gram_early[...]
    for turn, ref in zip(late, w_refs):
        gram = gram + split_basis(ref, w_split, turn)
    slabs = [gram[GRAM_ROWS * i : GRAM_ROWS * (i + 1)] for i in range(rank // GRAM_ROWS)]
    packed = jnp.concatenate(slabs, axis=1)
    gram_ref[...] = packed
    for index, out_ref in enumerate(out_refs):
        for at in range(far):
            block = index * far + at
            store(
                product(w_split, blocks, block, late), out_ref.at[pl.ds(slab * at, slab)], 0,
                begun.at[block],
            )
        out_ref[slab * far :] = packed


def own_side_kernel(near, width, n_col, owns, w_split, data_ref, out_ref, blocks, sems):
    order = [(at, turn) for at in enumerate(owns) for turn in range(n_col)]
    copies = block_copies(near, width, n_col, order, data_ref, blocks, sems)
    for copy in copies.values():
        copy.start()

    def multiply(at):
        for turn in range(n_col):
            copies[at, turn].wait()
        store(product(w_split, blocks, at, range(n_col)), out_ref.at[at], 0)

    for at in range(len(owns)):
        own_region(functools.partial(multiply, at))


def side_sum_kernel(slab, own_ref, gram_ref, *refs):
    far = own_ref.shape[0]
    got_refs, out_refs = refs[:-far], refs[-far:]
    gram = gram_ref[...]
    for got in got_refs:
        gram = gram + got[slab * far :]
    for at, out_ref in enumerate(out_refs):
        total = own_ref[at]
        for got in got_refs:
            total = total + got[slab * at : slab * (at + 1)]
        out_ref[:slab] = total
        out_ref[slab:] = gram


def sweep_kernel(width, *refs):
    parts, h_ref, out_ref = refs[:-2], refs[-2], refs[-1]
    rank = h_ref.shape[0]
    row_at = lax.axis_index("prow")
    total = parts[0][...]
    for part in parts[1:]:
        total = total + part[...]
    pieces = width // LANES
    cross = jnp.concatenate([total[rank * i : rank * (i + 1)] for i in range(pieces)], axis=1)
    packed = total[rank * pieces :]
    gram = jnp.concatenate(
        [packed[:, rank * i : rank * (i + 1)] for i in range(rank // GRAM_ROWS)], axis=0
    )
    h = h_ref[:, pl.ds(pl.multiple_of(row_at * width, width), width)]
    rest = cross - exact_dot(gram, h, ((1,), (0,)))
    rows = []
    for k in range(rank):
        inverse = 1.0 / gram[k : k + 1, k : k + 1]
        old = h[k : k + 1]
        fresh = jnp.maximum(old + rest[k : k + 1] * inverse, 0.0)
        rows.append(fresh)
        rest = rest - gram[:, k : k + 1] * (fresh - old)
    done = jnp.concatenate(rows, axis=0)
    for peer in range(out_ref.shape[0]):
        out_ref[peer] = done


def assemble_kernel(width, pieces, out_ref, sems):
    copies = []
    for peer in range(pieces.shape[0]):
        columns = pl.ds(width * peer, width)
        copies.append(pltpu.make_async_copy(pieces.at[peer], out_ref.at[:, columns], sems.at[peer]))
        copies[-1].start()
    for copy in copies:
        copy.wait()


def shards(n_row, n_col, data, w_trans, h_prior):
    rank, depth = w_trans.shape
    rows, cols = data.shape
    width = cols // n_row
    near = max(1, n_row // 4)
    far = n_row // near
    slab = rank * (width // LANES)
    turns = [*range(far // 2, far), *range(far // 2 - 1, -1, -1)]
    sides = range(1, near)

    def permute(value, axis, turn):
        size = n_row if axis == "prow" else n_col
        return lax.ppermute(value, axis, [(i, i ^ turn) for i in range(size)])

    w_parts = [w_trans] + [permute(w_trans, "pcol", t) for t in range(1, n_col)]
    early = list(range(1, min(2, n_col)))
    late = [turn for turn in range(n_col) if turn not in early]
    others = [(side, turn) for side in sides for turn in turns]
    owns = [(0, turn) for turn in turns]
    split_parts = jax.ShapeDtypeStruct((n_col, 2 * rank, depth), jnp.bfloat16)
    blocks, begun, w_early, gram_early = call(
        functools.partial(load_kernel, near, width, n_col, early, late, others),
        [
            floats(len(others), rows, width),
            floats(len(others), slab, LANES),
            split_parts,
            floats(rank, rank),
        ],
        [*(w_parts[t] for t in early), data], "load_other_side", 40,
        [VMEM] * len(early) + [HBM], [pltpu.SemaphoreType.DMA((len(others), n_col))],
        pl.CostEstimate(
            flops=0, bytes_accessed=8 * rows * width * len(others), transcendentals=0
        ),
    )
    *sent, w_split, gram = call(
        functools.partial(other_side_kernel, slab, far, early, late),
        [floats(far * slab + GRAM_ROWS, LANES)] * len(sides)
        + [split_parts, floats(GRAM_ROWS, LANES)],
        [*(w_parts[t] for t in late), w_early, gram_early, blocks, begun], "other_side", 8,
    )
    got = [permute(sent[side - 1], "prow", side) for side in sides]
    own = call(
        functools.partial(own_side_kernel, near, width, n_col, owns),
        floats(far, slab, LANES), [w_split, data], "own_side", 40, [VMEM, HBM],
        [
            pltpu.VMEM((far, rows, width), jnp.float32),
            pltpu.SemaphoreType.DMA((far, n_col)),
        ],
    )
    sums = call(
        functools.partial(side_sum_kernel, slab),
        [floats(slab + GRAM_ROWS, LANES)] * far, [own, gram, *got], "side_sum",
    )
    parts = [
        permute(value, "prow", turn * near) if turn else value
        for turn, value in zip(turns, sums)
    ]
    fresh = call(
        functools.partial(sweep_kernel, width), floats(n_row, rank, width),
        [*parts, h_prior], "row_sweep",
    )
    pieces = lax.all_to_all(fresh, "prow", 0, 0)
    return call(
        functools.partial(assemble_kernel, width), floats(rank, cols), [pieces], "assemble",
        scratch=[pltpu.SemaphoreType.DMA((n_row,))], out_specs=HBM,
    )


def solution(mesh):
    n_row, n_col = mesh.shape["prow"], mesh.shape["pcol"]
    placed = (P("prow", "pcol"), P(None, ("prow", "pcol")), P(None, "pcol"))
    return jax.shard_map(
        functools.partial(shards, n_row, n_col),
        mesh=mesh, in_specs=placed, out_specs=P(None, "pcol"), check_vma=False,
    )
```

```python
import functools

import jax
import jax.numpy as jnp
from jax import lax
from jax.experimental import pallas as pl
from jax.experimental.pallas import tpu as pltpu
from jax.sharding import PartitionSpec as P

LANES = 128
GRAM_ROWS = 8
VMEM = pl.BlockSpec(memory_space=pltpu.VMEM)
HBM = pl.BlockSpec(memory_space=pltpu.HBM)


def call(kernel, out_shape, operands, name, mebibytes=4, in_specs=None, scratch=(), cost=None,
         out_specs=VMEM):
    many = isinstance(out_shape, list)
    return pl.pallas_call(
        kernel,
        out_shape=out_shape,
        in_specs=in_specs or [VMEM] * len(operands),
        out_specs=[out_specs] * len(out_shape) if many else out_specs,
        compiler_params=pltpu.CompilerParams(vmem_limit_bytes=mebibytes * 1024 * 1024),
        scratch_shapes=list(scratch),
        cost_estimate=cost,
        name=name,
    )(*operands)


def floats(*shape):
    return jax.ShapeDtypeStruct(shape, jnp.float32)


def split(value):
    high = value.astype(jnp.bfloat16)
    low = (value - high.astype(jnp.float32)).astype(jnp.bfloat16)
    return high, low


def exact_dot(left, right, dims):
    return lax.dot_general(
        left, right, (dims, ((), ())),
        precision=lax.Precision.HIGHEST, preferred_element_type=jnp.float32,
    )


def block_start(near, width, side_turn, level_turn):
    row_at = lax.axis_index("prow")
    side, level = lax.rem(row_at, near), lax.div(row_at, near)
    peer = (level ^ level_turn) * near + (side ^ side_turn)
    return pl.multiple_of(peer * width, width)


def row_part(depth, turn):
    return pl.ds(pl.multiple_of((lax.axis_index("pcol") ^ turn) * depth, depth), depth)


def block_copies(near, width, n_col, order, data_ref, out_ref, sems):
    depth = data_ref.shape[0] // n_col
    copies = {}
    for (at, turns), turn in order:
        columns = pl.ds(block_start(near, width, *turns), width)
        rows = row_part(depth, turn)
        copies[at, turn] = pltpu.make_async_copy(
            data_ref.at[rows, columns], out_ref.at[at, rows], sems.at[at, turn]
        )
    return copies


def split_basis(part_ref, out_ref, turn):
    rank = part_ref.shape[0]
    part = part_ref[...]
    high, low = split(part)
    out_ref[turn, :rank] = high
    out_ref[turn, rank:] = low
    return exact_dot(part, part, ((1,), (1,)))


def product(w_split, blocks, at, turns):
    rank, depth = w_split.shape[1] // 2, w_split.shape[2]
    total = None
    for turn in turns:
        high, low = split(blocks[at, row_part(depth, turn)])
        upper = jnp.dot(w_split[turn], high, preferred_element_type=jnp.float32)
        term = (
            upper[:rank]
            + upper[rank:]
            + jnp.dot(w_split[turn, :rank], low, preferred_element_type=jnp.float32)
        )
        total = term if total is None else total + term
    return total


def store(cross, out_ref, row, before=None):
    rank = cross.shape[0]
    for i in range(cross.shape[1] // LANES):
        rows = slice(row + rank * i, row + rank * (i + 1))
        piece = cross[:, LANES * i : LANES * (i + 1)]
        out_ref[rows] = piece if before is None else piece + before[rows]


def own_region(compute):
    pl.when(lax.axis_index("prow") >= 0)(compute)


def load_kernel(near, width, n_col, early, late, others, *refs):
    w_refs, data_ref = refs[: len(early)], refs[len(early)]
    blocks, begun, w_split, gram_ref, sems = refs[len(early) + 1 :]
    order = [(at, turn) for turn in early + late for at in enumerate(others)]
    copies = block_copies(near, width, n_col, order, data_ref, blocks, sems)
    for copy in copies.values():
        copy.start()

    def compute():
        gram = split_basis(w_refs[0], w_split, early[0])
        for turn, ref in list(zip(early, w_refs))[1:]:
            gram = gram + split_basis(ref, w_split, turn)
        gram_ref[...] = gram
        for at in range(len(others)):
            for turn in early:
                copies[at, turn].wait()
            store(product(w_split, blocks, at, early), begun.at[at], 0)

    own_region(compute)
    for (_, turn), copy in copies.items():
        if turn not in early:
            copy.wait()


def other_side_kernel(slab, far, early, late, *refs):
    w_refs, (w_early, gram_early, blocks, begun) = refs[: len(late)], refs[len(late) :][:4]
    *out_refs, w_split, gram_ref = refs[len(late) + 4 :]
    rank = w_refs[0].shape[0]
    for turn in early:
        w_split[turn] = w_early[turn]
    gram = gram_early[...]
    for turn, ref in zip(late, w_refs):
        gram = gram + split_basis(ref, w_split, turn)
    slabs = [gram[GRAM_ROWS * i : GRAM_ROWS * (i + 1)] for i in range(rank // GRAM_ROWS)]
    packed = jnp.concatenate(slabs, axis=1)
    gram_ref[...] = packed
    for index, out_ref in enumerate(out_refs):
        for at in range(far):
            block = index * far + at
            store(
                product(w_split, blocks, block, late), out_ref.at[pl.ds(slab * at, slab)], 0,
                begun.at[block],
            )
        out_ref[slab * far :] = packed


def own_side_kernel(near, width, n_col, owns, w_split, data_ref, out_ref, blocks, sems):
    order = [(at, turn) for at in enumerate(owns) for turn in range(n_col)]
    copies = block_copies(near, width, n_col, order, data_ref, blocks, sems)
    for copy in copies.values():
        copy.start()

    def multiply(at):
        for turn in range(n_col):
            copies[at, turn].wait()
        store(product(w_split, blocks, at, range(n_col)), out_ref.at[at], 0)

    for at in range(len(owns)):
        own_region(functools.partial(multiply, at))


def side_sum_kernel(slab, own_ref, gram_ref, *refs):
    far = own_ref.shape[0]
    got_refs, out_refs = refs[:-far], refs[-far:]
    gram = gram_ref[...]
    for got in got_refs:
        gram = gram + got[slab * far :]
    for at, out_ref in enumerate(out_refs):
        total = own_ref[at]
        for got in got_refs:
            total = total + got[slab * at : slab * (at + 1)]
        out_ref[:slab] = total
        out_ref[slab:] = gram


def sweep_kernel(width, *refs):
    parts, h_ref, out_ref = refs[:-2], refs[-2], refs[-1]
    rank = h_ref.shape[0]
    row_at = lax.axis_index("prow")
    total = parts[0][...]
    for part in parts[1:]:
        total = total + part[...]
    pieces = width // LANES
    cross = jnp.concatenate([total[rank * i : rank * (i + 1)] for i in range(pieces)], axis=1)
    packed = total[rank * pieces :]
    gram = jnp.concatenate(
        [packed[:, rank * i : rank * (i + 1)] for i in range(rank // GRAM_ROWS)], axis=0
    )
    h = h_ref[:, pl.ds(pl.multiple_of(row_at * width, width), width)]
    rest = cross - exact_dot(gram, h, ((1,), (0,)))
    rows = []
    for k in range(rank):
        inverse = 1.0 / gram[k : k + 1, k : k + 1]
        old = h[k : k + 1]
        fresh = jnp.maximum(old + rest[k : k + 1] * inverse, 0.0)
        rows.append(fresh)
        rest = rest - gram[:, k : k + 1] * (fresh - old)
    done = jnp.concatenate(rows, axis=0)
    for peer in range(out_ref.shape[0]):
        out_ref[peer] = done


def assemble_kernel(width, ring, pieces, out_ref, sems):
    copies = []
    for at, peer in enumerate(ring):
        columns = pl.ds(width * peer, width)
        copies.append(pltpu.make_async_copy(pieces.at[at], out_ref.at[:, columns], sems.at[at]))
        copies[-1].start()
    for copy in copies:
        copy.wait()


def shards(n_row, n_col, data, w_trans, h_prior):
    rank, depth = w_trans.shape
    rows, cols = data.shape
    width = cols // n_row
    near = max(1, n_row // 4)
    far = n_row // near
    slab = rank * (width // LANES)
    turns = [*range(far // 2, far), *range(far // 2 - 1, -1, -1)]
    sides = range(1, near)

    def permute(value, axis, turn):
        size = n_row if axis == "prow" else n_col
        return lax.ppermute(value, axis, [(i, i ^ turn) for i in range(size)])

    w_parts = [w_trans] + [permute(w_trans, "pcol", t) for t in range(1, n_col)]
    early = list(range(1, min(2, n_col)))
    late = [turn for turn in range(n_col) if turn not in early]
    others = [(side, turn) for side in sides for turn in turns]
    owns = [(0, turn) for turn in turns]
    split_parts = jax.ShapeDtypeStruct((n_col, 2 * rank, depth), jnp.bfloat16)
    blocks, begun, w_early, gram_early = call(
        functools.partial(load_kernel, near, width, n_col, early, late, others),
        [
            floats(len(others), rows, width),
            floats(len(others), slab, LANES),
            split_parts,
            floats(rank, rank),
        ],
        [*(w_parts[t] for t in early), data], "load_other_side", 40,
        [VMEM] * len(early) + [HBM], [pltpu.SemaphoreType.DMA((len(others), n_col))],
        pl.CostEstimate(
            flops=0, bytes_accessed=8 * rows * width * len(others), transcendentals=0
        ),
    )
    *sent, w_split, gram = call(
        functools.partial(other_side_kernel, slab, far, early, late),
        [floats(far * slab + GRAM_ROWS, LANES)] * len(sides)
        + [split_parts, floats(GRAM_ROWS, LANES)],
        [*(w_parts[t] for t in late), w_early, gram_early, blocks, begun], "other_side", 8,
    )
    got = [permute(sent[side - 1], "prow", side) for side in sides]
    own = call(
        functools.partial(own_side_kernel, near, width, n_col, owns),
        floats(far, slab, LANES), [w_split, data], "own_side", 40, [VMEM, HBM],
        [
            pltpu.VMEM((far, rows, width), jnp.float32),
            pltpu.SemaphoreType.DMA((far, n_col)),
        ],
    )
    sums = call(
        functools.partial(side_sum_kernel, slab),
        [floats(slab + GRAM_ROWS, LANES)] * far, [own, gram, *got], "side_sum",
    )
    parts = [
        permute(value, "prow", turn * near) if turn else value
        for turn, value in zip(turns, sums)
    ]
    fresh = call(
        functools.partial(sweep_kernel, width), floats(n_row, rank, width),
        [*parts, h_prior], "row_sweep",
    )
    ring = [
        level * near + side
        for side in range(near) for level in (range(far) if side % 2 == 0 else range(far)[::-1])
    ]
    pieces = lax.all_to_all(fresh, "prow", 0, 0, axis_index_groups=[ring])
    return call(
        functools.partial(assemble_kernel, width, ring), floats(rank, cols), [pieces], "assemble",
        scratch=[pltpu.SemaphoreType.DMA((n_row,))], out_specs=HBM,
    )


def solution(mesh):
    n_row, n_col = mesh.shape["prow"], mesh.shape["pcol"]
    placed = (P("prow", "pcol"), P(None, ("prow", "pcol")), P(None, "pcol"))
    return jax.shard_map(
        functools.partial(shards, n_row, n_col),
        mesh=mesh, in_specs=placed, out_specs=P(None, "pcol"), check_vma=False,
    )
```

```python
import functools

import jax
import jax.numpy as jnp
from jax import lax
from jax.experimental import pallas as pl
from jax.experimental.pallas import tpu as pltpu
from jax.sharding import PartitionSpec as P

LANES = 128
GRAM_ROWS = 8
VMEM = pl.BlockSpec(memory_space=pltpu.VMEM)
HBM = pl.BlockSpec(memory_space=pltpu.HBM)


def call(kernel, out_shape, operands, name, mebibytes=4, in_specs=None, scratch=(), cost=None,
         out_specs=VMEM):
    many = isinstance(out_shape, list)
    return pl.pallas_call(
        kernel,
        out_shape=out_shape,
        in_specs=in_specs or [VMEM] * len(operands),
        out_specs=[out_specs] * len(out_shape) if many else out_specs,
        compiler_params=pltpu.CompilerParams(vmem_limit_bytes=mebibytes * 1024 * 1024),
        scratch_shapes=list(scratch),
        cost_estimate=cost,
        name=name,
    )(*operands)


def floats(*shape):
    return jax.ShapeDtypeStruct(shape, jnp.float32)


def split(value):
    high = value.astype(jnp.bfloat16)
    low = (value - high.astype(jnp.float32)).astype(jnp.bfloat16)
    return high, low


def exact_dot(left, right, dims):
    return lax.dot_general(
        left, right, (dims, ((), ())),
        precision=lax.Precision.HIGHEST, preferred_element_type=jnp.float32,
    )


def block_start(near, width, side_turn, level_turn):
    row_at = lax.axis_index("prow")
    side, level = lax.rem(row_at, near), lax.div(row_at, near)
    peer = (level ^ level_turn) * near + (side ^ side_turn)
    return pl.multiple_of(peer * width, width)


def row_part(depth, turn):
    return pl.ds(pl.multiple_of((lax.axis_index("pcol") ^ turn) * depth, depth), depth)


def block_copies(near, width, n_col, order, data_ref, out_ref, sems):
    depth = data_ref.shape[0] // n_col
    copies = {}
    for (at, turns), turn in order:
        columns = pl.ds(block_start(near, width, *turns), width)
        rows = row_part(depth, turn)
        copies[at, turn] = pltpu.make_async_copy(
            data_ref.at[rows, columns], out_ref.at[at, rows], sems.at[at, turn]
        )
    return copies


def split_basis(part_ref, out_ref, turn):
    rank = part_ref.shape[0]
    part = part_ref[...]
    high, low = split(part)
    out_ref[turn, :rank] = high
    out_ref[turn, rank:] = low
    return exact_dot(part, part, ((1,), (1,)))


def product(w_split, blocks, at, turns):
    rank, depth = w_split.shape[1] // 2, w_split.shape[2]
    total = None
    for turn in turns:
        high, low = split(blocks[at, row_part(depth, turn)])
        upper = jnp.dot(w_split[turn], high, preferred_element_type=jnp.float32)
        term = (
            upper[:rank]
            + upper[rank:]
            + jnp.dot(w_split[turn, :rank], low, preferred_element_type=jnp.float32)
        )
        total = term if total is None else total + term
    return total


def store(cross, out_ref, row, before=None):
    rank = cross.shape[0]
    for i in range(cross.shape[1] // LANES):
        rows = slice(row + rank * i, row + rank * (i + 1))
        piece = cross[:, LANES * i : LANES * (i + 1)]
        out_ref[rows] = piece if before is None else piece + before[rows]


def own_region(compute):
    pl.when(lax.axis_index("prow") >= 0)(compute)


def load_kernel(near, width, n_col, early, late, others, *refs):
    w_refs, data_ref = refs[: len(early)], refs[len(early)]
    blocks, begun, w_split, gram_ref, sems = refs[len(early) + 1 :]
    order = [(at, turn) for turn in early + late for at in enumerate(others)]
    copies = block_copies(near, width, n_col, order, data_ref, blocks, sems)
    for copy in copies.values():
        copy.start()

    def compute():
        gram = split_basis(w_refs[0], w_split, early[0])
        for turn, ref in list(zip(early, w_refs))[1:]:
            gram = gram + split_basis(ref, w_split, turn)
        gram_ref[...] = gram
        for at in range(len(others)):
            for turn in early:
                copies[at, turn].wait()
            store(product(w_split, blocks, at, early), begun.at[at], 0)

    own_region(compute)
    for (_, turn), copy in copies.items():
        if turn not in early:
            copy.wait()


def other_side_kernel(slab, far, early, late, *refs):
    w_refs, (w_early, gram_early, blocks, begun) = refs[: len(late)], refs[len(late) :][:4]
    *out_refs, w_split, gram_ref = refs[len(late) + 4 :]
    rank = w_refs[0].shape[0]
    for turn in early:
        w_split[turn] = w_early[turn]
    gram = gram_early[...]
    for turn, ref in zip(late, w_refs):
        gram = gram + split_basis(ref, w_split, turn)
    slabs = [gram[GRAM_ROWS * i : GRAM_ROWS * (i + 1)] for i in range(rank // GRAM_ROWS)]
    packed = jnp.concatenate(slabs, axis=1)
    gram_ref[...] = packed
    for index, out_ref in enumerate(out_refs):
        for at in range(far):
            block = index * far + at
            store(
                product(w_split, blocks, block, late), out_ref.at[pl.ds(slab * at, slab)], 0,
                begun.at[block],
            )
        out_ref[slab * far :] = packed


def own_side_kernel(near, width, n_col, owns, w_split, data_ref, out_ref, blocks, sems):
    order = [(at, turn) for at in enumerate(owns) for turn in range(n_col)]
    copies = block_copies(near, width, n_col, order, data_ref, blocks, sems)
    for copy in copies.values():
        copy.start()

    def multiply(at):
        for turn in range(n_col):
            copies[at, turn].wait()
        store(product(w_split, blocks, at, range(n_col)), out_ref.at[at], 0)

    for at in range(len(owns)):
        own_region(functools.partial(multiply, at))


def side_sum_kernel(slab, turns, pairs, own_ref, gram_ref, *refs):
    got_refs, out_refs = refs[: -len(pairs)], refs[-len(pairs) :]
    gram = gram_ref[...]
    for got in got_refs:
        gram = gram + got[slab * len(turns) :]
    for pair, out_ref in zip(pairs, out_refs):
        for at, turn in enumerate(pair):
            place = turns.index(turn)
            total = own_ref[place]
            for got in got_refs:
                total = total + got[slab * place : slab * (place + 1)]
            out_ref[slab * at : slab * (at + 1)] = total
        out_ref[slab * len(pair) :] = gram


def peer_start(near, width, level, side):
    return pl.multiple_of((level * near + side) * width, width)


def sweep_kernel(near, width, swapped, *refs):
    parts, h_ref, out_ref = refs[:-2], refs[-2], refs[-1]
    rank = h_ref.shape[0]
    row_at = lax.axis_index("prow")
    side, level = lax.rem(row_at, near), lax.div(row_at, near)
    pieces = width // LANES
    slab = rank * pieces
    packed, chunks = None, [None, None]
    for part, swap in zip(parts, swapped):
        gram_part = part[2 * slab :]
        packed = gram_part if packed is None else packed + gram_part
        for at in range(2):
            place = 1 - at if swap else at
            piece = part[slab * place : slab * (place + 1)]
            chunks[at] = piece if chunks[at] is None else chunks[at] + piece
    cross = jnp.concatenate(
        [chunk[rank * i : rank * (i + 1)] for chunk in chunks for i in range(pieces)], axis=1
    )
    gram = jnp.concatenate(
        [packed[:, rank * i : rank * (i + 1)] for i in range(rank // GRAM_ROWS)], axis=0
    )
    starts = [peer_start(near, width, at, side) for at in (level, level ^ 2)]
    h = jnp.concatenate([h_ref[:, pl.ds(start, width)] for start in starts], axis=1)
    rest = cross - exact_dot(gram, h, ((1,), (0,)))
    rows = []
    for k in range(rank):
        inverse = 1.0 / gram[k : k + 1, k : k + 1]
        old = h[k : k + 1]
        fresh = jnp.maximum(old + rest[k : k + 1] * inverse, 0.0)
        rows.append(fresh)
        rest = rest - gram[:, k : k + 1] * (fresh - old)
    done = jnp.concatenate(rows, axis=0)
    for member in range(out_ref.shape[0]):
        for at in range(2):
            out_ref[member, at] = done[:, width * at : width * (at + 1)]


def assemble_kernel(near, width, pieces, out_ref, sems):
    level = lax.div(lax.axis_index("prow"), near)
    copies = []
    for member in range(pieces.shape[0]):
        above, side = member // near, member % near
        theirs = lax.div(level, 2) * 2 + above
        for at, source in enumerate((theirs, theirs ^ 2)):
            columns = pl.ds(peer_start(near, width, source, side), width)
            copy = pltpu.make_async_copy(
                pieces.at[member, at], out_ref.at[:, columns], sems.at[member, at]
            )
            copy.start()
            copies.append(copy)
    for copy in copies:
        copy.wait()


def shards(n_row, n_col, data, w_trans, h_prior):
    rank, depth = w_trans.shape
    rows, cols = data.shape
    width = cols // n_row
    near = max(1, n_row // 4)
    far = n_row // near
    slab = rank * (width // LANES)
    turns = [*range(far // 2, far), *range(far // 2 - 1, -1, -1)]
    sides = range(1, near)

    def permute(value, axis, turn):
        size = n_row if axis == "prow" else n_col
        return lax.ppermute(value, axis, [(i, i ^ turn) for i in range(size)])

    w_parts = [w_trans] + [permute(w_trans, "pcol", t) for t in range(1, n_col)]
    early = list(range(1, min(2, n_col)))
    late = [turn for turn in range(n_col) if turn not in early]
    others = [(side, turn) for side in sides for turn in turns]
    owns = [(0, turn) for turn in turns]
    split_parts = jax.ShapeDtypeStruct((n_col, 2 * rank, depth), jnp.bfloat16)
    blocks, begun, w_early, gram_early = call(
        functools.partial(load_kernel, near, width, n_col, early, late, others),
        [
            floats(len(others), rows, width),
            floats(len(others), slab, LANES),
            split_parts,
            floats(rank, rank),
        ],
        [*(w_parts[t] for t in early), data], "load_other_side", 40,
        [VMEM] * len(early) + [HBM], [pltpu.SemaphoreType.DMA((len(others), n_col))],
        pl.CostEstimate(
            flops=0, bytes_accessed=8 * rows * width * len(others), transcendentals=0
        ),
    )
    *sent, w_split, gram = call(
        functools.partial(other_side_kernel, slab, far, early, late),
        [floats(far * slab + GRAM_ROWS, LANES)] * len(sides)
        + [split_parts, floats(GRAM_ROWS, LANES)],
        [*(w_parts[t] for t in late), w_early, gram_early, blocks, begun], "other_side", 8,
    )
    got = [permute(sent[side - 1], "prow", side) for side in sides]
    own = call(
        functools.partial(own_side_kernel, near, width, n_col, owns),
        floats(far, slab, LANES), [w_split, data], "own_side", 40, [VMEM, HBM],
        [
            pltpu.VMEM((far, rows, width), jnp.float32),
            pltpu.SemaphoreType.DMA((far, n_col)),
        ],
    )
    pairs = [(2, 0), (3, 1), (1, 3)]
    sums = call(
        functools.partial(side_sum_kernel, slab, turns, pairs),
        [floats(2 * slab + GRAM_ROWS, LANES)] * len(pairs), [own, gram, *got], "side_sum",
    )
    parts = [permute(value, "prow", pair[0] * near) for pair, value in zip(pairs, sums)]
    parts.append(sums[0])
    members = 2 * near
    fresh = call(
        functools.partial(sweep_kernel, near, width, [False, False, False, True]),
        floats(members, 2, rank, width), [*parts, h_prior], "row_sweep",
    )
    groups = [[low + at for at in range(members)] for low in range(0, n_row, members)]
    pieces = lax.all_to_all(fresh, "prow", 0, 0, axis_index_groups=groups)
    return call(
        functools.partial(assemble_kernel, near, width), floats(rank, cols), [pieces],
        "assemble", scratch=[pltpu.SemaphoreType.DMA((members, 2))], out_specs=HBM,
    )


def solution(mesh):
    n_row, n_col = mesh.shape["prow"], mesh.shape["pcol"]
    placed = (P("prow", "pcol"), P(None, ("prow", "pcol")), P(None, "pcol"))
    return jax.shard_map(
        functools.partial(shards, n_row, n_col),
        mesh=mesh, in_specs=placed, out_specs=P(None, "pcol"), check_vma=False,
    )
```

```python
import functools

import jax
import jax.numpy as jnp
from jax import lax
from jax.experimental import pallas as pl
from jax.experimental.pallas import tpu as pltpu
from jax.sharding import PartitionSpec as P

LANES = 128
GRAM_ROWS = 8
VMEM = pl.BlockSpec(memory_space=pltpu.VMEM)
HBM = pl.BlockSpec(memory_space=pltpu.HBM)


def call(kernel, out_shape, operands, name, mebibytes=4, in_specs=None, scratch=(), cost=None,
         out_specs=VMEM):
    many = isinstance(out_shape, list)
    return pl.pallas_call(
        kernel,
        out_shape=out_shape,
        in_specs=in_specs or [VMEM] * len(operands),
        out_specs=[out_specs] * len(out_shape) if many else out_specs,
        compiler_params=pltpu.CompilerParams(vmem_limit_bytes=mebibytes * 1024 * 1024),
        scratch_shapes=list(scratch),
        cost_estimate=cost,
        name=name,
    )(*operands)


def floats(*shape):
    return jax.ShapeDtypeStruct(shape, jnp.float32)


def split(value):
    high = value.astype(jnp.bfloat16)
    low = (value - high.astype(jnp.float32)).astype(jnp.bfloat16)
    return high, low


def exact_dot(left, right, dims):
    return lax.dot_general(
        left, right, (dims, ((), ())),
        precision=lax.Precision.HIGHEST, preferred_element_type=jnp.float32,
    )


def block_start(near, width, side_turn, level_turn):
    row_at = lax.axis_index("prow")
    side, level = lax.rem(row_at, near), lax.div(row_at, near)
    peer = (level ^ level_turn) * near + (side ^ side_turn)
    return pl.multiple_of(peer * width, width)


def row_part(depth, turn):
    return pl.ds(pl.multiple_of((lax.axis_index("pcol") ^ turn) * depth, depth), depth)


def block_copies(near, width, n_col, order, data_ref, out_ref, sems):
    depth = data_ref.shape[0] // n_col
    copies = {}
    for (at, turns), turn in order:
        columns = pl.ds(block_start(near, width, *turns), width)
        rows = row_part(depth, turn)
        copies[at, turn] = pltpu.make_async_copy(
            data_ref.at[rows, columns], out_ref.at[at, rows], sems.at[at, turn]
        )
    return copies


def split_basis(part_ref, out_ref, turn):
    rank = part_ref.shape[0]
    part = part_ref[...]
    high, low = split(part)
    out_ref[turn, :rank] = high
    out_ref[turn, rank:] = low
    return exact_dot(part, part, ((1,), (1,)))


def product(w_split, blocks, at, turns):
    rank, depth = w_split.shape[1] // 2, w_split.shape[2]
    total = None
    for turn in turns:
        high, low = split(blocks[at, row_part(depth, turn)])
        upper = jnp.dot(w_split[turn], high, preferred_element_type=jnp.float32)
        term = (
            upper[:rank]
            + upper[rank:]
            + jnp.dot(w_split[turn, :rank], low, preferred_element_type=jnp.float32)
        )
        total = term if total is None else total + term
    return total


def store(cross, out_ref, row, before=None):
    rank = cross.shape[0]
    for i in range(cross.shape[1] // LANES):
        rows = slice(row + rank * i, row + rank * (i + 1))
        piece = cross[:, LANES * i : LANES * (i + 1)]
        out_ref[rows] = piece if before is None else piece + before[rows]


def own_region(compute):
    pl.when(lax.axis_index("prow") >= 0)(compute)


def load_kernel(near, width, n_col, early, late, others, *refs):
    w_refs, data_ref = refs[: len(early)], refs[len(early)]
    blocks, begun, w_split, gram_ref, sems = refs[len(early) + 1 :]
    order = [(at, turn) for turn in early + late for at in enumerate(others)]
    copies = block_copies(near, width, n_col, order, data_ref, blocks, sems)
    for copy in copies.values():
        copy.start()

    def compute():
        gram = split_basis(w_refs[0], w_split, early[0])
        for turn, ref in list(zip(early, w_refs))[1:]:
            gram = gram + split_basis(ref, w_split, turn)
        gram_ref[...] = gram
        for at in range(len(others)):
            for turn in early:
                copies[at, turn].wait()
            store(product(w_split, blocks, at, early), begun.at[at], 0)

    own_region(compute)
    for (_, turn), copy in copies.items():
        if turn not in early:
            copy.wait()


def other_side_kernel(slab, far, early, late, *refs):
    w_refs, (w_early, gram_early, blocks, begun) = refs[: len(late)], refs[len(late) :][:4]
    *out_refs, w_split, gram_ref = refs[len(late) + 4 :]
    rank = w_refs[0].shape[0]
    for turn in early:
        w_split[turn] = w_early[turn]
    gram = gram_early[...]
    for turn, ref in zip(late, w_refs):
        gram = gram + split_basis(ref, w_split, turn)
    slabs = [gram[GRAM_ROWS * i : GRAM_ROWS * (i + 1)] for i in range(rank // GRAM_ROWS)]
    packed = jnp.concatenate(slabs, axis=1)
    gram_ref[...] = packed
    for index, out_ref in enumerate(out_refs):
        for at in range(far):
            block = index * far + at
            store(
                product(w_split, blocks, block, late), out_ref.at[pl.ds(slab * at, slab)], 0,
                begun.at[block],
            )
        out_ref[slab * far :] = packed


def own_side_kernel(near, width, n_col, owns, w_split, data_ref, out_ref, blocks, sems):
    order = [(at, turn) for at in enumerate(owns) for turn in range(n_col)]
    copies = block_copies(near, width, n_col, order, data_ref, blocks, sems)
    for copy in copies.values():
        copy.start()

    def multiply(at):
        for turn in range(n_col):
            copies[at, turn].wait()
        store(product(w_split, blocks, at, range(n_col)), out_ref.at[at], 0)

    for at in range(len(owns)):
        own_region(functools.partial(multiply, at))


def side_sum_kernel(slab, turns, pairs, own_ref, gram_ref, *refs):
    got_refs, out_refs = refs[: -len(pairs)], refs[-len(pairs) :]
    gram = gram_ref[...]
    for got in got_refs:
        gram = gram + got[slab * len(turns) :]
    for pair, out_ref in zip(pairs, out_refs):
        for at, turn in enumerate(pair):
            place = turns.index(turn)
            total = own_ref[place]
            for got in got_refs:
                total = total + got[slab * place : slab * (place + 1)]
            out_ref[slab * at : slab * (at + 1)] = total
        out_ref[slab * len(pair) :] = gram


def peer_start(near, width, level, side):
    return pl.multiple_of((level * near + side) * width, width)


def sweep_kernel(near, width, *refs):
    parts, h_ref, out_ref = refs[:-2], refs[-2], refs[-1]
    rank = h_ref.shape[0]
    row_at = lax.axis_index("prow")
    side, level = lax.rem(row_at, near), lax.div(row_at, near)
    pieces = width // LANES
    slab = rank * pieces
    packed, chunks = None, [None, None]
    for part in parts:
        gram_part = part[2 * slab :]
        packed = gram_part if packed is None else packed + gram_part
        for at in range(2):
            piece = part[slab * at : slab * (at + 1)]
            chunks[at] = piece if chunks[at] is None else chunks[at] + piece
    cross = jnp.concatenate(
        [chunk[rank * i : rank * (i + 1)] for chunk in chunks for i in range(pieces)], axis=1
    )
    gram = jnp.concatenate(
        [packed[:, rank * i : rank * (i + 1)] for i in range(rank // GRAM_ROWS)], axis=0
    )
    starts = [peer_start(near, width, at, side) for at in (level, level ^ 2)]
    h = jnp.concatenate([h_ref[:, pl.ds(start, width)] for start in starts], axis=1)
    rest = cross - exact_dot(gram, h, ((1,), (0,)))
    rows = []
    for k in range(rank):
        inverse = 1.0 / gram[k : k + 1, k : k + 1]
        old = h[k : k + 1]
        fresh = jnp.maximum(old + rest[k : k + 1] * inverse, 0.0)
        rows.append(fresh)
        rest = rest - gram[:, k : k + 1] * (fresh - old)
    done = jnp.concatenate(rows, axis=0)
    for at in range(2):
        out_ref[at] = done[:, width * at : width * (at + 1)]


def assemble_kernel(near, width, members, *refs):
    piece_refs, (out_ref, sems) = refs[:-2], refs[-2:]
    row_at = lax.axis_index("prow")
    side, level = lax.rem(row_at, near), lax.div(row_at, near)
    copies = []
    for member, ((above, side_turn), piece_ref) in enumerate(zip(members, piece_refs)):
        theirs = level ^ above
        for at, source in enumerate((theirs, theirs ^ 2)):
            columns = pl.ds(peer_start(near, width, source, side ^ side_turn), width)
            copy = pltpu.make_async_copy(
                piece_ref.at[at], out_ref.at[:, columns], sems.at[member, at]
            )
            copy.start()
            copies.append(copy)
    for copy in copies:
        copy.wait()


def shards(n_row, n_col, data, w_trans, h_prior):
    rank, depth = w_trans.shape
    rows, cols = data.shape
    width = cols // n_row
    near = max(1, n_row // 4)
    far = n_row // near
    slab = rank * (width // LANES)
    turns = [*range(far // 2, far), *range(far // 2 - 1, -1, -1)]
    sides = range(1, near)

    def permute(value, axis, turn):
        size = n_row if axis == "prow" else n_col
        return lax.ppermute(value, axis, [(i, i ^ turn) for i in range(size)])

    w_parts = [w_trans] + [permute(w_trans, "pcol", t) for t in range(1, n_col)]
    early = list(range(1, min(2, n_col)))
    late = [turn for turn in range(n_col) if turn not in early]
    others = [(side, turn) for side in sides for turn in turns]
    owns = [(0, turn) for turn in turns]
    split_parts = jax.ShapeDtypeStruct((n_col, 2 * rank, depth), jnp.bfloat16)
    blocks, begun, w_early, gram_early = call(
        functools.partial(load_kernel, near, width, n_col, early, late, others),
        [
            floats(len(others), rows, width),
            floats(len(others), slab, LANES),
            split_parts,
            floats(rank, rank),
        ],
        [*(w_parts[t] for t in early), data], "load_other_side", 40,
        [VMEM] * len(early) + [HBM], [pltpu.SemaphoreType.DMA((len(others), n_col))],
        pl.CostEstimate(
            flops=0, bytes_accessed=8 * rows * width * len(others), transcendentals=0
        ),
    )
    *sent, w_split, gram = call(
        functools.partial(other_side_kernel, slab, far, early, late),
        [floats(far * slab + GRAM_ROWS, LANES)] * len(sides)
        + [split_parts, floats(GRAM_ROWS, LANES)],
        [*(w_parts[t] for t in late), w_early, gram_early, blocks, begun], "other_side", 8,
    )
    got = [permute(sent[side - 1], "prow", side) for side in sides]
    own = call(
        functools.partial(own_side_kernel, near, width, n_col, owns),
        floats(far, slab, LANES), [w_split, data], "own_side", 40, [VMEM, HBM],
        [
            pltpu.VMEM((far, rows, width), jnp.float32),
            pltpu.SemaphoreType.DMA((far, n_col)),
        ],
    )
    pairs = [(2, 0), (3, 1), (1, 3), (0, 2)]
    sums = call(
        functools.partial(side_sum_kernel, slab, turns, pairs),
        [floats(2 * slab + GRAM_ROWS, LANES)] * len(pairs), [own, gram, *got], "side_sum",
    )
    parts = [
        permute(value, "prow", pair[0] * near) if pair[0] else value
        for pair, value in zip(pairs, sums)
    ]
    fresh = call(
        functools.partial(sweep_kernel, near, width), floats(2, rank, width), [*parts, h_prior],
        "row_sweep",
    )
    members = [(above, side) for above in range(2) for side in range(near)]
    pieces = [
        permute(fresh, "prow", above * near + side) if above or side else fresh
        for above, side in members
    ]
    return call(
        functools.partial(assemble_kernel, near, width, members), floats(rank, cols), pieces,
        "assemble", scratch=[pltpu.SemaphoreType.DMA((len(members), 2))], out_specs=HBM,
    )


def solution(mesh):
    n_row, n_col = mesh.shape["prow"], mesh.shape["pcol"]
    placed = (P("prow", "pcol"), P(None, ("prow", "pcol")), P(None, "pcol"))
    return jax.shard_map(
        functools.partial(shards, n_row, n_col),
        mesh=mesh, in_specs=placed, out_specs=P(None, "pcol"), check_vma=False,
    )
```

```python
import functools

import jax
import jax.numpy as jnp
from jax import lax
from jax.experimental import pallas as pl
from jax.experimental.pallas import tpu as pltpu
from jax.sharding import PartitionSpec as P

LANES = 128
GRAM_ROWS = 8
VMEM = pl.BlockSpec(memory_space=pltpu.VMEM)
HBM = pl.BlockSpec(memory_space=pltpu.HBM)


def call(kernel, out_shape, operands, name, mebibytes=4, in_specs=None, scratch=(), cost=None,
         out_specs=VMEM):
    many = isinstance(out_shape, list)
    return pl.pallas_call(
        kernel,
        out_shape=out_shape,
        in_specs=in_specs or [VMEM] * len(operands),
        out_specs=[out_specs] * len(out_shape) if many else out_specs,
        compiler_params=pltpu.CompilerParams(vmem_limit_bytes=mebibytes * 1024 * 1024),
        scratch_shapes=list(scratch),
        cost_estimate=cost,
        name=name,
    )(*operands)


def floats(*shape):
    return jax.ShapeDtypeStruct(shape, jnp.float32)


def split(value):
    high = value.astype(jnp.bfloat16)
    low = (value - high.astype(jnp.float32)).astype(jnp.bfloat16)
    return high, low


def exact_dot(left, right, dims):
    return lax.dot_general(
        left, right, (dims, ((), ())),
        precision=lax.Precision.HIGHEST, preferred_element_type=jnp.float32,
    )


def block_start(near, width, side_turn, level_turn):
    row_at = lax.axis_index("prow")
    side, level = lax.rem(row_at, near), lax.div(row_at, near)
    peer = (level ^ level_turn) * near + (side ^ side_turn)
    return pl.multiple_of(peer * width, width)


def row_part(depth, turn):
    return pl.ds(pl.multiple_of((lax.axis_index("pcol") ^ turn) * depth, depth), depth)


def block_copies(near, width, n_col, order, data_ref, out_ref, sems):
    depth = data_ref.shape[0] // n_col
    copies = {}
    for (at, turns), turn in order:
        columns = pl.ds(block_start(near, width, *turns), width)
        rows = row_part(depth, turn)
        copies[at, turn] = pltpu.make_async_copy(
            data_ref.at[rows, columns], out_ref.at[at, rows], sems.at[at, turn]
        )
    return copies


def split_basis(part_ref, out_ref, turn):
    rank = part_ref.shape[0]
    part = part_ref[...]
    high, low = split(part)
    out_ref[turn, :rank] = high
    out_ref[turn, rank:] = low
    return exact_dot(part, part, ((1,), (1,)))


def product(w_split, blocks, at, turns):
    rank, depth = w_split.shape[1] // 2, w_split.shape[2]
    total = None
    for turn in turns:
        high, low = split(blocks[at, row_part(depth, turn)])
        upper = jnp.dot(w_split[turn], high, preferred_element_type=jnp.float32)
        term = (
            upper[:rank]
            + upper[rank:]
            + jnp.dot(w_split[turn, :rank], low, preferred_element_type=jnp.float32)
        )
        total = term if total is None else total + term
    return total


def store(cross, out_ref, row, before=None):
    rank = cross.shape[0]
    for i in range(cross.shape[1] // LANES):
        rows = slice(row + rank * i, row + rank * (i + 1))
        piece = cross[:, LANES * i : LANES * (i + 1)]
        out_ref[rows] = piece if before is None else piece + before[rows]


def own_region(compute):
    pl.when(lax.axis_index("prow") >= 0)(compute)


def load_kernel(near, width, n_col, early, late, others, *refs):
    w_refs, data_ref = refs[: len(early)], refs[len(early)]
    blocks, begun, w_split, gram_ref, sems = refs[len(early) + 1 :]
    order = [(at, turn) for turn in early + late for at in enumerate(others)]
    copies = block_copies(near, width, n_col, order, data_ref, blocks, sems)
    for copy in copies.values():
        copy.start()

    def compute():
        gram = split_basis(w_refs[0], w_split, early[0])
        for turn, ref in list(zip(early, w_refs))[1:]:
            gram = gram + split_basis(ref, w_split, turn)
        gram_ref[...] = gram
        for at in range(len(others)):
            for turn in early:
                copies[at, turn].wait()
            store(product(w_split, blocks, at, early), begun.at[at], 0)

    own_region(compute)
    for (_, turn), copy in copies.items():
        if turn not in early:
            copy.wait()


def other_side_kernel(near, width, n_col, slab, far, early, late, own, *refs):
    w_refs, (w_early, gram_early, blocks, begun, data_ref) = refs[: len(late)], refs[len(late) :][:5]
    *out_refs, w_split, gram_ref, own_block, sems = refs[len(late) + 5 :]
    rank = w_refs[0].shape[0]
    order = [((0, own), turn) for turn in range(n_col)]
    copies = block_copies(near, width, n_col, order, data_ref, own_block, sems)
    for copy in copies.values():
        copy.start()

    def compute():
        for turn in early:
            w_split[turn] = w_early[turn]
        gram = gram_early[...]
        for turn, ref in zip(late, w_refs):
            gram = gram + split_basis(ref, w_split, turn)
        slabs = [gram[GRAM_ROWS * i : GRAM_ROWS * (i + 1)] for i in range(rank // GRAM_ROWS)]
        packed = jnp.concatenate(slabs, axis=1)
        gram_ref[...] = packed
        for index, out_ref in enumerate(out_refs):
            for at in range(far):
                block = index * far + at
                store(
                    product(w_split, blocks, block, late), out_ref.at[pl.ds(slab * at, slab)], 0,
                    begun.at[block],
                )
            out_ref[slab * far :] = packed

    own_region(compute)
    for copy in copies.values():
        copy.wait()


def own_side_kernel(near, width, n_col, owns, w_split, own_block, data_ref, out_ref, rest, sems):
    order = [(at, turn) for at in enumerate(owns[1:]) for turn in range(n_col)]
    copies = block_copies(near, width, n_col, order, data_ref, rest, sems)
    for copy in copies.values():
        copy.start()

    def multiply(at):
        for turn in range(n_col):
            copies[at, turn].wait()
        store(product(w_split, rest, at, range(n_col)), out_ref.at[at + 1], 0)

    own_region(lambda: store(product(w_split, own_block, 0, range(n_col)), out_ref.at[0], 0))
    for at in range(len(owns) - 1):
        own_region(functools.partial(multiply, at))


def side_sum_kernel(slab, turns, pairs, own_ref, gram_ref, *refs):
    got_refs, out_refs = refs[: -len(pairs)], refs[-len(pairs) :]
    gram = gram_ref[...]
    for got in got_refs:
        gram = gram + got[slab * len(turns) :]
    for pair, out_ref in zip(pairs, out_refs):
        for at, turn in enumerate(pair):
            place = turns.index(turn)
            total = own_ref[place]
            for got in got_refs:
                total = total + got[slab * place : slab * (place + 1)]
            out_ref[slab * at : slab * (at + 1)] = total
        out_ref[slab * len(pair) :] = gram


def peer_start(near, width, level, side):
    return pl.multiple_of((level * near + side) * width, width)


def sweep_kernel(near, width, *refs):
    parts, h_ref, out_ref = refs[:-2], refs[-2], refs[-1]
    rank = h_ref.shape[0]
    row_at = lax.axis_index("prow")
    side, level = lax.rem(row_at, near), lax.div(row_at, near)
    pieces = width // LANES
    slab = rank * pieces
    packed, chunks = None, [None, None]
    for part in parts:
        gram_part = part[2 * slab :]
        packed = gram_part if packed is None else packed + gram_part
        for at in range(2):
            piece = part[slab * at : slab * (at + 1)]
            chunks[at] = piece if chunks[at] is None else chunks[at] + piece
    cross = jnp.concatenate(
        [chunk[rank * i : rank * (i + 1)] for chunk in chunks for i in range(pieces)], axis=1
    )
    gram = jnp.concatenate(
        [packed[:, rank * i : rank * (i + 1)] for i in range(rank // GRAM_ROWS)], axis=0
    )
    starts = [peer_start(near, width, at, side) for at in (level, level ^ 2)]
    h = jnp.concatenate([h_ref[:, pl.ds(start, width)] for start in starts], axis=1)
    rest = cross - exact_dot(gram, h, ((1,), (0,)))
    rows = []
    for k in range(rank):
        inverse = 1.0 / gram[k : k + 1, k : k + 1]
        old = h[k : k + 1]
        fresh = jnp.maximum(old + rest[k : k + 1] * inverse, 0.0)
        rows.append(fresh)
        rest = rest - gram[:, k : k + 1] * (fresh - old)
    done = jnp.concatenate(rows, axis=0)
    for at in range(2):
        out_ref[at] = done[:, width * at : width * (at + 1)]


def assemble_kernel(near, width, members, *refs):
    piece_refs, (out_ref, sems) = refs[:-2], refs[-2:]
    row_at = lax.axis_index("prow")
    side, level = lax.rem(row_at, near), lax.div(row_at, near)
    copies = []
    for member, ((above, side_turn), piece_ref) in enumerate(zip(members, piece_refs)):
        theirs = level ^ above
        for at, source in enumerate((theirs, theirs ^ 2)):
            columns = pl.ds(peer_start(near, width, source, side ^ side_turn), width)
            copy = pltpu.make_async_copy(
                piece_ref.at[at], out_ref.at[:, columns], sems.at[member, at]
            )
            copy.start()
            copies.append(copy)
    for copy in copies:
        copy.wait()


def shards(n_row, n_col, data, w_trans, h_prior):
    rank, depth = w_trans.shape
    rows, cols = data.shape
    width = cols // n_row
    near = max(1, n_row // 4)
    far = n_row // near
    slab = rank * (width // LANES)
    turns = [*range(far // 2, far), *range(far // 2 - 1, -1, -1)]
    sides = range(1, near)

    def permute(value, axis, turn):
        size = n_row if axis == "prow" else n_col
        return lax.ppermute(value, axis, [(i, i ^ turn) for i in range(size)])

    w_parts = [w_trans] + [permute(w_trans, "pcol", t) for t in range(1, n_col)]
    early = list(range(1, min(2, n_col)))
    late = [turn for turn in range(n_col) if turn not in early]
    others = [(side, turn) for side in sides for turn in turns]
    owns = [(0, turn) for turn in turns]
    split_parts = jax.ShapeDtypeStruct((n_col, 2 * rank, depth), jnp.bfloat16)
    blocks, begun, w_early, gram_early = call(
        functools.partial(load_kernel, near, width, n_col, early, late, others),
        [
            floats(len(others), rows, width),
            floats(len(others), slab, LANES),
            split_parts,
            floats(rank, rank),
        ],
        [*(w_parts[t] for t in early), data], "load_other_side", 40,
        [VMEM] * len(early) + [HBM], [pltpu.SemaphoreType.DMA((len(others), n_col))],
        pl.CostEstimate(
            flops=0, bytes_accessed=8 * rows * width * len(others), transcendentals=0
        ),
    )
    *sent, w_split, gram, own_block = call(
        functools.partial(
            other_side_kernel, near, width, n_col, slab, far, early, late, owns[0]
        ),
        [floats(far * slab + GRAM_ROWS, LANES)] * len(sides)
        + [split_parts, floats(GRAM_ROWS, LANES), floats(1, rows, width)],
        [*(w_parts[t] for t in late), w_early, gram_early, blocks, begun, data], "other_side", 37,
        [VMEM] * (len(late) + 4) + [HBM], [pltpu.SemaphoreType.DMA((1, n_col))],
    )
    got = [permute(sent[side - 1], "prow", side) for side in sides]
    own = call(
        functools.partial(own_side_kernel, near, width, n_col, owns),
        floats(far, slab, LANES), [w_split, own_block, data], "own_side", 40,
        [VMEM] * 2 + [HBM],
        [
            pltpu.VMEM((far - 1, rows, width), jnp.float32),
            pltpu.SemaphoreType.DMA((far - 1, n_col)),
        ],
    )
    pairs = [(2, 0), (3, 1), (1, 3), (0, 2)]
    sums = call(
        functools.partial(side_sum_kernel, slab, turns, pairs),
        [floats(2 * slab + GRAM_ROWS, LANES)] * len(pairs), [own, gram, *got], "side_sum",
    )
    parts = [
        permute(value, "prow", pair[0] * near) if pair[0] else value
        for pair, value in zip(pairs, sums)
    ]
    fresh = call(
        functools.partial(sweep_kernel, near, width), floats(2, rank, width), [*parts, h_prior],
        "row_sweep",
    )
    members = [(above, side) for above in range(2) for side in range(near)]
    pieces = [
        permute(fresh, "prow", above * near + side) if above or side else fresh
        for above, side in members
    ]
    return call(
        functools.partial(assemble_kernel, near, width, members), floats(rank, cols), pieces,
        "assemble", scratch=[pltpu.SemaphoreType.DMA((len(members), 2))], out_specs=HBM,
    )


def solution(mesh):
    n_row, n_col = mesh.shape["prow"], mesh.shape["pcol"]
    placed = (P("prow", "pcol"), P(None, ("prow", "pcol")), P(None, "pcol"))
    return jax.shard_map(
        functools.partial(shards, n_row, n_col),
        mesh=mesh, in_specs=placed, out_specs=P(None, "pcol"), check_vma=False,
    )
```

```python
import functools

import jax
import jax.numpy as jnp
from jax import lax
from jax.experimental import pallas as pl
from jax.experimental.pallas import tpu as pltpu
from jax.sharding import PartitionSpec as P

LANES = 128
GRAM_ROWS = 8
VMEM = pl.BlockSpec(memory_space=pltpu.VMEM)
HBM = pl.BlockSpec(memory_space=pltpu.HBM)


def call(kernel, out_shape, operands, name, mebibytes=4, in_specs=None, scratch=(), cost=None,
         out_specs=VMEM):
    many = isinstance(out_shape, list)
    return pl.pallas_call(
        kernel,
        out_shape=out_shape,
        in_specs=in_specs or [VMEM] * len(operands),
        out_specs=[out_specs] * len(out_shape) if many else out_specs,
        compiler_params=pltpu.CompilerParams(vmem_limit_bytes=mebibytes * 1024 * 1024),
        scratch_shapes=list(scratch),
        cost_estimate=cost,
        name=name,
    )(*operands)


def floats(*shape):
    return jax.ShapeDtypeStruct(shape, jnp.float32)


def split(value):
    high = value.astype(jnp.bfloat16)
    low = (value - high.astype(jnp.float32)).astype(jnp.bfloat16)
    return high, low


def exact_dot(left, right, dims):
    return lax.dot_general(
        left, right, (dims, ((), ())),
        precision=lax.Precision.HIGHEST, preferred_element_type=jnp.float32,
    )


def block_start(near, width, side_turn, level_turn):
    row_at = lax.axis_index("prow")
    side, level = lax.rem(row_at, near), lax.div(row_at, near)
    peer = (level ^ level_turn) * near + (side ^ side_turn)
    return pl.multiple_of(peer * width, width)


def row_part(depth, turn):
    return pl.ds(pl.multiple_of((lax.axis_index("pcol") ^ turn) * depth, depth), depth)


def block_copies(near, width, n_col, order, data_ref, out_ref, sems):
    depth = data_ref.shape[0] // n_col
    copies = {}
    for (at, turns), turn in order:
        columns = pl.ds(block_start(near, width, *turns), width)
        rows = row_part(depth, turn)
        copies[at, turn] = pltpu.make_async_copy(
            data_ref.at[rows, columns], out_ref.at[at, rows], sems.at[at, turn]
        )
    return copies


def split_basis(part_ref, out_ref, turn):
    rank = part_ref.shape[0]
    part = part_ref[...]
    high, low = split(part)
    out_ref[turn, :rank] = high
    out_ref[turn, rank:] = low
    return exact_dot(part, part, ((1,), (1,)))


def product(w_split, blocks, at, turns):
    rank, depth = w_split.shape[1] // 2, w_split.shape[2]
    total = None
    for turn in turns:
        high, low = split(blocks[at, row_part(depth, turn)])
        upper = jnp.dot(w_split[turn], high, preferred_element_type=jnp.float32)
        term = (
            upper[:rank]
            + upper[rank:]
            + jnp.dot(w_split[turn, :rank], low, preferred_element_type=jnp.float32)
        )
        total = term if total is None else total + term
    return total


def store(cross, out_ref, row, before=None):
    rank = cross.shape[0]
    for i in range(cross.shape[1] // LANES):
        rows = slice(row + rank * i, row + rank * (i + 1))
        piece = cross[:, LANES * i : LANES * (i + 1)]
        out_ref[rows] = piece if before is None else piece + before[rows]


def own_region(compute):
    pl.when(lax.axis_index("prow") >= 0)(compute)


def load_kernel(near, width, n_col, early, late, others, *refs):
    w_refs, data_ref = refs[: len(early)], refs[len(early)]
    blocks, begun, w_split, gram_ref, sems = refs[len(early) + 1 :]
    order = [(at, turn) for turn in early + late for at in enumerate(others)]
    copies = block_copies(near, width, n_col, order, data_ref, blocks, sems)
    for copy in copies.values():
        copy.start()

    def compute():
        gram = split_basis(w_refs[0], w_split, early[0])
        for turn, ref in list(zip(early, w_refs))[1:]:
            gram = gram + split_basis(ref, w_split, turn)
        gram_ref[...] = gram
        for at in range(len(others)):
            for turn in early:
                copies[at, turn].wait()
            store(product(w_split, blocks, at, early), begun.at[at], 0)

    own_region(compute)
    for (_, turn), copy in copies.items():
        if turn not in early:
            copy.wait()


def other_side_kernel(near, width, n_col, slab, far, early, late, own, *refs):
    w_refs, (w_early, gram_early, blocks, begun, data_ref) = refs[: len(late)], refs[len(late) :][:5]
    *out_refs, w_split, gram_ref, own_block, sems = refs[len(late) + 5 :]
    rank = w_refs[0].shape[0]
    order = [((0, own), turn) for turn in range(n_col)]
    copies = block_copies(near, width, n_col, order, data_ref, own_block, sems)
    for copy in copies.values():
        copy.start()

    def compute():
        for turn in early:
            w_split[turn] = w_early[turn]
        gram = gram_early[...]
        for turn, ref in zip(late, w_refs):
            gram = gram + split_basis(ref, w_split, turn)
        slabs = [gram[GRAM_ROWS * i : GRAM_ROWS * (i + 1)] for i in range(rank // GRAM_ROWS)]
        packed = jnp.concatenate(slabs, axis=1)
        gram_ref[...] = packed
        for index, out_ref in enumerate(out_refs):
            for at in range(far):
                block = index * far + at
                store(
                    product(w_split, blocks, block, late), out_ref.at[pl.ds(slab * at, slab)], 0,
                    begun.at[block],
                )
            out_ref[slab * far :] = packed

    own_region(compute)
    for copy in copies.values():
        copy.wait()


def own_side_kernel(near, width, n_col, owns, w_split, own_block, data_ref, out_ref, rest, sems):
    order = [(at, turn) for at in enumerate(owns[1:]) for turn in range(n_col)]
    copies = block_copies(near, width, n_col, order, data_ref, rest, sems)
    for copy in copies.values():
        copy.start()

    def multiply(at):
        for turn in range(n_col):
            copies[at, turn].wait()
        store(product(w_split, rest, at, range(n_col)), out_ref.at[at + 1], 0)

    own_region(lambda: store(product(w_split, own_block, 0, range(n_col)), out_ref.at[0], 0))
    for at in range(len(owns) - 1):
        own_region(functools.partial(multiply, at))


def side_sum_kernel(slab, turns, pairs, own_ref, gram_ref, *refs):
    got_refs, out_refs = refs[: -len(pairs)], refs[-len(pairs) :]
    gram = gram_ref[...]
    for got in got_refs:
        gram = gram + got[slab * len(turns) :]
    for pair, out_ref in zip(pairs, out_refs):
        for at, turn in enumerate(pair):
            place = turns.index(turn)
            total = own_ref[place]
            for got in got_refs:
                total = total + got[slab * place : slab * (place + 1)]
            out_ref[slab * at : slab * (at + 1)] = total
        out_ref[slab * len(pair) :] = gram


def peer_start(near, width, level, side):
    return pl.multiple_of((level * near + side) * width, width)


def sweep_kernel(near, width, *refs):
    parts, h_ref, out_ref = refs[:-2], refs[-2], refs[-1]
    rank = h_ref.shape[0]
    row_at = lax.axis_index("prow")
    side, level = lax.rem(row_at, near), lax.div(row_at, near)
    pieces = width // LANES
    slab = rank * pieces
    packed, chunks = None, [None, None]
    for part in parts:
        gram_part = part[2 * slab :]
        packed = gram_part if packed is None else packed + gram_part
        for at in range(2):
            piece = part[slab * at : slab * (at + 1)]
            chunks[at] = piece if chunks[at] is None else chunks[at] + piece
    cross = jnp.concatenate(
        [chunk[rank * i : rank * (i + 1)] for chunk in chunks for i in range(pieces)], axis=1
    )
    gram = jnp.concatenate(
        [packed[:, rank * i : rank * (i + 1)] for i in range(rank // GRAM_ROWS)], axis=0
    )
    starts = [peer_start(near, width, at, side) for at in (level, level ^ 2)]
    h = jnp.concatenate([h_ref[:, pl.ds(start, width)] for start in starts], axis=1)
    rest = cross - exact_dot(gram, h, ((1,), (0,)))
    rows = []
    for k in range(rank):
        inverse = 1.0 / gram[k : k + 1, k : k + 1]
        old = h[k : k + 1]
        fresh = jnp.maximum(old + rest[k : k + 1] * inverse, 0.0)
        rows.append(fresh)
        rest = rest - gram[:, k : k + 1] * (fresh - old)
    done = jnp.concatenate(rows, axis=0)
    for at in range(2):
        out_ref[at] = done[:, width * at : width * (at + 1)]


def assemble_kernel(near, width, members, *refs):
    piece_refs, (out_ref, sems) = refs[:-2], refs[-2:]
    row_at = lax.axis_index("prow")
    side, level = lax.rem(row_at, near), lax.div(row_at, near)
    copies = []
    for member, ((above, side_turn), piece_ref) in enumerate(zip(members, piece_refs)):
        theirs = level ^ above
        for at, source in enumerate((theirs, theirs ^ 2)):
            columns = pl.ds(peer_start(near, width, source, side ^ side_turn), width)
            copy = pltpu.make_async_copy(
                piece_ref.at[at], out_ref.at[:, columns], sems.at[member, at]
            )
            copy.start()
            copies.append(copy)
    for copy in copies:
        copy.wait()


def shards(n_row, n_col, data, w_trans, h_prior):
    rank, depth = w_trans.shape
    rows, cols = data.shape
    width = cols // n_row
    near = max(1, n_row // 4)
    far = n_row // near
    slab = rank * (width // LANES)
    turns = [*range(far // 2, far), *range(far // 2 - 1, -1, -1)]
    sides = range(1, near)

    def permute(value, axis, turn):
        size = n_row if axis == "prow" else n_col
        return lax.ppermute(value, axis, [(i, i ^ turn) for i in range(size)])

    w_parts = [w_trans] + [permute(w_trans, "pcol", t) for t in range(1, n_col)]
    early = list(range(1, min(2, n_col)))
    late = [turn for turn in range(n_col) if turn not in early]
    others = [(side, turn) for side in sides for turn in turns]
    owns = [(0, turn) for turn in turns]
    split_parts = jax.ShapeDtypeStruct((n_col, 2 * rank, depth), jnp.bfloat16)
    blocks, begun, w_early, gram_early = call(
        functools.partial(load_kernel, near, width, n_col, early, late, others),
        [
            floats(len(others), rows, width),
            floats(len(others), slab, LANES),
            split_parts,
            floats(rank, rank),
        ],
        [*(w_parts[t] for t in early), data], "load_other_side", 40,
        [VMEM] * len(early) + [HBM], [pltpu.SemaphoreType.DMA((len(others), n_col))],
        pl.CostEstimate(
            flops=0, bytes_accessed=8 * rows * width * len(others), transcendentals=0
        ),
    )
    *sent, w_split, gram, own_block = call(
        functools.partial(
            other_side_kernel, near, width, n_col, slab, far, early, late, owns[0]
        ),
        [floats(far * slab + GRAM_ROWS, LANES)] * len(sides)
        + [split_parts, floats(GRAM_ROWS, LANES), floats(1, rows, width)],
        [*(w_parts[t] for t in late), w_early, gram_early, blocks, begun, data], "other_side", 37,
        [VMEM] * (len(late) + 4) + [HBM], [pltpu.SemaphoreType.DMA((1, n_col))],
    )
    got = [permute(sent[side - 1], "prow", side) for side in sides]
    own = call(
        functools.partial(own_side_kernel, near, width, n_col, owns),
        floats(far, slab, LANES), [w_split, own_block, data], "own_side", 40,
        [VMEM] * 2 + [HBM],
        [
            pltpu.VMEM((far - 1, rows, width), jnp.float32),
            pltpu.SemaphoreType.DMA((far - 1, n_col)),
        ],
    )
    pairs = [(2, 0), (3, 1), (1, 3), (0, 2)]
    sums = call(
        functools.partial(side_sum_kernel, slab, turns, pairs),
        [floats(2 * slab + GRAM_ROWS, LANES)] * len(pairs), [own, gram, *got], "side_sum",
    )
    parts = [
        permute(value, "prow", pair[0] * near) if pair[0] else value
        for pair, value in zip(pairs, sums)
    ]
    fresh = call(
        functools.partial(sweep_kernel, near, width), floats(2, rank, width), [*parts, h_prior],
        "row_sweep",
    )
    members = [(0, 0), (1, 0)] + [(above, side) for above in range(2) for side in sides]
    pieces = [
        permute(fresh, "prow", above * near + side) if above or side else fresh
        for above, side in members
    ]
    return call(
        functools.partial(assemble_kernel, near, width, members), floats(rank, cols), pieces,
        "assemble", scratch=[pltpu.SemaphoreType.DMA((len(members), 2))], out_specs=HBM,
    )


def solution(mesh):
    n_row, n_col = mesh.shape["prow"], mesh.shape["pcol"]
    placed = (P("prow", "pcol"), P(None, ("prow", "pcol")), P(None, "pcol"))
    return jax.shard_map(
        functools.partial(shards, n_row, n_col),
        mesh=mesh, in_specs=placed, out_specs=P(None, "pcol"), check_vma=False,
    )
```

```python
import functools

import jax
import jax.numpy as jnp
from jax import lax
from jax.experimental import pallas as pl
from jax.experimental.pallas import tpu as pltpu
from jax.sharding import PartitionSpec as P

LANES = 128
GRAM_ROWS = 8
VMEM = pl.BlockSpec(memory_space=pltpu.VMEM)
HBM = pl.BlockSpec(memory_space=pltpu.HBM)


def call(kernel, out_shape, operands, name, mebibytes=4, in_specs=None, scratch=(), cost=None,
         out_specs=VMEM):
    many = isinstance(out_shape, list)
    return pl.pallas_call(
        kernel,
        out_shape=out_shape,
        in_specs=in_specs or [VMEM] * len(operands),
        out_specs=[out_specs] * len(out_shape) if many else out_specs,
        compiler_params=pltpu.CompilerParams(vmem_limit_bytes=mebibytes * 1024 * 1024),
        scratch_shapes=list(scratch),
        cost_estimate=cost,
        name=name,
    )(*operands)


def floats(*shape):
    return jax.ShapeDtypeStruct(shape, jnp.float32)


def split(value):
    high = value.astype(jnp.bfloat16)
    low = (value - high.astype(jnp.float32)).astype(jnp.bfloat16)
    return high, low


def exact_dot(left, right, dims):
    return lax.dot_general(
        left, right, (dims, ((), ())),
        precision=lax.Precision.HIGHEST, preferred_element_type=jnp.float32,
    )


def block_start(near, width, side_turn, level_turn):
    row_at = lax.axis_index("prow")
    side, level = lax.rem(row_at, near), lax.div(row_at, near)
    peer = (level ^ level_turn) * near + (side ^ side_turn)
    return pl.multiple_of(peer * width, width)


def row_part(depth, turn):
    return pl.ds(pl.multiple_of((lax.axis_index("pcol") ^ turn) * depth, depth), depth)


def block_copies(near, width, n_col, order, data_ref, out_ref, sems):
    depth = data_ref.shape[0] // n_col
    copies = {}
    for (at, turns), turn in order:
        columns = pl.ds(block_start(near, width, *turns), width)
        rows = row_part(depth, turn)
        copies[at, turn] = pltpu.make_async_copy(
            data_ref.at[rows, columns], out_ref.at[at, rows], sems.at[at, turn]
        )
    return copies


def split_basis(part_ref, out_ref, turn):
    rank = part_ref.shape[0]
    part = part_ref[...]
    high, low = split(part)
    out_ref[turn, :rank] = high
    out_ref[turn, rank:] = low
    return exact_dot(part, part, ((1,), (1,)))


def product(w_split, blocks, at, turns):
    rank, depth = w_split.shape[1] // 2, w_split.shape[2]
    total = None
    for turn in turns:
        high, low = split(blocks[at, row_part(depth, turn)])
        upper = jnp.dot(w_split[turn], high, preferred_element_type=jnp.float32)
        term = (
            upper[:rank]
            + upper[rank:]
            + jnp.dot(w_split[turn, :rank], low, preferred_element_type=jnp.float32)
        )
        total = term if total is None else total + term
    return total


def store(cross, out_ref, row, before=None):
    rank = cross.shape[0]
    for i in range(cross.shape[1] // LANES):
        rows = slice(row + rank * i, row + rank * (i + 1))
        piece = cross[:, LANES * i : LANES * (i + 1)]
        out_ref[rows] = piece if before is None else piece + before[rows]


def own_region(compute):
    pl.when(lax.axis_index("prow") >= 0)(compute)


def load_kernel(near, width, n_col, early, late, others, *refs):
    w_refs, data_ref = refs[: len(early)], refs[len(early)]
    blocks, begun, w_split, gram_ref, sems = refs[len(early) + 1 :]
    order = [(at, turn) for turn in early + late for at in enumerate(others)]
    copies = block_copies(near, width, n_col, order, data_ref, blocks, sems)
    for copy in copies.values():
        copy.start()

    def compute():
        gram = split_basis(w_refs[0], w_split, early[0])
        for turn, ref in list(zip(early, w_refs))[1:]:
            gram = gram + split_basis(ref, w_split, turn)
        gram_ref[...] = gram
        for at in range(len(others)):
            for turn in early:
                copies[at, turn].wait()
            store(product(w_split, blocks, at, early), begun.at[at], 0)

    own_region(compute)
    for (_, turn), copy in copies.items():
        if turn not in early:
            copy.wait()


def other_side_kernel(near, width, n_col, slab, far, early, late, own, *refs):
    w_refs, (w_early, gram_early, blocks, begun, data_ref) = refs[: len(late)], refs[len(late) :][:5]
    *out_refs, w_split, gram_ref, own_block, sems = refs[len(late) + 5 :]
    rank = w_refs[0].shape[0]
    order = [((0, own), turn) for turn in range(n_col)]
    copies = block_copies(near, width, n_col, order, data_ref, own_block, sems)
    for copy in copies.values():
        copy.start()

    def compute():
        for turn in early:
            w_split[turn] = w_early[turn]
        gram = gram_early[...]
        for turn, ref in zip(late, w_refs):
            gram = gram + split_basis(ref, w_split, turn)
        slabs = [gram[GRAM_ROWS * i : GRAM_ROWS * (i + 1)] for i in range(rank // GRAM_ROWS)]
        packed = jnp.concatenate(slabs, axis=1)
        gram_ref[...] = packed
        for index, out_ref in enumerate(out_refs):
            for at in range(far):
                block = index * far + at
                store(
                    product(w_split, blocks, block, late), out_ref.at[pl.ds(slab * at, slab)], 0,
                    begun.at[block],
                )
            out_ref[slab * far :] = packed

    own_region(compute)
    for copy in copies.values():
        copy.wait()


def own_side_kernel(near, width, n_col, owns, w_split, own_block, data_ref, out_ref, rest, sems):
    order = [(at, turn) for at in enumerate(owns[1:]) for turn in range(n_col)]
    copies = block_copies(near, width, n_col, order, data_ref, rest, sems)
    for copy in copies.values():
        copy.start()

    def multiply(at):
        for turn in range(n_col):
            copies[at, turn].wait()
        store(product(w_split, rest, at, range(n_col)), out_ref.at[at + 1], 0)

    own_region(lambda: store(product(w_split, own_block, 0, range(n_col)), out_ref.at[0], 0))
    for at in range(len(owns) - 1):
        own_region(functools.partial(multiply, at))


def side_sum_kernel(slab, turns, pairs, own_ref, gram_ref, *refs):
    got_refs, out_refs = refs[: -len(pairs)], refs[-len(pairs) :]
    gram = gram_ref[...]
    for got in got_refs:
        gram = gram + got[slab * len(turns) :]
    for pair, out_ref in zip(pairs, out_refs):
        for at, turn in enumerate(pair):
            place = turns.index(turn)
            total = own_ref[place]
            for got in got_refs:
                total = total + got[slab * place : slab * (place + 1)]
            out_ref[slab * at : slab * (at + 1)] = total
        out_ref[slab * len(pair) :] = gram


def peer_start(near, width, level, side):
    return pl.multiple_of((level * near + side) * width, width)


def sweep_kernel(near, width, *refs):
    parts, h_ref, out_ref = refs[:-2], refs[-2], refs[-1]
    rank = h_ref.shape[0]
    row_at = lax.axis_index("prow")
    side, level = lax.rem(row_at, near), lax.div(row_at, near)
    pieces = width // LANES
    slab = rank * pieces
    packed, chunks = None, [None, None]
    odd = lax.rem(level, 2)
    for part, first in zip(parts, (1 - odd, 0, odd, 0)):
        gram_part = part[2 * slab :]
        packed = gram_part if packed is None else packed + gram_part
        for at, place in enumerate((first, 1 - first)):
            piece = part[pl.ds(pl.multiple_of(slab * place, slab), slab)]
            chunks[at] = piece if chunks[at] is None else chunks[at] + piece
    cross = jnp.concatenate(
        [chunk[rank * i : rank * (i + 1)] for chunk in chunks for i in range(pieces)], axis=1
    )
    gram = jnp.concatenate(
        [packed[:, rank * i : rank * (i + 1)] for i in range(rank // GRAM_ROWS)], axis=0
    )
    starts = [peer_start(near, width, at, side) for at in (level, level ^ 2)]
    h = jnp.concatenate([h_ref[:, pl.ds(start, width)] for start in starts], axis=1)
    rest = cross - exact_dot(gram, h, ((1,), (0,)))
    rows = []
    for k in range(rank):
        inverse = 1.0 / gram[k : k + 1, k : k + 1]
        old = h[k : k + 1]
        fresh = jnp.maximum(old + rest[k : k + 1] * inverse, 0.0)
        rows.append(fresh)
        rest = rest - gram[:, k : k + 1] * (fresh - old)
    done = jnp.concatenate(rows, axis=0)
    for at in range(2):
        out_ref[at] = done[:, width * at : width * (at + 1)]


def assemble_kernel(near, width, members, *refs):
    piece_refs, (out_ref, sems) = refs[:-2], refs[-2:]
    row_at = lax.axis_index("prow")
    side, level = lax.rem(row_at, near), lax.div(row_at, near)
    copies = []
    for member, ((above, side_turn), piece_ref) in enumerate(zip(members, piece_refs)):
        theirs = level ^ above
        for at, source in enumerate((theirs, theirs ^ 2)):
            columns = pl.ds(peer_start(near, width, source, side ^ side_turn), width)
            copy = pltpu.make_async_copy(
                piece_ref.at[at], out_ref.at[:, columns], sems.at[member, at]
            )
            copy.start()
            copies.append(copy)
    for copy in copies:
        copy.wait()


def shards(n_row, n_col, data, w_trans, h_prior):
    rank, depth = w_trans.shape
    rows, cols = data.shape
    width = cols // n_row
    near = max(1, n_row // 4)
    far = n_row // near
    slab = rank * (width // LANES)
    turns = [*range(far // 2, far), *range(far // 2 - 1, -1, -1)]
    sides = range(1, near)

    def permute(value, axis, turn):
        size = n_row if axis == "prow" else n_col
        return lax.ppermute(value, axis, [(i, i ^ turn) for i in range(size)])

    w_parts = [w_trans] + [permute(w_trans, "pcol", t) for t in range(1, n_col)]
    early = list(range(1, min(2, n_col)))
    late = [turn for turn in range(n_col) if turn not in early]
    others = [(side, turn) for side in sides for turn in turns]
    owns = [(0, turn) for turn in turns]
    split_parts = jax.ShapeDtypeStruct((n_col, 2 * rank, depth), jnp.bfloat16)
    blocks, begun, w_early, gram_early = call(
        functools.partial(load_kernel, near, width, n_col, early, late, others),
        [
            floats(len(others), rows, width),
            floats(len(others), slab, LANES),
            split_parts,
            floats(rank, rank),
        ],
        [*(w_parts[t] for t in early), data], "load_other_side", 40,
        [VMEM] * len(early) + [HBM], [pltpu.SemaphoreType.DMA((len(others), n_col))],
        pl.CostEstimate(
            flops=0, bytes_accessed=8 * rows * width * len(others), transcendentals=0
        ),
    )
    *sent, w_split, gram, own_block = call(
        functools.partial(
            other_side_kernel, near, width, n_col, slab, far, early, late, owns[0]
        ),
        [floats(far * slab + GRAM_ROWS, LANES)] * len(sides)
        + [split_parts, floats(GRAM_ROWS, LANES), floats(1, rows, width)],
        [*(w_parts[t] for t in late), w_early, gram_early, blocks, begun, data], "other_side", 37,
        [VMEM] * (len(late) + 4) + [HBM], [pltpu.SemaphoreType.DMA((1, n_col))],
    )
    got = [permute(sent[side - 1], "prow", side) for side in sides]
    own = call(
        functools.partial(own_side_kernel, near, width, n_col, owns),
        floats(far, slab, LANES), [w_split, own_block, data], "own_side", 40,
        [VMEM] * 2 + [HBM],
        [
            pltpu.VMEM((far - 1, rows, width), jnp.float32),
            pltpu.SemaphoreType.DMA((far - 1, n_col)),
        ],
    )
    pairs = [(1, 3), (2, 0), (1, 3), (0, 2)]
    sums = call(
        functools.partial(side_sum_kernel, slab, turns, pairs),
        [floats(2 * slab + GRAM_ROWS, LANES)] * len(pairs), [own, gram, *got], "side_sum",
    )
    parts = [
        lax.ppermute(value, "prow", [(i, (i + shift * near) % n_row) for i in range(n_row)])
        for shift, value in enumerate(sums[:3], 1)
    ]
    parts.append(sums[3])
    fresh = call(
        functools.partial(sweep_kernel, near, width), floats(2, rank, width), [*parts, h_prior],
        "row_sweep",
    )
    members = [(0, 0), (1, 0)] + [(above, side) for above in range(2) for side in sides]
    pieces = [
        permute(fresh, "prow", above * near + side) if above or side else fresh
        for above, side in members
    ]
    return call(
        functools.partial(assemble_kernel, near, width, members), floats(rank, cols), pieces,
        "assemble", scratch=[pltpu.SemaphoreType.DMA((len(members), 2))], out_specs=HBM,
    )


def solution(mesh):
    n_row, n_col = mesh.shape["prow"], mesh.shape["pcol"]
    placed = (P("prow", "pcol"), P(None, ("prow", "pcol")), P(None, "pcol"))
    return jax.shard_map(
        functools.partial(shards, n_row, n_col),
        mesh=mesh, in_specs=placed, out_specs=P(None, "pcol"), check_vma=False,
    )
```

```python
import functools

import jax
import jax.numpy as jnp
from jax import lax
from jax.experimental import pallas as pl
from jax.experimental.pallas import tpu as pltpu
from jax.sharding import PartitionSpec as P

LANES = 128
GRAM_ROWS = 8
VMEM = pl.BlockSpec(memory_space=pltpu.VMEM)
HBM = pl.BlockSpec(memory_space=pltpu.HBM)


def call(kernel, out_shape, operands, name, mebibytes=4, in_specs=None, scratch=(), cost=None,
         out_specs=VMEM):
    many = isinstance(out_shape, list)
    return pl.pallas_call(
        kernel,
        out_shape=out_shape,
        in_specs=in_specs or [VMEM] * len(operands),
        out_specs=[out_specs] * len(out_shape) if many else out_specs,
        compiler_params=pltpu.CompilerParams(vmem_limit_bytes=mebibytes * 1024 * 1024),
        scratch_shapes=list(scratch),
        cost_estimate=cost,
        name=name,
    )(*operands)


def floats(*shape):
    return jax.ShapeDtypeStruct(shape, jnp.float32)


def split(value):
    high = value.astype(jnp.bfloat16)
    low = (value - high.astype(jnp.float32)).astype(jnp.bfloat16)
    return high, low


def exact_dot(left, right, dims):
    return lax.dot_general(
        left, right, (dims, ((), ())),
        precision=lax.Precision.HIGHEST, preferred_element_type=jnp.float32,
    )


def block_start(near, width, side_turn, level_turn):
    row_at = lax.axis_index("prow")
    side, level = lax.rem(row_at, near), lax.div(row_at, near)
    peer = (level ^ level_turn) * near + (side ^ side_turn)
    return pl.multiple_of(peer * width, width)


def row_part(depth, turn):
    return pl.ds(pl.multiple_of((lax.axis_index("pcol") ^ turn) * depth, depth), depth)


def block_copies(near, width, n_col, order, data_ref, out_ref, sems):
    depth = data_ref.shape[0] // n_col
    copies = {}
    for (at, turns), turn in order:
        columns = pl.ds(block_start(near, width, *turns), width)
        rows = row_part(depth, turn)
        copies[at, turn] = pltpu.make_async_copy(
            data_ref.at[rows, columns], out_ref.at[at, rows], sems.at[at, turn]
        )
    return copies


def split_basis(part_ref, out_ref, turn):
    rank = part_ref.shape[0]
    part = part_ref[...]
    high, low = split(part)
    out_ref[turn, :rank] = high
    out_ref[turn, rank:] = low
    return exact_dot(part, part, ((1,), (1,)))


def product(w_split, blocks, at, turns):
    rank, depth = w_split.shape[1] // 2, w_split.shape[2]
    total = None
    for turn in turns:
        high, low = split(blocks[at, row_part(depth, turn)])
        upper = jnp.dot(w_split[turn], high, preferred_element_type=jnp.float32)
        term = (
            upper[:rank]
            + upper[rank:]
            + jnp.dot(w_split[turn, :rank], low, preferred_element_type=jnp.float32)
        )
        total = term if total is None else total + term
    return total


def store(cross, out_ref, row, before=None):
    rank = cross.shape[0]
    for i in range(cross.shape[1] // LANES):
        rows = slice(row + rank * i, row + rank * (i + 1))
        piece = cross[:, LANES * i : LANES * (i + 1)]
        out_ref[rows] = piece if before is None else piece + before[rows]


def own_region(compute):
    pl.when(lax.axis_index("prow") >= 0)(compute)


def load_kernel(near, width, n_col, early, late, others, *refs):
    w_refs, data_ref = refs[: len(early)], refs[len(early)]
    blocks, begun, w_split, gram_ref, sems = refs[len(early) + 1 :]
    order = [(at, turn) for turn in early + late for at in enumerate(others)]
    copies = block_copies(near, width, n_col, order, data_ref, blocks, sems)
    for copy in copies.values():
        copy.start()

    def compute():
        gram = split_basis(w_refs[0], w_split, early[0])
        for turn, ref in list(zip(early, w_refs))[1:]:
            gram = gram + split_basis(ref, w_split, turn)
        gram_ref[...] = gram
        for at in range(len(others)):
            for turn in early:
                copies[at, turn].wait()
            store(product(w_split, blocks, at, early), begun.at[at], 0)

    own_region(compute)
    for (_, turn), copy in copies.items():
        if turn not in early:
            copy.wait()


def other_side_kernel(near, width, n_col, slab, far, early, late, own, fetched, *refs):
    w_refs, (w_early, gram_early, blocks, begun, data_ref) = refs[: len(late)], refs[len(late) :][:5]
    *out_refs, w_split, gram_ref, own_block, sems = refs[len(late) + 5 :]
    rank = w_refs[0].shape[0]
    order = [((0, own), turn) for turn in fetched]
    copies = block_copies(near, width, n_col, order, data_ref, own_block, sems)
    for copy in copies.values():
        copy.start()

    def compute():
        for turn in early:
            w_split[turn] = w_early[turn]
        gram = gram_early[...]
        for turn, ref in zip(late, w_refs):
            gram = gram + split_basis(ref, w_split, turn)
        slabs = [gram[GRAM_ROWS * i : GRAM_ROWS * (i + 1)] for i in range(rank // GRAM_ROWS)]
        packed = jnp.concatenate(slabs, axis=1)
        gram_ref[...] = packed
        for index, out_ref in enumerate(out_refs):
            for at in range(far):
                block = index * far + at
                store(
                    product(w_split, blocks, block, late), out_ref.at[pl.ds(slab * at, slab)], 0,
                    begun.at[block],
                )
            out_ref[slab * far :] = packed

    own_region(compute)
    for copy in copies.values():
        copy.wait()


def own_side_kernel(near, width, n_col, owns, fetched, w_split, first_rows, data_ref, *refs):
    out_ref, blocks, sems = refs
    order = [(at, turn) for at in enumerate(owns) for turn in range(n_col)]
    order = [(at, turn) for at, turn in order if at[0] or turn not in fetched]
    copies = block_copies(near, width, n_col, order, data_ref, blocks, sems)
    for copy in copies.values():
        copy.start()

    def multiply(at):
        total = None if at else product(w_split, first_rows, 0, fetched)
        for turn in range(n_col):
            if (at, turn) in copies:
                copies[at, turn].wait()
                term = product(w_split, blocks, at, [turn])
                total = term if total is None else total + term
        store(total, out_ref.at[at], 0)

    for at in range(len(owns)):
        own_region(functools.partial(multiply, at))


def side_sum_kernel(slab, turns, pairs, own_ref, gram_ref, *refs):
    got_refs, out_refs = refs[: -len(pairs)], refs[-len(pairs) :]
    gram = gram_ref[...]
    for got in got_refs:
        gram = gram + got[slab * len(turns) :]
    for pair, out_ref in zip(pairs, out_refs):
        for at, turn in enumerate(pair):
            place = turns.index(turn)
            total = own_ref[place]
            for got in got_refs:
                total = total + got[slab * place : slab * (place + 1)]
            out_ref[slab * at : slab * (at + 1)] = total
        out_ref[slab * len(pair) :] = gram


def peer_start(near, width, level, side):
    return pl.multiple_of((level * near + side) * width, width)


def sweep_kernel(near, width, *refs):
    parts, h_ref, out_ref = refs[:-2], refs[-2], refs[-1]
    rank = h_ref.shape[0]
    row_at = lax.axis_index("prow")
    side, level = lax.rem(row_at, near), lax.div(row_at, near)
    pieces = width // LANES
    slab = rank * pieces
    packed, chunks = None, [None, None]
    for part in parts:
        gram_part = part[2 * slab :]
        packed = gram_part if packed is None else packed + gram_part
        for at in range(2):
            piece = part[slab * at : slab * (at + 1)]
            chunks[at] = piece if chunks[at] is None else chunks[at] + piece
    cross = jnp.concatenate(
        [chunk[rank * i : rank * (i + 1)] for chunk in chunks for i in range(pieces)], axis=1
    )
    gram = jnp.concatenate(
        [packed[:, rank * i : rank * (i + 1)] for i in range(rank // GRAM_ROWS)], axis=0
    )
    starts = [peer_start(near, width, at, side) for at in (level, level ^ 2)]
    h = jnp.concatenate([h_ref[:, pl.ds(start, width)] for start in starts], axis=1)
    rest = cross - exact_dot(gram, h, ((1,), (0,)))
    rows = []
    for k in range(rank):
        inverse = 1.0 / gram[k : k + 1, k : k + 1]
        old = h[k : k + 1]
        fresh = jnp.maximum(old + rest[k : k + 1] * inverse, 0.0)
        rows.append(fresh)
        rest = rest - gram[:, k : k + 1] * (fresh - old)
    done = jnp.concatenate(rows, axis=0)
    for at in range(2):
        out_ref[at] = done[:, width * at : width * (at + 1)]


def assemble_kernel(near, width, members, *refs):
    piece_refs, (out_ref, sems) = refs[:-2], refs[-2:]
    row_at = lax.axis_index("prow")
    side, level = lax.rem(row_at, near), lax.div(row_at, near)
    copies = []
    for member, ((above, side_turn), piece_ref) in enumerate(zip(members, piece_refs)):
        theirs = level ^ above
        for at, source in enumerate((theirs, theirs ^ 2)):
            columns = pl.ds(peer_start(near, width, source, side ^ side_turn), width)
            copy = pltpu.make_async_copy(
                piece_ref.at[at], out_ref.at[:, columns], sems.at[member, at]
            )
            copy.start()
            copies.append(copy)
    for copy in copies:
        copy.wait()


def shards(n_row, n_col, data, w_trans, h_prior):
    rank, depth = w_trans.shape
    rows, cols = data.shape
    width = cols // n_row
    near = max(1, n_row // 4)
    far = n_row // near
    slab = rank * (width // LANES)
    turns = [*range(far // 2, far), *range(far // 2 - 1, -1, -1)]
    sides = range(1, near)

    def permute(value, axis, turn):
        size = n_row if axis == "prow" else n_col
        return lax.ppermute(value, axis, [(i, i ^ turn) for i in range(size)])

    w_parts = [w_trans] + [permute(w_trans, "pcol", t) for t in range(1, n_col)]
    early = list(range(1, min(2, n_col)))
    late = [turn for turn in range(n_col) if turn not in early]
    others = [(side, turn) for side in sides for turn in turns]
    owns = [(0, turn) for turn in turns]
    split_parts = jax.ShapeDtypeStruct((n_col, 2 * rank, depth), jnp.bfloat16)
    blocks, begun, w_early, gram_early = call(
        functools.partial(load_kernel, near, width, n_col, early, late, others),
        [
            floats(len(others), rows, width),
            floats(len(others), slab, LANES),
            split_parts,
            floats(rank, rank),
        ],
        [*(w_parts[t] for t in early), data], "load_other_side", 40,
        [VMEM] * len(early) + [HBM], [pltpu.SemaphoreType.DMA((len(others), n_col))],
        pl.CostEstimate(
            flops=0, bytes_accessed=8 * rows * width * len(others), transcendentals=0
        ),
    )
    fetched = list(range(n_col // 2))
    *sent, w_split, gram, own_block = call(
        functools.partial(
            other_side_kernel, near, width, n_col, slab, far, early, late, owns[0], fetched
        ),
        [floats(far * slab + GRAM_ROWS, LANES)] * len(sides)
        + [split_parts, floats(GRAM_ROWS, LANES), floats(1, rows, width)],
        [*(w_parts[t] for t in late), w_early, gram_early, blocks, begun, data], "other_side", 37,
        [VMEM] * (len(late) + 4) + [HBM], [pltpu.SemaphoreType.DMA((1, n_col))],
    )
    got = [permute(sent[side - 1], "prow", side) for side in sides]
    own = call(
        functools.partial(own_side_kernel, near, width, n_col, owns, fetched),
        floats(far, slab, LANES), [w_split, own_block, data], "own_side", 40,
        [VMEM] * 2 + [HBM],
        [
            pltpu.VMEM((far, rows, width), jnp.float32),
            pltpu.SemaphoreType.DMA((far, n_col)),
        ],
    )
    pairs = [(2, 0), (3, 1), (1, 3), (0, 2)]
    sums = call(
        functools.partial(side_sum_kernel, slab, turns, pairs),
        [floats(2 * slab + GRAM_ROWS, LANES)] * len(pairs), [own, gram, *got], "side_sum",
    )
    parts = [
        permute(value, "prow", pair[0] * near) if pair[0] else value
        for pair, value in zip(pairs, sums)
    ]
    fresh = call(
        functools.partial(sweep_kernel, near, width), floats(2, rank, width), [*parts, h_prior],
        "row_sweep",
    )
    members = [(0, 0), (1, 0)] + [(above, side) for above in range(2) for side in sides]
    pieces = [
        permute(fresh, "prow", above * near + side) if above or side else fresh
        for above, side in members
    ]
    return call(
        functools.partial(assemble_kernel, near, width, members), floats(rank, cols), pieces,
        "assemble", scratch=[pltpu.SemaphoreType.DMA((len(members), 2))], out_specs=HBM,
    )


def solution(mesh):
    n_row, n_col = mesh.shape["prow"], mesh.shape["pcol"]
    placed = (P("prow", "pcol"), P(None, ("prow", "pcol")), P(None, "pcol"))
    return jax.shard_map(
        functools.partial(shards, n_row, n_col),
        mesh=mesh, in_specs=placed, out_specs=P(None, "pcol"), check_vma=False,
    )
```

```python
import functools

import jax
import jax.numpy as jnp
from jax import lax
from jax.experimental import pallas as pl
from jax.experimental.pallas import tpu as pltpu
from jax.sharding import PartitionSpec as P

LANES = 128
GRAM_ROWS = 8
VMEM = pl.BlockSpec(memory_space=pltpu.VMEM)
HBM = pl.BlockSpec(memory_space=pltpu.HBM)


def call(kernel, out_shape, operands, name, mebibytes=4, in_specs=None, scratch=(), cost=None,
         out_specs=VMEM):
    many = isinstance(out_shape, list)
    return pl.pallas_call(
        kernel,
        out_shape=out_shape,
        in_specs=in_specs or [VMEM] * len(operands),
        out_specs=[out_specs] * len(out_shape) if many else out_specs,
        compiler_params=pltpu.CompilerParams(vmem_limit_bytes=mebibytes * 1024 * 1024),
        scratch_shapes=list(scratch),
        cost_estimate=cost,
        name=name,
    )(*operands)


def floats(*shape):
    return jax.ShapeDtypeStruct(shape, jnp.float32)


def split(value):
    high = value.astype(jnp.bfloat16)
    low = (value - high.astype(jnp.float32)).astype(jnp.bfloat16)
    return high, low


def exact_dot(left, right, dims):
    return lax.dot_general(
        left, right, (dims, ((), ())),
        precision=lax.Precision.HIGHEST, preferred_element_type=jnp.float32,
    )


def block_start(near, width, side_turn, level_turn):
    row_at = lax.axis_index("prow")
    side, level = lax.rem(row_at, near), lax.div(row_at, near)
    peer = (level ^ level_turn) * near + (side ^ side_turn)
    return pl.multiple_of(peer * width, width)


def row_part(depth, turn):
    return pl.ds(pl.multiple_of((lax.axis_index("pcol") ^ turn) * depth, depth), depth)


def block_copies(near, width, n_col, order, data_ref, out_ref, sems):
    depth = data_ref.shape[0] // n_col
    copies = {}
    for (at, turns), turn in order:
        columns = pl.ds(block_start(near, width, *turns), width)
        rows = row_part(depth, turn)
        copies[at, turn] = pltpu.make_async_copy(
            data_ref.at[rows, columns], out_ref.at[at, rows], sems.at[at, turn]
        )
    return copies


def split_basis(part_ref, out_ref, turn):
    rank = part_ref.shape[0]
    part = part_ref[...]
    high, low = split(part)
    out_ref[turn, :rank] = high
    out_ref[turn, rank:] = low
    return exact_dot(part, part, ((1,), (1,)))


def product(w_split, blocks, at, turns):
    rank, depth = w_split.shape[1] // 2, w_split.shape[2]
    total = None
    for turn in turns:
        high, low = split(blocks[at, row_part(depth, turn)])
        upper = jnp.dot(w_split[turn], high, preferred_element_type=jnp.float32)
        term = (
            upper[:rank]
            + upper[rank:]
            + jnp.dot(w_split[turn, :rank], low, preferred_element_type=jnp.float32)
        )
        total = term if total is None else total + term
    return total


def store(cross, out_ref, row, before=None):
    rank = cross.shape[0]
    for i in range(cross.shape[1] // LANES):
        rows = slice(row + rank * i, row + rank * (i + 1))
        piece = cross[:, LANES * i : LANES * (i + 1)]
        out_ref[rows] = piece if before is None else piece + before[rows]


def own_region(compute):
    pl.when(lax.axis_index("prow") >= 0)(compute)


def load_kernel(near, width, n_col, early, late, others, *refs):
    w_refs, data_ref = refs[: len(early)], refs[len(early)]
    blocks, begun, w_split, gram_ref, sems = refs[len(early) + 1 :]
    order = [(at, turn) for turn in early + late for at in enumerate(others)]
    copies = block_copies(near, width, n_col, order, data_ref, blocks, sems)
    for copy in copies.values():
        copy.start()

    def compute():
        gram = split_basis(w_refs[0], w_split, early[0])
        for turn, ref in list(zip(early, w_refs))[1:]:
            gram = gram + split_basis(ref, w_split, turn)
        gram_ref[...] = gram
        for at in range(len(others)):
            for turn in early:
                copies[at, turn].wait()
            store(product(w_split, blocks, at, early), begun.at[at], 0)

    own_region(compute)
    for (_, turn), copy in copies.items():
        if turn not in early:
            copy.wait()


def other_side_kernel(near, width, n_col, slab, far, early, late, own, fetched, *refs):
    w_refs, (w_early, gram_early, blocks, begun, data_ref) = refs[: len(late)], refs[len(late) :][:5]
    *out_refs, w_split, gram_ref, own_block, sems = refs[len(late) + 5 :]
    rank = w_refs[0].shape[0]
    order = [((0, own), turn) for turn in fetched]
    copies = block_copies(near, width, n_col, order, data_ref, own_block, sems)
    for copy in copies.values():
        copy.start()

    def compute():
        for turn in early:
            w_split[turn] = w_early[turn]
        gram = gram_early[...]
        for turn, ref in zip(late, w_refs):
            gram = gram + split_basis(ref, w_split, turn)
        slabs = [gram[GRAM_ROWS * i : GRAM_ROWS * (i + 1)] for i in range(rank // GRAM_ROWS)]
        packed = jnp.concatenate(slabs, axis=1)
        gram_ref[...] = packed
        for index, out_ref in enumerate(out_refs):
            for at in range(far):
                block = index * far + at
                store(
                    product(w_split, blocks, block, late), out_ref.at[pl.ds(slab * at, slab)], 0,
                    begun.at[block],
                )
            out_ref[slab * far :] = packed

    own_region(compute)
    for copy in copies.values():
        copy.wait()


def own_side_kernel(near, width, n_col, owns, fetched, w_split, first_rows, data_ref, *refs):
    out_ref, blocks, sems = refs
    order = [(at, turn) for at in enumerate(owns) for turn in range(n_col)]
    order = [(at, turn) for at, turn in order if at[0] or turn not in fetched]
    copies = block_copies(near, width, n_col, order, data_ref, blocks, sems)
    for copy in copies.values():
        copy.start()

    def multiply(at):
        total = None if at else product(w_split, first_rows, 0, fetched)
        for turn in range(n_col):
            if (at, turn) in copies:
                copies[at, turn].wait()
                term = product(w_split, blocks, at, [turn])
                total = term if total is None else total + term
        store(total, out_ref.at[at], 0)

    for at in range(len(owns)):
        own_region(functools.partial(multiply, at))


def side_sum_kernel(slab, turns, pairs, own_ref, gram_ref, *refs):
    got_refs, out_refs = refs[: -len(pairs)], refs[-len(pairs) :]
    gram = gram_ref[...]
    for got in got_refs:
        gram = gram + got[slab * len(turns) :]
    for pair, out_ref in zip(pairs, out_refs):
        for at, turn in enumerate(pair):
            place = turns.index(turn)
            total = own_ref[place]
            for got in got_refs:
                total = total + got[slab * place : slab * (place + 1)]
            out_ref[slab * at : slab * (at + 1)] = total
        out_ref[slab * len(pair) :] = gram


def peer_start(near, width, level, side):
    return pl.multiple_of((level * near + side) * width, width)


def sweep_kernel(near, width, *refs):
    parts, h_ref, out_ref = refs[:-2], refs[-2], refs[-1]
    rank = h_ref.shape[0]
    row_at = lax.axis_index("prow")
    side, level = lax.rem(row_at, near), lax.div(row_at, near)
    pieces = width // LANES
    slab = rank * pieces
    packed, chunks = None, [None, None]
    for part in parts:
        gram_part = part[2 * slab :]
        packed = gram_part if packed is None else packed + gram_part
        for at in range(2):
            piece = part[slab * at : slab * (at + 1)]
            chunks[at] = piece if chunks[at] is None else chunks[at] + piece
    cross = jnp.concatenate(
        [chunk[rank * i : rank * (i + 1)] for chunk in chunks for i in range(pieces)], axis=1
    )
    gram = jnp.concatenate(
        [packed[:, rank * i : rank * (i + 1)] for i in range(rank // GRAM_ROWS)], axis=0
    )
    starts = [peer_start(near, width, at, side) for at in (level, level ^ 2)]
    h = jnp.concatenate([h_ref[:, pl.ds(start, width)] for start in starts], axis=1)
    rest = cross - exact_dot(gram, h, ((1,), (0,)))
    inverses = [1.0 / gram[k : k + 1, k : k + 1] for k in range(rank)]
    steps = []
    for k in range(rank):
        step = jnp.maximum(rest[k : k + 1] * inverses[k], -h[k : k + 1])
        steps.append(step)
        if k + 1 < rank:
            rest = rest - gram[:, k : k + 1] * step
    done = h + jnp.concatenate(steps, axis=0)
    for at in range(2):
        out_ref[at] = done[:, width * at : width * (at + 1)]


def assemble_kernel(near, width, members, *refs):
    piece_refs, (out_ref, sems) = refs[:-2], refs[-2:]
    row_at = lax.axis_index("prow")
    side, level = lax.rem(row_at, near), lax.div(row_at, near)
    copies = []
    for member, ((above, side_turn), piece_ref) in enumerate(zip(members, piece_refs)):
        theirs = level ^ above
        for at, source in enumerate((theirs, theirs ^ 2)):
            columns = pl.ds(peer_start(near, width, source, side ^ side_turn), width)
            copy = pltpu.make_async_copy(
                piece_ref.at[at], out_ref.at[:, columns], sems.at[member, at]
            )
            copy.start()
            copies.append(copy)
    for copy in copies:
        copy.wait()


def shards(n_row, n_col, data, w_trans, h_prior):
    rank, depth = w_trans.shape
    rows, cols = data.shape
    width = cols // n_row
    near = max(1, n_row // 4)
    far = n_row // near
    slab = rank * (width // LANES)
    turns = [*range(far // 2, far), *range(far // 2 - 1, -1, -1)]
    sides = range(1, near)

    def permute(value, axis, turn):
        size = n_row if axis == "prow" else n_col
        return lax.ppermute(value, axis, [(i, i ^ turn) for i in range(size)])

    w_parts = [w_trans] + [permute(w_trans, "pcol", t) for t in range(1, n_col)]
    early = list(range(1, min(2, n_col)))
    late = [turn for turn in range(n_col) if turn not in early]
    others = [(side, turn) for side in sides for turn in turns]
    owns = [(0, turn) for turn in turns]
    split_parts = jax.ShapeDtypeStruct((n_col, 2 * rank, depth), jnp.bfloat16)
    blocks, begun, w_early, gram_early = call(
        functools.partial(load_kernel, near, width, n_col, early, late, others),
        [
            floats(len(others), rows, width),
            floats(len(others), slab, LANES),
            split_parts,
            floats(rank, rank),
        ],
        [*(w_parts[t] for t in early), data], "load_other_side", 40,
        [VMEM] * len(early) + [HBM], [pltpu.SemaphoreType.DMA((len(others), n_col))],
        pl.CostEstimate(
            flops=0, bytes_accessed=8 * rows * width * len(others), transcendentals=0
        ),
    )
    fetched = list(range(n_col // 2))
    *sent, w_split, gram, own_block = call(
        functools.partial(
            other_side_kernel, near, width, n_col, slab, far, early, late, owns[0], fetched
        ),
        [floats(far * slab + GRAM_ROWS, LANES)] * len(sides)
        + [split_parts, floats(GRAM_ROWS, LANES), floats(1, rows, width)],
        [*(w_parts[t] for t in late), w_early, gram_early, blocks, begun, data], "other_side", 37,
        [VMEM] * (len(late) + 4) + [HBM], [pltpu.SemaphoreType.DMA((1, n_col))],
    )
    got = [permute(sent[side - 1], "prow", side) for side in sides]
    own = call(
        functools.partial(own_side_kernel, near, width, n_col, owns, fetched),
        floats(far, slab, LANES), [w_split, own_block, data], "own_side", 40,
        [VMEM] * 2 + [HBM],
        [
            pltpu.VMEM((far, rows, width), jnp.float32),
            pltpu.SemaphoreType.DMA((far, n_col)),
        ],
    )
    pairs = [(2, 0), (3, 1), (1, 3), (0, 2)]
    sums = call(
        functools.partial(side_sum_kernel, slab, turns, pairs),
        [floats(2 * slab + GRAM_ROWS, LANES)] * len(pairs), [own, gram, *got], "side_sum",
    )
    parts = [
        permute(value, "prow", pair[0] * near) if pair[0] else value
        for pair, value in zip(pairs, sums)
    ]
    fresh = call(
        functools.partial(sweep_kernel, near, width), floats(2, rank, width), [*parts, h_prior],
        "row_sweep",
    )
    members = [(0, 0), (1, 0)] + [(above, side) for above in range(2) for side in sides]
    pieces = [
        permute(fresh, "prow", above * near + side) if above or side else fresh
        for above, side in members
    ]
    return call(
        functools.partial(assemble_kernel, near, width, members), floats(rank, cols), pieces,
        "assemble", scratch=[pltpu.SemaphoreType.DMA((len(members), 2))], out_specs=HBM,
    )


def solution(mesh):
    n_row, n_col = mesh.shape["prow"], mesh.shape["pcol"]
    placed = (P("prow", "pcol"), P(None, ("prow", "pcol")), P(None, "pcol"))
    return jax.shard_map(
        functools.partial(shards, n_row, n_col),
        mesh=mesh, in_specs=placed, out_specs=P(None, "pcol"), check_vma=False,
    )
```

```python
import functools

import jax
import jax.numpy as jnp
from jax import lax
from jax.experimental import pallas as pl
from jax.experimental.pallas import tpu as pltpu
from jax.sharding import PartitionSpec as P

LANES = 128
GRAM_ROWS = 8
VMEM = pl.BlockSpec(memory_space=pltpu.VMEM)
HBM = pl.BlockSpec(memory_space=pltpu.HBM)


def call(kernel, out_shape, operands, name, mebibytes=4, in_specs=None, scratch=(), cost=None,
         out_specs=VMEM):
    many = isinstance(out_shape, list)
    return pl.pallas_call(
        kernel,
        out_shape=out_shape,
        in_specs=in_specs or [VMEM] * len(operands),
        out_specs=[out_specs] * len(out_shape) if many else out_specs,
        compiler_params=pltpu.CompilerParams(vmem_limit_bytes=mebibytes * 1024 * 1024),
        scratch_shapes=list(scratch),
        cost_estimate=cost,
        name=name,
    )(*operands)


def floats(*shape):
    return jax.ShapeDtypeStruct(shape, jnp.float32)


def split(value):
    high = value.astype(jnp.bfloat16)
    low = (value - high.astype(jnp.float32)).astype(jnp.bfloat16)
    return high, low


def exact_dot(left, right, dims):
    return lax.dot_general(
        left, right, (dims, ((), ())),
        precision=lax.Precision.HIGHEST, preferred_element_type=jnp.float32,
    )


def block_start(near, width, side_turn, level_turn):
    row_at = lax.axis_index("prow")
    side, level = lax.rem(row_at, near), lax.div(row_at, near)
    peer = (level ^ level_turn) * near + (side ^ side_turn)
    return pl.multiple_of(peer * width, width)


def row_part(depth, turn):
    return pl.ds(pl.multiple_of((lax.axis_index("pcol") ^ turn) * depth, depth), depth)


def block_copies(near, width, n_col, order, data_ref, out_ref, sems):
    depth = data_ref.shape[0] // n_col
    copies = {}
    for (at, turns), turn in order:
        columns = pl.ds(block_start(near, width, *turns), width)
        rows = row_part(depth, turn)
        copies[at, turn] = pltpu.make_async_copy(
            data_ref.at[rows, columns], out_ref.at[at, rows], sems.at[at, turn]
        )
    return copies


def split_basis(part_ref, out_ref, turn):
    rank = part_ref.shape[0]
    part = part_ref[...]
    high, low = split(part)
    out_ref[turn, :rank] = high
    out_ref[turn, rank:] = low
    return exact_dot(part, part, ((1,), (1,)))


def product(w_split, blocks, at, turns):
    rank, depth = w_split.shape[1] // 2, w_split.shape[2]
    total = None
    for turn in turns:
        high, low = split(blocks[at, row_part(depth, turn)])
        upper = jnp.dot(w_split[turn], high, preferred_element_type=jnp.float32)
        term = (
            upper[:rank]
            + upper[rank:]
            + jnp.dot(w_split[turn, :rank], low, preferred_element_type=jnp.float32)
        )
        total = term if total is None else total + term
    return total


def store(cross, out_ref, row, before=None):
    rank = cross.shape[0]
    for i in range(cross.shape[1] // LANES):
        rows = slice(row + rank * i, row + rank * (i + 1))
        piece = cross[:, LANES * i : LANES * (i + 1)]
        out_ref[rows] = piece if before is None else piece + before[rows]


def own_region(compute):
    pl.when(lax.axis_index("prow") >= 0)(compute)


def load_kernel(near, width, n_col, early, late, others, *refs):
    w_refs, data_ref = refs[: len(early)], refs[len(early)]
    blocks, begun, w_split, gram_ref, sems = refs[len(early) + 1 :]
    order = [(at, turn) for turn in early + late for at in enumerate(others)]
    copies = block_copies(near, width, n_col, order, data_ref, blocks, sems)
    for copy in copies.values():
        copy.start()

    def compute():
        gram = split_basis(w_refs[0], w_split, early[0])
        for turn, ref in list(zip(early, w_refs))[1:]:
            gram = gram + split_basis(ref, w_split, turn)
        gram_ref[...] = gram
        for at in range(len(others)):
            for turn in early:
                copies[at, turn].wait()
            store(product(w_split, blocks, at, early), begun.at[at], 0)

    own_region(compute)
    for (_, turn), copy in copies.items():
        if turn not in early:
            copy.wait()


def other_side_kernel(near, width, n_col, slab, far, early, late, own, fetched, *refs):
    w_refs, (w_early, gram_early, blocks, begun, data_ref) = refs[: len(late)], refs[len(late) :][:5]
    *out_refs, w_split, gram_ref, own_block, sems = refs[len(late) + 5 :]
    rank = w_refs[0].shape[0]
    order = [((0, own), turn) for turn in fetched]
    copies = block_copies(near, width, n_col, order, data_ref, own_block, sems)
    for copy in copies.values():
        copy.start()

    def compute():
        for turn in early:
            w_split[turn] = w_early[turn]
        gram = gram_early[...]
        for turn, ref in zip(late, w_refs):
            gram = gram + split_basis(ref, w_split, turn)
        slabs = [gram[GRAM_ROWS * i : GRAM_ROWS * (i + 1)] for i in range(rank // GRAM_ROWS)]
        packed = jnp.concatenate(slabs, axis=1)
        gram_ref[...] = packed
        for index, out_ref in enumerate(out_refs):
            for at in range(far):
                block = index * far + at
                store(
                    product(w_split, blocks, block, late), out_ref.at[pl.ds(slab * at, slab)], 0,
                    begun.at[block],
                )
            out_ref[slab * far :] = packed

    own_region(compute)
    for copy in copies.values():
        copy.wait()


def own_side_kernel(near, width, n_col, owns, fetched, w_split, first_rows, data_ref, *refs):
    out_ref, blocks, sems = refs
    order = [(at, turn) for at in enumerate(owns) for turn in range(n_col)]
    order = [(at, turn) for at, turn in order if at[0] or turn not in fetched]
    copies = block_copies(near, width, n_col, order, data_ref, blocks, sems)
    for copy in copies.values():
        copy.start()

    def multiply(at):
        total = None if at else product(w_split, first_rows, 0, fetched)
        for turn in range(n_col):
            if (at, turn) in copies:
                copies[at, turn].wait()
                term = product(w_split, blocks, at, [turn])
                total = term if total is None else total + term
        store(total, out_ref.at[at], 0)

    for at in range(len(owns)):
        own_region(functools.partial(multiply, at))


def side_sum_kernel(slab, turns, pairs, own_ref, gram_ref, *refs):
    got_refs, out_refs = refs[: -len(pairs)], refs[-len(pairs) :]
    gram = gram_ref[...]
    for got in got_refs:
        gram = gram + got[slab * len(turns) :]
    for pair, out_ref in zip(pairs, out_refs):
        for at, turn in enumerate(pair):
            place = turns.index(turn)
            total = own_ref[place]
            for got in got_refs:
                total = total + got[slab * place : slab * (place + 1)]
            out_ref[slab * at : slab * (at + 1)] = total
        out_ref[slab * len(pair) :] = gram


def peer_start(near, width, level, side):
    return pl.multiple_of((level * near + side) * width, width)


def sweep_kernel(near, width, *refs):
    parts, h_ref, out_ref = refs[:-2], refs[-2], refs[-1]
    rank = h_ref.shape[0]
    row_at = lax.axis_index("prow")
    side, level = lax.rem(row_at, near), lax.div(row_at, near)
    pieces = width // LANES
    slab = rank * pieces
    two, three, one, own = (part[...] for part in parts)
    total = (own + two) + (one + three)
    packed = total[2 * slab :]
    chunks = [total[slab * at : slab * (at + 1)] for at in range(2)]
    cross = jnp.concatenate(
        [chunk[rank * i : rank * (i + 1)] for chunk in chunks for i in range(pieces)], axis=1
    )
    gram = jnp.concatenate(
        [packed[:, rank * i : rank * (i + 1)] for i in range(rank // GRAM_ROWS)], axis=0
    )
    starts = [peer_start(near, width, at, side) for at in (level, level ^ 2)]
    h = jnp.concatenate([h_ref[:, pl.ds(start, width)] for start in starts], axis=1)
    rest = cross - exact_dot(gram, h, ((1,), (0,)))
    inverses = [1.0 / gram[k : k + 1, k : k + 1] for k in range(rank)]
    steps = []
    for k in range(rank):
        step = jnp.maximum(rest[k : k + 1] * inverses[k], -h[k : k + 1])
        steps.append(step)
        if k + 1 < rank:
            rest = rest - gram[:, k : k + 1] * step
    done = h + jnp.concatenate(steps, axis=0)
    for at in range(2):
        out_ref[at] = done[:, width * at : width * (at + 1)]


def assemble_kernel(near, width, members, *refs):
    piece_refs, (out_ref, sems) = refs[:-2], refs[-2:]
    row_at = lax.axis_index("prow")
    side, level = lax.rem(row_at, near), lax.div(row_at, near)
    copies = []
    for member, ((above, side_turn), piece_ref) in enumerate(zip(members, piece_refs)):
        theirs = level ^ above
        for at, source in enumerate((theirs, theirs ^ 2)):
            columns = pl.ds(peer_start(near, width, source, side ^ side_turn), width)
            copy = pltpu.make_async_copy(
                piece_ref.at[at], out_ref.at[:, columns], sems.at[member, at]
            )
            copy.start()
            copies.append(copy)
    for copy in copies:
        copy.wait()


def shards(n_row, n_col, data, w_trans, h_prior):
    rank, depth = w_trans.shape
    rows, cols = data.shape
    width = cols // n_row
    near = max(1, n_row // 4)
    far = n_row // near
    slab = rank * (width // LANES)
    turns = [*range(far // 2, far), *range(far // 2 - 1, -1, -1)]
    sides = range(1, near)

    def permute(value, axis, turn):
        size = n_row if axis == "prow" else n_col
        return lax.ppermute(value, axis, [(i, i ^ turn) for i in range(size)])

    w_parts = [w_trans] + [permute(w_trans, "pcol", t) for t in range(1, n_col)]
    early = list(range(1, min(2, n_col)))
    late = [turn for turn in range(n_col) if turn not in early]
    others = [(side, turn) for side in sides for turn in turns]
    owns = [(0, turn) for turn in turns]
    split_parts = jax.ShapeDtypeStruct((n_col, 2 * rank, depth), jnp.bfloat16)
    blocks, begun, w_early, gram_early = call(
        functools.partial(load_kernel, near, width, n_col, early, late, others),
        [
            floats(len(others), rows, width),
            floats(len(others), slab, LANES),
            split_parts,
            floats(rank, rank),
        ],
        [*(w_parts[t] for t in early), data], "load_other_side", 40,
        [VMEM] * len(early) + [HBM], [pltpu.SemaphoreType.DMA((len(others), n_col))],
        pl.CostEstimate(
            flops=0, bytes_accessed=8 * rows * width * len(others), transcendentals=0
        ),
    )
    fetched = list(range(n_col // 2))
    *sent, w_split, gram, own_block = call(
        functools.partial(
            other_side_kernel, near, width, n_col, slab, far, early, late, owns[0], fetched
        ),
        [floats(far * slab + GRAM_ROWS, LANES)] * len(sides)
        + [split_parts, floats(GRAM_ROWS, LANES), floats(1, rows, width)],
        [*(w_parts[t] for t in late), w_early, gram_early, blocks, begun, data], "other_side", 37,
        [VMEM] * (len(late) + 4) + [HBM], [pltpu.SemaphoreType.DMA((1, n_col))],
    )
    got = [permute(sent[side - 1], "prow", side) for side in sides]
    own = call(
        functools.partial(own_side_kernel, near, width, n_col, owns, fetched),
        floats(far, slab, LANES), [w_split, own_block, data], "own_side", 40,
        [VMEM] * 2 + [HBM],
        [
            pltpu.VMEM((far, rows, width), jnp.float32),
            pltpu.SemaphoreType.DMA((far, n_col)),
        ],
    )
    pairs = [(2, 0), (3, 1), (1, 3), (0, 2)]
    sums = call(
        functools.partial(side_sum_kernel, slab, turns, pairs),
        [floats(2 * slab + GRAM_ROWS, LANES)] * len(pairs), [own, gram, *got], "side_sum",
    )
    parts = [
        permute(value, "prow", pair[0] * near) if pair[0] else value
        for pair, value in zip(pairs, sums)
    ]
    fresh = call(
        functools.partial(sweep_kernel, near, width), floats(2, rank, width), [*parts, h_prior],
        "row_sweep",
    )
    members = [(0, 0), (1, 0)] + [(above, side) for above in range(2) for side in sides]
    pieces = [
        permute(fresh, "prow", above * near + side) if above or side else fresh
        for above, side in members
    ]
    return call(
        functools.partial(assemble_kernel, near, width, members), floats(rank, cols), pieces,
        "assemble", scratch=[pltpu.SemaphoreType.DMA((len(members), 2))], out_specs=HBM,
    )


def solution(mesh):
    n_row, n_col = mesh.shape["prow"], mesh.shape["pcol"]
    placed = (P("prow", "pcol"), P(None, ("prow", "pcol")), P(None, "pcol"))
    return jax.shard_map(
        functools.partial(shards, n_row, n_col),
        mesh=mesh, in_specs=placed, out_specs=P(None, "pcol"), check_vma=False,
    )
```

```python
import functools

import jax
import jax.numpy as jnp
from jax import lax
from jax.experimental import pallas as pl
from jax.experimental.pallas import tpu as pltpu
from jax.sharding import PartitionSpec as P

LANES = 128
GRAM_ROWS = 8
LEVELS = 4
VMEM = pl.BlockSpec(memory_space=pltpu.VMEM)
HBM = pl.BlockSpec(memory_space=pltpu.HBM)


def call(kernel, out_shape, operands, name, mebibytes=4, in_specs=None, scratch=(), cost=None,
         out_specs=VMEM):
    many = isinstance(out_shape, list)
    return pl.pallas_call(
        kernel,
        out_shape=out_shape,
        in_specs=in_specs or [VMEM] * len(operands),
        out_specs=[out_specs] * len(out_shape) if many else out_specs,
        compiler_params=pltpu.CompilerParams(vmem_limit_bytes=mebibytes * 1024 * 1024),
        scratch_shapes=list(scratch),
        cost_estimate=cost,
        name=name,
    )(*operands)


def floats(*shape):
    return jax.ShapeDtypeStruct(shape, jnp.float32)


def split(value):
    high = value.astype(jnp.bfloat16)
    low = (value - high.astype(jnp.float32)).astype(jnp.bfloat16)
    return high, low


def exact_dot(left, right, dims):
    return lax.dot_general(
        left, right, (dims, ((), ())),
        precision=lax.Precision.HIGHEST, preferred_element_type=jnp.float32,
    )


def peer_start(near, width, level, side):
    return pl.multiple_of((side * LEVELS + level) * width, width)


def block_start(near, width, side_turn, level_turn):
    row_at = lax.axis_index("prow")
    side, level = lax.rem(row_at, near), lax.div(row_at, near)
    return peer_start(near, width, level ^ level_turn, side ^ side_turn)


def row_part(depth, turn):
    return pl.ds(pl.multiple_of((lax.axis_index("pcol") ^ turn) * depth, depth), depth)


def block_copies(near, width, n_col, order, data_ref, out_ref, sems):
    depth = data_ref.shape[0] // n_col
    copies = {}
    for (at, turns), turn in order:
        columns = pl.ds(block_start(near, width, *turns), width)
        rows = row_part(depth, turn)
        copies[at, turn] = pltpu.make_async_copy(
            data_ref.at[rows, columns], out_ref.at[at, rows], sems.at[at, turn]
        )
    return copies


def split_basis(part_ref, out_ref, turn):
    rank = part_ref.shape[0]
    part = part_ref[...]
    high, low = split(part)
    out_ref[turn, :rank] = high
    out_ref[turn, rank:] = low
    return exact_dot(part, part, ((1,), (1,)))


def product(w_split, blocks, at, turns):
    rank, depth = w_split.shape[1] // 2, w_split.shape[2]
    total = None
    for turn in turns:
        high, low = split(blocks[at, row_part(depth, turn)])
        upper = jnp.dot(w_split[turn], high, preferred_element_type=jnp.float32)
        term = (
            upper[:rank]
            + upper[rank:]
            + jnp.dot(w_split[turn, :rank], low, preferred_element_type=jnp.float32)
        )
        total = term if total is None else total + term
    return total


def store(cross, out_ref, row, before=None):
    rank = cross.shape[0]
    for i in range(cross.shape[1] // LANES):
        rows = slice(row + rank * i, row + rank * (i + 1))
        piece = cross[:, LANES * i : LANES * (i + 1)]
        out_ref[rows] = piece if before is None else piece + before[rows]


def own_region(compute):
    pl.when(lax.axis_index("prow") >= 0)(compute)


def load_kernel(near, width, n_col, early, late, others, *refs):
    w_refs, data_ref = refs[: len(early)], refs[len(early)]
    blocks, begun, w_split, gram_ref, sems = refs[len(early) + 1 :]
    order = [(at, turn) for turn in early + late for at in enumerate(others)]
    copies = block_copies(near, width, n_col, order, data_ref, blocks, sems)
    for copy in copies.values():
        copy.start()

    def compute():
        gram = split_basis(w_refs[0], w_split, early[0])
        for turn, ref in list(zip(early, w_refs))[1:]:
            gram = gram + split_basis(ref, w_split, turn)
        gram_ref[...] = gram
        for at in range(len(others)):
            for turn in early:
                copies[at, turn].wait()
            store(product(w_split, blocks, at, early), begun.at[at], 0)

    own_region(compute)
    for (_, turn), copy in copies.items():
        if turn not in early:
            copy.wait()


def other_side_kernel(near, width, n_col, slab, far, early, late, own, fetched, *refs):
    w_refs, (w_early, gram_early, blocks, begun, data_ref) = refs[: len(late)], refs[len(late) :][:5]
    *out_refs, w_split, gram_ref, own_block, sems = refs[len(late) + 5 :]
    rank = w_refs[0].shape[0]
    order = [((0, own), turn) for turn in fetched]
    copies = block_copies(near, width, n_col, order, data_ref, own_block, sems)
    for copy in copies.values():
        copy.start()

    def compute():
        for turn in early:
            w_split[turn] = w_early[turn]
        gram = gram_early[...]
        for turn, ref in zip(late, w_refs):
            gram = gram + split_basis(ref, w_split, turn)
        slabs = [gram[GRAM_ROWS * i : GRAM_ROWS * (i + 1)] for i in range(rank // GRAM_ROWS)]
        packed = jnp.concatenate(slabs, axis=1)
        gram_ref[...] = packed
        for index, out_ref in enumerate(out_refs):
            for at in range(far):
                block = index * far + at
                store(
                    product(w_split, blocks, block, late), out_ref.at[pl.ds(slab * at, slab)], 0,
                    begun.at[block],
                )
            out_ref[slab * far :] = packed

    own_region(compute)
    for copy in copies.values():
        copy.wait()


def own_side_kernel(near, width, n_col, owns, fetched, w_split, first_rows, data_ref, *refs):
    out_ref, blocks, sems = refs
    order = [(at, turn) for at in enumerate(owns) for turn in range(n_col)]
    order = [(at, turn) for at, turn in order if at[0] or turn not in fetched]
    copies = block_copies(near, width, n_col, order, data_ref, blocks, sems)
    for copy in copies.values():
        copy.start()

    def multiply(at):
        total = None if at else product(w_split, first_rows, 0, fetched)
        for turn in range(n_col):
            if (at, turn) in copies:
                copies[at, turn].wait()
                term = product(w_split, blocks, at, [turn])
                total = term if total is None else total + term
        store(total, out_ref.at[at], 0)

    for at in range(len(owns)):
        own_region(functools.partial(multiply, at))


def side_sum_kernel(slab, turns, pairs, own_ref, gram_ref, *refs):
    got_refs, out_refs = refs[: -len(pairs)], refs[-len(pairs) :]
    gram = gram_ref[...]
    for got in got_refs:
        gram = gram + got[slab * len(turns) :]
    for pair, out_ref in zip(pairs, out_refs):
        for at, turn in enumerate(pair):
            place = turns.index(turn)
            total = own_ref[place]
            for got in got_refs:
                total = total + got[slab * place : slab * (place + 1)]
            out_ref[slab * at : slab * (at + 1)] = total
        out_ref[slab * len(pair) :] = gram


def sweep_kernel(near, width, *refs):
    parts, h_ref, out_ref = refs[:-2], refs[-2], refs[-1]
    rank = h_ref.shape[0]
    row_at = lax.axis_index("prow")
    side, level = lax.rem(row_at, near), lax.div(row_at, near)
    pieces = width // LANES
    slab = rank * pieces
    two, three, one, own = (part[...] for part in parts)
    total = (own + two) + (one + three)
    packed = total[2 * slab :]
    chunks = [total[slab * at : slab * (at + 1)] for at in range(2)]
    cross = jnp.concatenate(
        [chunk[rank * i : rank * (i + 1)] for chunk in chunks for i in range(pieces)], axis=1
    )
    gram = jnp.concatenate(
        [packed[:, rank * i : rank * (i + 1)] for i in range(rank // GRAM_ROWS)], axis=0
    )
    starts = [peer_start(near, width, at, side) for at in (level, level ^ 2)]
    h = jnp.concatenate([h_ref[:, pl.ds(start, width)] for start in starts], axis=1)
    rest = cross - exact_dot(gram, h, ((1,), (0,)))
    inverses = [1.0 / gram[k : k + 1, k : k + 1] for k in range(rank)]
    steps = []
    for k in range(rank):
        step = jnp.maximum(rest[k : k + 1] * inverses[k], -h[k : k + 1])
        steps.append(step)
        if k + 1 < rank:
            rest = rest - gram[:, k : k + 1] * step
    done = h + jnp.concatenate(steps, axis=0)
    for at in range(2):
        out_ref[at] = done[:, width * at : width * (at + 1)]


def assemble_kernel(near, width, members, *refs):
    piece_refs, (out_ref, sems) = refs[:-2], refs[-2:]
    row_at = lax.axis_index("prow")
    side, level = lax.rem(row_at, near), lax.div(row_at, near)
    copies = []
    for member, ((above, side_turn), piece_ref) in enumerate(zip(members, piece_refs)):
        theirs = level ^ above
        for at, source in enumerate((theirs, theirs ^ 2)):
            columns = pl.ds(peer_start(near, width, source, side ^ side_turn), width)
            copy = pltpu.make_async_copy(
                piece_ref.at[at], out_ref.at[:, columns], sems.at[member, at]
            )
            copy.start()
            copies.append(copy)
    for copy in copies:
        copy.wait()


def shards(n_row, n_col, data, w_trans, h_prior):
    rank, depth = w_trans.shape
    rows, cols = data.shape
    width = cols // n_row
    near = max(1, n_row // LEVELS)
    far = n_row // near
    slab = rank * (width // LANES)
    turns = [*range(far // 2, far), *range(far // 2 - 1, -1, -1)]
    sides = range(1, near)

    def permute(value, axis, turn):
        size = n_row if axis == "prow" else n_col
        return lax.ppermute(value, axis, [(i, i ^ turn) for i in range(size)])

    w_parts = [w_trans] + [permute(w_trans, "pcol", t) for t in range(1, n_col)]
    early = list(range(1, min(2, n_col)))
    late = [turn for turn in range(n_col) if turn not in early]
    others = [(side, turn) for side in sides for turn in turns]
    owns = [(0, turn) for turn in turns]
    split_parts = jax.ShapeDtypeStruct((n_col, 2 * rank, depth), jnp.bfloat16)
    blocks, begun, w_early, gram_early = call(
        functools.partial(load_kernel, near, width, n_col, early, late, others),
        [
            floats(len(others), rows, width),
            floats(len(others), slab, LANES),
            split_parts,
            floats(rank, rank),
        ],
        [*(w_parts[t] for t in early), data], "load_other_side", 40,
        [VMEM] * len(early) + [HBM], [pltpu.SemaphoreType.DMA((len(others), n_col))],
        pl.CostEstimate(
            flops=0, bytes_accessed=8 * rows * width * len(others), transcendentals=0
        ),
    )
    fetched = list(range(n_col // 2))
    *sent, w_split, gram, own_block = call(
        functools.partial(
            other_side_kernel, near, width, n_col, slab, far, early, late, owns[0], fetched
        ),
        [floats(far * slab + GRAM_ROWS, LANES)] * len(sides)
        + [split_parts, floats(GRAM_ROWS, LANES), floats(1, rows, width)],
        [*(w_parts[t] for t in late), w_early, gram_early, blocks, begun, data], "other_side", 37,
        [VMEM] * (len(late) + 4) + [HBM], [pltpu.SemaphoreType.DMA((1, n_col))],
    )
    got = [permute(sent[side - 1], "prow", side) for side in sides]
    own = call(
        functools.partial(own_side_kernel, near, width, n_col, owns, fetched),
        floats(far, slab, LANES), [w_split, own_block, data], "own_side", 40,
        [VMEM] * 2 + [HBM],
        [
            pltpu.VMEM((far, rows, width), jnp.float32),
            pltpu.SemaphoreType.DMA((far, n_col)),
        ],
    )
    pairs = [(2, 0), (3, 1), (1, 3), (0, 2)]
    sums = call(
        functools.partial(side_sum_kernel, slab, turns, pairs),
        [floats(2 * slab + GRAM_ROWS, LANES)] * len(pairs), [own, gram, *got], "side_sum",
    )
    parts = [
        permute(value, "prow", pair[0] * near) if pair[0] else value
        for pair, value in zip(pairs, sums)
    ]
    fresh = call(
        functools.partial(sweep_kernel, near, width), floats(2, rank, width), [*parts, h_prior],
        "row_sweep",
    )
    members = [(0, 0), (1, 0)] + [(above, side) for above in range(2) for side in sides]
    pieces = [
        permute(fresh, "prow", above * near + side) if above or side else fresh
        for above, side in members
    ]
    return call(
        functools.partial(assemble_kernel, near, width, members), floats(rank, cols), pieces,
        "assemble", scratch=[pltpu.SemaphoreType.DMA((len(members), 2))], out_specs=HBM,
    )


def solution(mesh):
    n_row, n_col = mesh.shape["prow"], mesh.shape["pcol"]
    placed = (P("prow", "pcol"), P(None, ("prow", "pcol")), P(None, "pcol"))
    return jax.shard_map(
        functools.partial(shards, n_row, n_col),
        mesh=mesh, in_specs=placed, out_specs=P(None, "pcol"), check_vma=False,
    )
```

```python
import functools

import jax
import jax.numpy as jnp
from jax import lax
from jax.experimental import pallas as pl
from jax.experimental.pallas import tpu as pltpu
from jax.sharding import PartitionSpec as P

LANES = 128
GRAM_ROWS = 8
LEVELS = 4
VMEM = pl.BlockSpec(memory_space=pltpu.VMEM)
HBM = pl.BlockSpec(memory_space=pltpu.HBM)


def call(kernel, out_shape, operands, name, mebibytes=4, in_specs=None, scratch=(), cost=None,
         out_specs=VMEM):
    many = isinstance(out_shape, list)
    return pl.pallas_call(
        kernel,
        out_shape=out_shape,
        in_specs=in_specs or [VMEM] * len(operands),
        out_specs=[out_specs] * len(out_shape) if many else out_specs,
        compiler_params=pltpu.CompilerParams(vmem_limit_bytes=mebibytes * 1024 * 1024),
        scratch_shapes=list(scratch),
        cost_estimate=cost,
        name=name,
    )(*operands)


def floats(*shape):
    return jax.ShapeDtypeStruct(shape, jnp.float32)


def split(value):
    high = value.astype(jnp.bfloat16)
    low = (value - high.astype(jnp.float32)).astype(jnp.bfloat16)
    return high, low


def exact_dot(left, right, dims):
    return lax.dot_general(
        left, right, (dims, ((), ())),
        precision=lax.Precision.HIGHEST, preferred_element_type=jnp.float32,
    )


def peer_start(near, width, level, side):
    return pl.multiple_of((side * LEVELS + level) * width, width)


def block_start(near, width, side_turn, level_turn):
    row_at = lax.axis_index("prow")
    side, level = lax.rem(row_at, near), lax.div(row_at, near)
    return peer_start(near, width, level ^ level_turn, side ^ side_turn)


def row_part(depth, turn):
    return pl.ds(pl.multiple_of((lax.axis_index("pcol") ^ turn) * depth, depth), depth)


def block_copies(near, width, n_col, order, data_ref, out_ref, sems):
    depth = data_ref.shape[0] // n_col
    copies = {}
    for (at, turns), turn in order:
        columns = pl.ds(block_start(near, width, *turns), width)
        rows = row_part(depth, turn)
        copies[at, turn] = pltpu.make_async_copy(
            data_ref.at[rows, columns], out_ref.at[at, rows], sems.at[at, turn]
        )
    return copies


def split_basis(part_ref, out_ref, turn):
    rank = part_ref.shape[0]
    part = part_ref[...]
    high, low = split(part)
    out_ref[turn, :rank] = high
    out_ref[turn, rank:] = low
    return exact_dot(part, part, ((1,), (1,)))


def product(w_split, blocks, at, turns):
    rank, depth = w_split.shape[1] // 2, w_split.shape[2]
    total = None
    for turn in turns:
        high, low = split(blocks[at, row_part(depth, turn)])
        upper = jnp.dot(w_split[turn], high, preferred_element_type=jnp.float32)
        term = (
            upper[:rank]
            + upper[rank:]
            + jnp.dot(w_split[turn, :rank], low, preferred_element_type=jnp.float32)
        )
        total = term if total is None else total + term
    return total


def store(cross, out_ref, row, before=None):
    rank = cross.shape[0]
    for i in range(cross.shape[1] // LANES):
        rows = slice(row + rank * i, row + rank * (i + 1))
        piece = cross[:, LANES * i : LANES * (i + 1)]
        out_ref[rows] = piece if before is None else piece + before[rows]


def own_region(compute):
    pl.when(lax.axis_index("prow") >= 0)(compute)


def load_kernel(near, width, n_col, early, late, others, own, fetched, *refs):
    w_refs, data_ref = refs[: len(early)], refs[len(early)]
    blocks, begun, w_split, gram_ref, own_block, sems, own_sems = refs[len(early) + 1 :]
    order = [(at, turn) for turn in early + late for at in enumerate(others)]
    copies = block_copies(near, width, n_col, order, data_ref, blocks, sems)
    order = [((0, own), turn) for turn in fetched]
    own_copies = block_copies(near, width, n_col, order, data_ref, own_block, own_sems)
    for copy in [*copies.values(), *own_copies.values()]:
        copy.start()

    def compute():
        gram = split_basis(w_refs[0], w_split, early[0])
        for turn, ref in list(zip(early, w_refs))[1:]:
            gram = gram + split_basis(ref, w_split, turn)
        gram_ref[...] = gram
        for at in range(len(others)):
            for turn in early:
                copies[at, turn].wait()
            store(product(w_split, blocks, at, early), begun.at[at], 0)

    own_region(compute)
    for (_, turn), copy in copies.items():
        if turn not in early:
            copy.wait()
    for copy in own_copies.values():
        copy.wait()


def other_side_kernel(near, width, n_col, slab, far, early, late, own, fetched, *refs):
    w_refs, (w_early, gram_early, blocks, begun, data_ref) = refs[: len(late)], refs[len(late) :][:5]
    *out_refs, w_split, gram_ref, own_block, sems = refs[len(late) + 5 :]
    rank = w_refs[0].shape[0]
    order = [((0, own), turn) for turn in fetched]
    copies = block_copies(near, width, n_col, order, data_ref, own_block, sems)
    for copy in copies.values():
        copy.start()

    def compute():
        for turn in early:
            w_split[turn] = w_early[turn]
        gram = gram_early[...]
        for turn, ref in zip(late, w_refs):
            gram = gram + split_basis(ref, w_split, turn)
        slabs = [gram[GRAM_ROWS * i : GRAM_ROWS * (i + 1)] for i in range(rank // GRAM_ROWS)]
        packed = jnp.concatenate(slabs, axis=1)
        gram_ref[...] = packed
        for index, out_ref in enumerate(out_refs):
            for at in range(far):
                block = index * far + at
                store(
                    product(w_split, blocks, block, late), out_ref.at[pl.ds(slab * at, slab)], 0,
                    begun.at[block],
                )
            out_ref[slab * far :] = packed

    own_region(compute)
    for copy in copies.values():
        copy.wait()


def own_side_kernel(near, width, n_col, owns, halves, w_split, *refs):
    *held, data_ref, out_ref, rest, sems = refs
    order = [(at, turn) for at in enumerate(owns) for turn in range(n_col)]
    order = [((at - 1, turns), turn) for (at, turns), turn in order if at]
    copies = block_copies(near, width, n_col, order, data_ref, rest, sems)
    for copy in copies.values():
        copy.start()

    def multiply(at):
        total = None
        for turn in range(n_col):
            copies[at, turn].wait()
            term = product(w_split, rest, at, [turn])
            total = term if total is None else total + term
        store(total, out_ref.at[at + 1], 0)

    def multiply_held():
        terms = [product(w_split, ref, 0, turns) for ref, turns in zip(held, halves)]
        store(terms[0] + terms[1], out_ref.at[0], 0)

    own_region(multiply_held)
    for at in range(len(owns) - 1):
        own_region(functools.partial(multiply, at))


def side_sum_kernel(slab, turns, pairs, own_ref, gram_ref, *refs):
    got_refs, out_refs = refs[: -len(pairs)], refs[-len(pairs) :]
    gram = gram_ref[...]
    for got in got_refs:
        gram = gram + got[slab * len(turns) :]
    for pair, out_ref in zip(pairs, out_refs):
        for at, turn in enumerate(pair):
            place = turns.index(turn)
            total = own_ref[place]
            for got in got_refs:
                total = total + got[slab * place : slab * (place + 1)]
            out_ref[slab * at : slab * (at + 1)] = total
        out_ref[slab * len(pair) :] = gram


def sweep_kernel(near, width, *refs):
    parts, h_ref, out_ref = refs[:-2], refs[-2], refs[-1]
    rank = h_ref.shape[0]
    row_at = lax.axis_index("prow")
    side, level = lax.rem(row_at, near), lax.div(row_at, near)
    pieces = width // LANES
    slab = rank * pieces
    two, three, one, own = (part[...] for part in parts)
    total = (own + two) + (one + three)
    packed = total[2 * slab :]
    chunks = [total[slab * at : slab * (at + 1)] for at in range(2)]
    cross = jnp.concatenate(
        [chunk[rank * i : rank * (i + 1)] for chunk in chunks for i in range(pieces)], axis=1
    )
    gram = jnp.concatenate(
        [packed[:, rank * i : rank * (i + 1)] for i in range(rank // GRAM_ROWS)], axis=0
    )
    starts = [peer_start(near, width, at, side) for at in (level, level ^ 2)]
    h = jnp.concatenate([h_ref[:, pl.ds(start, width)] for start in starts], axis=1)
    rest = cross - exact_dot(gram, h, ((1,), (0,)))
    inverses = [1.0 / gram[k : k + 1, k : k + 1] for k in range(rank)]
    steps = []
    for k in range(rank):
        step = jnp.maximum(rest[k : k + 1] * inverses[k], -h[k : k + 1])
        steps.append(step)
        if k + 1 < rank:
            rest = rest - gram[:, k : k + 1] * step
    done = h + jnp.concatenate(steps, axis=0)
    for at in range(2):
        out_ref[at] = done[:, width * at : width * (at + 1)]


def assemble_kernel(near, width, members, *refs):
    piece_refs, (out_ref, sems) = refs[:-2], refs[-2:]
    row_at = lax.axis_index("prow")
    side, level = lax.rem(row_at, near), lax.div(row_at, near)
    copies = []
    for member, ((above, side_turn), piece_ref) in enumerate(zip(members, piece_refs)):
        theirs = level ^ above
        for at, source in enumerate((theirs, theirs ^ 2)):
            columns = pl.ds(peer_start(near, width, source, side ^ side_turn), width)
            copy = pltpu.make_async_copy(
                piece_ref.at[at], out_ref.at[:, columns], sems.at[member, at]
            )
            copy.start()
            copies.append(copy)
    for copy in copies:
        copy.wait()


def shards(n_row, n_col, data, w_trans, h_prior):
    rank, depth = w_trans.shape
    rows, cols = data.shape
    width = cols // n_row
    near = max(1, n_row // LEVELS)
    far = n_row // near
    slab = rank * (width // LANES)
    turns = [*range(far // 2, far), *range(far // 2 - 1, -1, -1)]
    sides = range(1, near)

    def permute(value, axis, turn):
        size = n_row if axis == "prow" else n_col
        return lax.ppermute(value, axis, [(i, i ^ turn) for i in range(size)])

    w_parts = [w_trans] + [permute(w_trans, "pcol", t) for t in range(1, n_col)]
    early = list(range(1, min(2, n_col)))
    late = [turn for turn in range(n_col) if turn not in early]
    others = [(side, turn) for side in sides for turn in turns]
    owns = [(0, turn) for turn in turns]
    split_parts = jax.ShapeDtypeStruct((n_col, 2 * rank, depth), jnp.bfloat16)
    halves = [list(range(n_col // 2)), list(range(n_col // 2, n_col))]
    blocks, begun, w_early, gram_early, own_a = call(
        functools.partial(
            load_kernel, near, width, n_col, early, late, others, owns[0], halves[0]
        ),
        [
            floats(len(others), rows, width),
            floats(len(others), slab, LANES),
            split_parts,
            floats(rank, rank),
            floats(1, rows, width),
        ],
        [*(w_parts[t] for t in early), data], "load_other_side", 40,
        [VMEM] * len(early) + [HBM],
        [pltpu.SemaphoreType.DMA((len(others), n_col)), pltpu.SemaphoreType.DMA((1, n_col))],
        pl.CostEstimate(
            flops=0, bytes_accessed=8 * rows * width * len(others), transcendentals=0
        ),
    )
    *sent, w_split, gram, own_block = call(
        functools.partial(
            other_side_kernel, near, width, n_col, slab, far, early, late, owns[0], halves[1]
        ),
        [floats(far * slab + GRAM_ROWS, LANES)] * len(sides)
        + [split_parts, floats(GRAM_ROWS, LANES), floats(1, rows, width)],
        [*(w_parts[t] for t in late), w_early, gram_early, blocks, begun, data], "other_side", 37,
        [VMEM] * (len(late) + 4) + [HBM], [pltpu.SemaphoreType.DMA((1, n_col))],
    )
    got = [permute(sent[side - 1], "prow", side) for side in sides]
    own = call(
        functools.partial(own_side_kernel, near, width, n_col, owns, halves),
        floats(far, slab, LANES), [w_split, own_a, own_block, data], "own_side", 40,
        [VMEM] * 3 + [HBM],
        [
            pltpu.VMEM((far - 1, rows, width), jnp.float32),
            pltpu.SemaphoreType.DMA((far - 1, n_col)),
        ],
    )
    pairs = [(2, 0), (3, 1), (1, 3), (0, 2)]
    sums = call(
        functools.partial(side_sum_kernel, slab, turns, pairs),
        [floats(2 * slab + GRAM_ROWS, LANES)] * len(pairs), [own, gram, *got], "side_sum",
    )
    parts = [
        permute(value, "prow", pair[0] * near) if pair[0] else value
        for pair, value in zip(pairs, sums)
    ]
    fresh = call(
        functools.partial(sweep_kernel, near, width), floats(2, rank, width), [*parts, h_prior],
        "row_sweep",
    )
    members = [(0, 0), (1, 0)] + [(above, side) for above in range(2) for side in sides]
    pieces = [
        permute(fresh, "prow", above * near + side) if above or side else fresh
        for above, side in members
    ]
    return call(
        functools.partial(assemble_kernel, near, width, members), floats(rank, cols), pieces,
        "assemble", scratch=[pltpu.SemaphoreType.DMA((len(members), 2))], out_specs=HBM,
    )


def solution(mesh):
    n_row, n_col = mesh.shape["prow"], mesh.shape["pcol"]
    placed = (P("prow", "pcol"), P(None, ("prow", "pcol")), P(None, "pcol"))
    return jax.shard_map(
        functools.partial(shards, n_row, n_col),
        mesh=mesh, in_specs=placed, out_specs=P(None, "pcol"), check_vma=False,
    )
```

```python
import functools

import jax
import jax.numpy as jnp
from jax import lax
from jax.experimental import pallas as pl
from jax.experimental.pallas import tpu as pltpu
from jax.sharding import PartitionSpec as P

LANES = 128
GRAM_ROWS = 8
LEVELS = 4
VMEM = pl.BlockSpec(memory_space=pltpu.VMEM)
HBM = pl.BlockSpec(memory_space=pltpu.HBM)


def call(kernel, out_shape, operands, name, mebibytes=4, in_specs=None, scratch=(), cost=None,
         out_specs=VMEM):
    many = isinstance(out_shape, list)
    return pl.pallas_call(
        kernel,
        out_shape=out_shape,
        in_specs=in_specs or [VMEM] * len(operands),
        out_specs=[out_specs] * len(out_shape) if many else out_specs,
        compiler_params=pltpu.CompilerParams(vmem_limit_bytes=mebibytes * 1024 * 1024),
        scratch_shapes=list(scratch),
        cost_estimate=cost,
        name=name,
    )(*operands)


def floats(*shape):
    return jax.ShapeDtypeStruct(shape, jnp.float32)


def split(value):
    high = value.astype(jnp.bfloat16)
    low = (value - high.astype(jnp.float32)).astype(jnp.bfloat16)
    return high, low


def exact_dot(left, right, dims):
    return lax.dot_general(
        left, right, (dims, ((), ())),
        precision=lax.Precision.HIGHEST, preferred_element_type=jnp.float32,
    )


def peer_start(near, width, level, side):
    return pl.multiple_of((side * LEVELS + level) * width, width)


def block_start(near, width, side_turn, level_turn):
    row_at = lax.axis_index("prow")
    side, level = lax.rem(row_at, near), lax.div(row_at, near)
    return peer_start(near, width, level ^ level_turn, side ^ side_turn)


def row_part(depth, turn):
    return pl.ds(pl.multiple_of((lax.axis_index("pcol") ^ turn) * depth, depth), depth)


def block_copies(near, width, n_col, order, data_ref, out_ref, sems):
    depth = data_ref.shape[0] // n_col
    copies = {}
    for (at, turns), turn in order:
        columns = pl.ds(block_start(near, width, *turns), width)
        rows = row_part(depth, turn)
        copies[at, turn] = pltpu.make_async_copy(
            data_ref.at[rows, columns], out_ref.at[at, rows], sems.at[at, turn]
        )
    return copies


def split_basis(part_ref, out_ref, turn):
    rank = part_ref.shape[0]
    part = part_ref[...]
    high, low = split(part)
    out_ref[turn, :rank] = high
    out_ref[turn, rank:] = low
    return exact_dot(part, part, ((1,), (1,)))


def product(w_split, blocks, at, turns):
    rank, depth = w_split.shape[1] // 2, w_split.shape[2]
    total = None
    for turn in turns:
        high, low = split(blocks[at, row_part(depth, turn)])
        upper = jnp.dot(w_split[turn], high, preferred_element_type=jnp.float32)
        term = (
            upper[:rank]
            + upper[rank:]
            + jnp.dot(w_split[turn, :rank], low, preferred_element_type=jnp.float32)
        )
        total = term if total is None else total + term
    return total


def store(cross, out_ref, row, before=None):
    rank = cross.shape[0]
    for i in range(cross.shape[1] // LANES):
        rows = slice(row + rank * i, row + rank * (i + 1))
        piece = cross[:, LANES * i : LANES * (i + 1)]
        out_ref[rows] = piece if before is None else piece + before[rows]


def own_region(compute):
    pl.when(lax.axis_index("prow") >= 0)(compute)


def load_kernel(near, width, n_col, early, late, others, own, fetched, *refs):
    w_refs, data_ref = refs[: len(early)], refs[len(early)]
    blocks, begun, w_split, gram_ref, own_block, sems, own_sems = refs[len(early) + 1 :]
    order = [(at, turn) for turn in early + late for at in enumerate(others)]
    copies = block_copies(near, width, n_col, order, data_ref, blocks, sems)
    order = [((0, own), turn) for turn in fetched]
    own_copies = block_copies(near, width, n_col, order, data_ref, own_block, own_sems)
    for copy in [*copies.values(), *own_copies.values()]:
        copy.start()

    def compute():
        gram = split_basis(w_refs[0], w_split, early[0])
        for turn, ref in list(zip(early, w_refs))[1:]:
            gram = gram + split_basis(ref, w_split, turn)
        gram_ref[...] = gram
        for at in range(len(others)):
            for turn in early:
                copies[at, turn].wait()
            store(product(w_split, blocks, at, early), begun.at[at], 0)

    own_region(compute)
    for (_, turn), copy in copies.items():
        if turn not in early:
            copy.wait()
    for copy in own_copies.values():
        copy.wait()


def other_side_kernel(near, width, n_col, slab, far, early, late, own, fetched, *refs):
    w_refs, (w_early, gram_early, blocks, begun, data_ref) = refs[: len(late)], refs[len(late) :][:5]
    *out_refs, w_split, gram_ref, own_block, sems = refs[len(late) + 5 :]
    rank = w_refs[0].shape[0]
    order = [((0, own), turn) for turn in fetched]
    copies = block_copies(near, width, n_col, order, data_ref, own_block, sems)
    for copy in copies.values():
        copy.start()

    def compute():
        for turn in early:
            w_split[turn] = w_early[turn]
        gram = gram_early[...]
        for turn, ref in zip(late, w_refs):
            gram = gram + split_basis(ref, w_split, turn)
        slabs = [gram[GRAM_ROWS * i : GRAM_ROWS * (i + 1)] for i in range(rank // GRAM_ROWS)]
        packed = jnp.concatenate(slabs, axis=1)
        gram_ref[...] = packed
        for index, out_ref in enumerate(out_refs):
            for at in range(far):
                block = index * far + at
                store(
                    product(w_split, blocks, block, late), out_ref.at[pl.ds(slab * at, slab)], 0,
                    begun.at[block],
                )
            out_ref[slab * far :] = packed

    own_region(compute)
    for copy in copies.values():
        copy.wait()


def own_side_kernel(near, width, n_col, owns, halves, w_split, *refs):
    *held, data_ref, out_ref, rest, sems = refs
    order = [(at, turn) for at in enumerate(owns) for turn in range(n_col)]
    order = [((at - 1, turns), turn) for (at, turns), turn in order if at]
    copies = block_copies(near, width, n_col, order, data_ref, rest, sems)
    for copy in copies.values():
        copy.start()

    def multiply(at):
        total = None
        for turn in range(n_col):
            copies[at, turn].wait()
            term = product(w_split, rest, at, [turn])
            total = term if total is None else total + term
        store(total, out_ref.at[at + 1], 0)

    def multiply_held():
        terms = [product(w_split, ref, 0, turns) for ref, turns in zip(held, halves)]
        store(terms[0] + terms[1], out_ref.at[0], 0)

    own_region(multiply_held)
    for at in range(len(owns) - 1):
        own_region(functools.partial(multiply, at))


def side_sum_kernel(slab, turns, pairs, own_ref, gram_ref, *refs):
    got_refs, out_refs = refs[: -len(pairs)], refs[-len(pairs) :]
    gram = gram_ref[...]
    for got in got_refs:
        gram = gram + got[slab * len(turns) :]
    for pair, out_ref in zip(pairs, out_refs):
        for at, turn in enumerate(pair):
            place = turns.index(turn)
            total = own_ref[place]
            for got in got_refs:
                total = total + got[slab * place : slab * (place + 1)]
            out_ref[slab * at : slab * (at + 1)] = total
        out_ref[slab * len(pair) :] = gram


def sweep_kernel(near, width, *refs):
    parts, h_ref, out_ref = refs[:-2], refs[-2], refs[-1]
    rank = h_ref.shape[0]
    row_at = lax.axis_index("prow")
    side, level = lax.rem(row_at, near), lax.div(row_at, near)
    pieces = width // LANES
    slab = rank * pieces
    two, three, one, own = (part[...] for part in parts)
    total = (own + two) + (one + three)
    packed = total[2 * slab :]
    chunks = [total[slab * at : slab * (at + 1)] for at in range(2)]
    cross = jnp.concatenate(
        [chunk[rank * i : rank * (i + 1)] for chunk in chunks for i in range(pieces)], axis=1
    )
    gram = jnp.concatenate(
        [packed[:, rank * i : rank * (i + 1)] for i in range(rank // GRAM_ROWS)], axis=0
    )
    starts = [peer_start(near, width, at, side) for at in (level, level ^ 2)]
    h = jnp.concatenate([h_ref[:, pl.ds(start, width)] for start in starts], axis=1)
    rest = cross - exact_dot(gram, h, ((1,), (0,)))
    inverses = [1.0 / gram[k : k + 1, k : k + 1] for k in range(rank)]
    steps = []
    for k in range(rank):
        step = jnp.maximum(rest[k : k + 1] * inverses[k], -h[k : k + 1])
        steps.append(step)
        if k + 1 < rank:
            rest = rest - gram[:, k : k + 1] * step
    done = h + jnp.concatenate(steps, axis=0)
    for at in range(2):
        out_ref[at] = done[:, width * at : width * (at + 1)]


def assemble_kernel(near, width, members, *refs):
    piece_refs, (out_ref, sems) = refs[:-2], refs[-2:]
    row_at = lax.axis_index("prow")
    side, level = lax.rem(row_at, near), lax.div(row_at, near)
    copies = []
    for member, ((above, side_turn), piece_ref) in enumerate(zip(members, piece_refs)):
        theirs = level ^ above
        for at, source in enumerate((theirs, theirs ^ 2)):
            columns = pl.ds(peer_start(near, width, source, side ^ side_turn), width)
            copy = pltpu.make_async_copy(
                piece_ref.at[at], out_ref.at[:, columns], sems.at[member, at]
            )
            copy.start()
            copies.append(copy)
    for copy in copies:
        copy.wait()


def shards(n_row, n_col, data, w_trans, h_prior):
    rank, depth = w_trans.shape
    rows, cols = data.shape
    width = cols // n_row
    near = max(1, n_row // LEVELS)
    far = n_row // near
    slab = rank * (width // LANES)
    turns = [*range(far // 2, far), *range(far // 2 - 1, -1, -1)]
    sides = range(1, near)

    def permute(value, axis, turn):
        size = n_row if axis == "prow" else n_col
        return lax.ppermute(value, axis, [(i, i ^ turn) for i in range(size)])

    w_parts = [w_trans] + [permute(w_trans, "pcol", t) for t in range(1, n_col)]
    early = list(range(1, min(2, n_col)))
    late = [turn for turn in range(n_col) if turn not in early]
    others = [(side, turn) for side in sides for turn in turns]
    owns = [(0, turn) for turn in turns]
    split_parts = jax.ShapeDtypeStruct((n_col, 2 * rank, depth), jnp.bfloat16)
    halves = [list(range(n_col // 2)), list(range(n_col // 2, n_col))]
    blocks, begun, w_early, gram_early, own_a = call(
        functools.partial(
            load_kernel, near, width, n_col, early, late, others, owns[0], halves[0]
        ),
        [
            floats(len(others), rows, width),
            floats(len(others), slab, LANES),
            split_parts,
            floats(rank, rank),
            floats(1, rows, width),
        ],
        [*(w_parts[t] for t in early), data], "load_other_side", 40,
        [VMEM] * len(early) + [HBM],
        [pltpu.SemaphoreType.DMA((len(others), n_col)), pltpu.SemaphoreType.DMA((1, n_col))],
        pl.CostEstimate(
            flops=0, bytes_accessed=8 * rows * width * len(others), transcendentals=0
        ),
    )
    *sent, w_split, gram, own_block = call(
        functools.partial(
            other_side_kernel, near, width, n_col, slab, far, early, late, owns[0], halves[1]
        ),
        [floats(far * slab + GRAM_ROWS, LANES)] * len(sides)
        + [split_parts, floats(GRAM_ROWS, LANES), floats(1, rows, width)],
        [*(w_parts[t] for t in late), w_early, gram_early, blocks, begun, data], "other_side", 37,
        [VMEM] * (len(late) + 4) + [HBM], [pltpu.SemaphoreType.DMA((1, n_col))],
    )
    got = [permute(sent[side - 1], "prow", side) for side in sides]
    own = call(
        functools.partial(own_side_kernel, near, width, n_col, owns, halves),
        floats(far, slab, LANES), [w_split, own_a, own_block, data], "own_side", 40,
        [VMEM] * 3 + [HBM],
        [
            pltpu.VMEM((far - 1, rows, width), jnp.float32),
            pltpu.SemaphoreType.DMA((far - 1, n_col)),
        ],
    )
    pairs = [(2, 0), (3, 1), (1, 3), (0, 2)]
    sums = call(
        functools.partial(side_sum_kernel, slab, turns, pairs),
        [floats(2 * slab + GRAM_ROWS, LANES)] * len(pairs), [own, gram, *got], "side_sum",
    )
    parts = [
        permute(value, "prow", pair[0] * near) if pair[0] else value
        for pair, value in zip(pairs, sums)
    ]
    fresh = call(
        functools.partial(sweep_kernel, near, width), floats(2, rank, width), [*parts, h_prior],
        "row_sweep",
    )
    members = [(0, 0), (1, 0)] + [(above, side) for above in (1, 0) for side in sides]
    pieces = [
        permute(fresh, "prow", above * near + side) if above or side else fresh
        for above, side in members
    ]
    return call(
        functools.partial(assemble_kernel, near, width, members), floats(rank, cols), pieces,
        "assemble", scratch=[pltpu.SemaphoreType.DMA((len(members), 2))], out_specs=HBM,
    )


def solution(mesh):
    n_row, n_col = mesh.shape["prow"], mesh.shape["pcol"]
    placed = (P("prow", "pcol"), P(None, ("prow", "pcol")), P(None, "pcol"))
    return jax.shard_map(
        functools.partial(shards, n_row, n_col),
        mesh=mesh, in_specs=placed, out_specs=P(None, "pcol"), check_vma=False,
    )
```
